32 devices in a mesh: fsdp: 8 (over z, x), ctx: 2 (over core), tp: 2 (over y).
Axes of the slice: x: 2, y: 2, z: 4, core: 2. Of those that a mesh axis runs over, the one named last changes fastest.
Arguments:
- tokens: bfloat16 [4096, 768], P(('fsdp', 'ctx')), may hold values from -6 to 6
- cotangent: bfloat16 [4096, 768], P(('fsdp', 'ctx')), may hold values from -6 to 6
- w_query: bfloat16 [768, 768], P(('fsdp', 'ctx'), 'tp'), may hold values from -0.25 to 0.25
- w_key: bfloat16 [768, 768], P(('fsdp', 'ctx'), 'tp'), may hold values from -0.25 to 0.25
- w_value: bfloat16 [768, 768], P(('fsdp', 'ctx'), 'tp'), may hold values from -0.21875 to 0.21875
- w_output: bfloat16 [768, 768], P(('fsdp', 'ctx'), 'tp'), may hold values from -2 to 2
- w_router: bfloat16 [768, 32], P(('fsdp', 'ctx')), may hold values from -0.25 to 0.25
- gain_attn: bfloat16 [768], P(('fsdp', 'ctx')), may hold values from 0.5 to 1.5
- gain_moe: bfloat16 [768], P(('fsdp', 'ctx')), may hold values from 0.5 to 1.5
- rel_table: float32 [32, 12], P(None, 'tp'), may hold values from -6 to 6
- w_in: bfloat16 [32, 768, 3072], P(('fsdp', 'ctx'), None, 'tp'), may hold values from -0.21875 to 0.21875
- w_out: bfloat16 [32, 3072, 768], P(('fsdp', 'ctx'), 'tp'), may hold values from -6 to 6
- lengths: int32 [8, 4], P('fsdp'), may hold values from 0 to 512, as said below
- routes: int32 [4096, 1], P(('fsdp', 'ctx')), may hold values from 0 to 31; in each aligned block of 256 rows (0 to 255, 256 to 511, ...) at most 10 rows name the same one
- keep_mask: int32 [4096], P(('fsdp', 'ctx')), may hold values 0 or 1
Outputs:
- result: float32 [4096, 768], P(('fsdp', 'ctx'))
- tokens_grad: float32 [4096, 768], P(('fsdp', 'ctx'))
- w_query_grad: float32 [768, 768], P(('fsdp', 'ctx'), 'tp')
- w_key_grad: float32 [768, 768], P(('fsdp', 'ctx'), 'tp')
- w_value_grad: float32 [768, 768], P(('fsdp', 'ctx'), 'tp')
- w_output_grad: float32 [768, 768], P(('fsdp', 'ctx'), 'tp')
- w_router_grad: float32 [768, 32], P(('fsdp', 'ctx'))
- gain_attn_grad: float32 [768], P(('fsdp', 'ctx'))
- gain_moe_grad: float32 [768], P(('fsdp', 'ctx'))
- rel_table_grad: float32 [32, 12], P(None, 'tp')
- w_in_grad: float32 [32, 768, 3072], P(('fsdp', 'ctx'), None, 'tp')
- w_out_grad: float32 [32, 3072, 768], P(('fsdp', 'ctx'), 'tp')
The draws below stay inside these ranges and needn't reach their ends.
Inputs may be any that keep to these rules, and one draw needn't show every extreme that they name: `lengths`: each row sums to 512. In one row a single sequence fills the whole pack and the other entries are 0. `routes`: within the 256 tokens of one device, at most 10 name one expert, a bound that some block reaches.
All inputs are finite; a program needn't handle non-finite values. No bound on the sum of `keep_mask` on one device may be relied on, other than what follows from the above.
Results may differ from the reference program's by a relative error of at most 0.015.
The reference program's roundings to bfloat16 on the way count: a program that leaves them out, or rounds other values in their place, can miss the bound.
Values may be sent and summed in bfloat16 or wider, within the bound.
No kernel may reach another device: no remote copies, remote signals or barrier semaphores. Data moves between devices by JAX's collectives and lax.ppermute only.
A program may use at most 128 MiB of HBM per device.

```python
import math
import jax
import jax.numpy as jnp
import numpy as np
from jax import lax

D = 768
H = 12
HEAD = 64
FF = 3072
BUCKETS = 32
EXPERTS = 32
TOK_DEV = 256
SEQS = 4
GRP = 512
TOKENS = 4096
HD = 768
SPLIT = 1
PIECES = 32
CAP = 10
N_FSDP = 8
N_CTX = 2


def draw_lengths(key, part):
    key = jax.random.fold_in(key, 7)
    whole_key, cut_key = jax.random.split(key)
    margin = TOK_DEV // 2
    cuts = jax.random.randint(cut_key, (N_FSDP, SEQS - 1), 1, GRP - margin)
    cuts = jnp.where(cuts >= TOK_DEV - margin // 2, cuts + margin, cuts)
    cuts = jnp.sort(cuts, axis=1)
    bounds = jnp.concatenate([jnp.zeros((N_FSDP, 1), jnp.int32), cuts.astype(jnp.int32), jnp.full((N_FSDP, 1), GRP, jnp.int32)], axis=1)
    spans = bounds[:, 1:] - bounds[:, :-1]
    whole_row = jax.random.randint(whole_key, (), 0, N_FSDP)
    single = jnp.concatenate([jnp.full((1,), GRP, jnp.int32), jnp.zeros((SEQS - 1,), jnp.int32)])
    row_hit = jnp.arange(N_FSDP)[:, None] == whole_row
    return jnp.where(row_hit, single[None, :], spans).astype(jnp.int32)


def touch_ends(result, own_key, smallest, high):
    shape = result.shape
    spot = [jax.random.randint(jax.random.fold_in(own_key, axis), (), 0, shape[axis]) for axis in range(len(shape))]
    result = result.at[tuple(spot)].set(smallest)
    longest = shape.index(max(shape))
    spot[longest] = (spot[longest] + 1) % shape[longest]
    return result.at[tuple(spot)].set(high)


def steps_of(own_key, shape, cuts, low, top_value):
    loudness, own = 1.0, jax.random.fold_in(own_key, 6)
    for dim, shards_of in cuts:
        heights = jnp.exp(jax.random.uniform(jax.random.fold_in(own, dim), (shards_of,), jnp.float32, low / len(cuts), top_value / len(cuts)))
        loudness = loudness * jnp.repeat(heights, shape[dim] // shards_of).reshape([-1 if axis == dim else 1 for axis in range(len(shape))])
    return loudness


def deal_out(own_key, own, number, rows, number_of, top, reach, lean):
    order = jax.random.permutation(own_key, number_of)
    crowded, usual = portions_of(number_of, rows * top, reach, lean, True), portions_of(number_of, rows * top, reach, lean, False)
    places = jnp.arange(number_of)

    def named(tallies, offset_by):
        used = int((tallies > 0).sum())
        fixed = max(1, used // 4)
        moved = fixed + (places - fixed + offset_by * (used - fixed)) % max(1, number_of - fixed)
        return jnp.zeros((number_of,), jnp.int32).at[order[jnp.where(places < fixed, places, moved)]].set(jnp.asarray(tallies, jnp.int32))

    tallies = jnp.where(number % 4 == 0, named(crowded, number // 4), named(usual, number - number // 4 - 1))
    mixed = jax.random.permutation(jax.random.fold_in(own, 3), number_of)
    donor, sink = mixed[0:number_of // 2 * 2:2], mixed[1:number_of // 2 * 2:2]
    room = jnp.minimum(tallies[donor] - 1, reach - tallies[sink]) // 2
    room = jnp.where((donor == order[0]) | (sink == order[0]) | (tallies[sink] == 0), 0, jnp.maximum(room, 0))
    moved = jax.random.randint(jax.random.fold_in(own, 4), (number_of // 2,), 0, 1 << 20) % (room + 1)
    tallies = tallies.at[donor].add(-moved).at[sink].add(moved)
    labels = jnp.searchsorted(jnp.cumsum(tallies), jnp.arange(rows * top), side="right").astype(jnp.int32)
    listing = labels.reshape(top, rows).T
    listing = listing[jax.random.permutation(jax.random.fold_in(own, 1), rows)]
    offset_by = jax.random.randint(jax.random.fold_in(own, 2), (rows, 1), 0, top)
    return jnp.take_along_axis(listing, (jnp.arange(top)[None, :] + offset_by) % top, axis=1)


def portions_of(number_of, total, bound, slope, full):
    loads = [(1 << 20) // math.isqrt(rank ** slope) + 1 for rank in range(1, number_of + 1)]
    largest = bound if full else min(bound, max(-(-total // number_of), total * loads[0] // sum(loads)))
    least = 1 if total - largest >= number_of - 1 else 0
    counts, rest = [largest] + [least] * (number_of - 1), total - largest - least * (number_of - 1)
    while rest > 0:
        free = [i for i in range(1, number_of) if counts[i] < largest] or [i for i in range(1, number_of) if counts[i] < bound]
        pool, budget = sum([loads[i] for i in free]), rest
        for i in free:
            more = min(bound - counts[i], max(1, budget * loads[i] // pool), rest)
            counts[i] = counts[i] + more
            rest = rest - more
    return np.array(counts)


def bell_draw(own_key, extent, width, most, cuts=(), kind=jnp.bfloat16):
    result = width * jax.random.normal(own_key, extent, jnp.float32)
    if cuts:
        result = result * steps_of(own_key, extent, cuts, -0.22, 0.18)
    return jnp.clip(result, -most, most).astype(kind)


def setup_inputs(seed: int = 0) -> dict:
    seeds = jax.random.split(jax.random.key(seed), 16)
    tokens = bell_draw(seeds[0], (TOKENS, D), 1.0, 6.0, ((0, 16),))
    cotangent = bell_draw(seeds[1], (TOKENS, D), 1.0, 6.0, ((0, 16),))
    w_query = bell_draw(seeds[2], (D, HD), ((1.8 * D ** -1 * HEAD ** -0.5) ** 0.5), 0.25, ((0, 16), (1, 2)))
    w_key = bell_draw(seeds[3], (D, HD), ((1.8 * D ** -1 * HEAD ** -0.5) ** 0.5), 0.25, ((0, 16), (1, 2)))
    w_value = bell_draw(seeds[4], (D, HD), D ** -0.5, 0.21875, ((0, 16), (1, 2)))
    w_output = bell_draw(seeds[5], (D, HD), (4.0 * D ** -0.5), 2.0, ((0, 16), (1, 2)))
    w_router = bell_draw(seeds[6], (D, EXPERTS), (0.5 * D ** -0.5), 0.25, ((0, 16),))
    gain_attn = jnp.clip(1.0 + 0.1 * jax.random.normal(seeds[7], (D,), jnp.float32), 0.5, 1.5).astype(jnp.bfloat16)
    gain_moe = jnp.clip(1.0 + 0.1 * jax.random.normal(seeds[8], (D,), jnp.float32), 0.5, 1.5).astype(jnp.bfloat16)
    rel_table = bell_draw(seeds[9], (BUCKETS, H), 1.0, 6.0, ((1, 2),), jnp.float32)
    w_in = bell_draw(seeds[10], (PIECES, D, FF // SPLIT), D ** -0.5, 0.21875, ((0, 16), (2, 2)))
    w_out = bell_draw(seeds[11], (PIECES, FF // SPLIT, D), (2.0 * EXPERTS * FF ** -0.5), 6.0, ((0, 16), (1, 2)))
    lengths = draw_lengths(jax.random.fold_in(seeds[15], 71), 0)
    routes_keys = jax.random.split(jax.random.fold_in(seeds[13], 1), TOKENS // TOK_DEV)
    routes_turns = jax.random.permutation(jax.random.fold_in(seeds[13], 3), TOKENS // TOK_DEV)
    routes = jax.vmap(lambda own, number: deal_out(jax.random.fold_in(seeds[13], 2), own, number, TOK_DEV, EXPERTS, 1, CAP, 2))(routes_keys, routes_turns).reshape((TOKENS, 1))
    keep_mask = touch_ends((jax.random.randint(seeds[14], (TOKENS,), 0, 16) < 15).astype(jnp.int32), jax.random.fold_in(seeds[14], 1), 0, 1)
    return {"tokens": tokens, "cotangent": cotangent, "w_query": w_query, "w_key": w_key, "w_value": w_value, "w_output": w_output, "w_router": w_router, "gain_attn": gain_attn, "gain_moe": gain_moe, "rel_table": rel_table, "w_in": w_in, "w_out": w_out, "lengths": lengths, "routes": routes, "keep_mask": keep_mask}


epsilon = 1e-06
masked_value = -1e+30
bucket_edges = (12, 16, 23, 32, 46, 64, 91)
highest = lax.Precision.HIGHEST

@jax.custom_vjp
def low(v):
    return lax.optimization_barrier(v.astype(jnp.bfloat16)).astype(jnp.float32)

@jax.custom_vjp
def low_back(v):
    return v

def low_keep(v):
    return (low(v), None)

def low_pass(kept, grad):
    return (grad,)

def back_keep(v):
    return (v, None)

def back_low(kept, grad):
    return (low(grad),)
low.defvjp(low_keep, low_pass)
low_back.defvjp(back_keep, back_low)

def bucket_index(offset):
    side = jnp.where(offset > 0, 16, 0).astype(jnp.int32)
    distance = jnp.abs(offset).astype(jnp.int32)
    far_bucket = 8 + sum(((distance >= edge).astype(jnp.int32) for edge in bucket_edges))
    return (side + jnp.where(distance < 8, distance, far_bucket)).astype(jnp.int32)

def rms_scale(values):
    return lax.rsqrt(lax.optimization_barrier(jnp.mean(values * values, axis=-1, keepdims=True)) + epsilon)

def reference(tokens, cotangent, w_query, w_key, w_value, w_output, w_router, gain_attn, gain_moe, rel_table, w_in, w_out, lengths, routes, keep_mask):
    seq_ends = jnp.cumsum(lengths, axis=1).astype(jnp.int32)
    positions = jnp.arange(GRP, dtype=jnp.int32)
    segment = lax.optimization_barrier(jnp.sum((positions[None, :, None] >= seq_ends[:, None, :]).astype(jnp.int32), axis=2)).astype(jnp.int32)
    buckets = bucket_index(positions[None, :] - positions[:, None])
    device_blocks = N_FSDP * N_CTX
    slot_count = device_blocks * CAP
    expert_pick = routes[:, 0].astype(jnp.int32)
    pick_blocks = expert_pick.reshape(device_blocks, TOK_DEV)
    kept_blocks = keep_mask.reshape(device_blocks, TOK_DEV).astype(jnp.int32)
    expert_ids = jnp.arange(EXPERTS, dtype=jnp.int32)
    chosen = (pick_blocks[:, :, None] == expert_ids[None, None, :]).astype(jnp.int32) * kept_blocks[:, :, None]
    earlier = lax.optimization_barrier(jnp.sum((jnp.cumsum(chosen, axis=1).astype(jnp.int32) - chosen) * chosen, axis=2)).astype(jnp.int32)
    slot_place = jnp.where(kept_blocks == 1, pick_blocks * CAP + earlier, EXPERTS * CAP).astype(jnp.int32)
    onehot = (expert_pick[:, None] == expert_ids[None, :]).astype(jnp.float32)
    kept_rows = keep_mask.astype(jnp.float32)

    def forward(inputs, wq, wk, wv, wo, wr, gain_one, gain_two, table, win, wout):
        normed_one = inputs * rms_scale(inputs)
        hidden_one = low(normed_one * gain_one)
        queries = low(low_back(jnp.dot(hidden_one, wq, precision=highest)))
        keys = low(low_back(jnp.dot(hidden_one, wk, precision=highest)))
        values = low(low_back(jnp.dot(hidden_one, wv, precision=highest)))

        def attend(pack_group):
            query_pack, key_pack, value_pack, doc_pack = pack_group
            query_heads = query_pack.reshape(GRP, H, HEAD)
            key_heads = key_pack.reshape(GRP, H, HEAD)
            value_heads = value_pack.reshape(GRP, H, HEAD)
            scores = jnp.einsum('qhd,khd->hqk', query_heads, key_heads, precision=highest) + table.T[:, buckets]
            scores = low_back(scores)
            same_doc = doc_pack[:, None] == doc_pack[None, :]
            scores = jnp.where(same_doc[None], scores, masked_value)
            chances = jax.nn.softmax(scores, axis=-1)
            mixed_rows = jnp.einsum('hqk,khd->qhd', low(chances), value_heads, precision=highest)
            return mixed_rows.reshape(GRP, HD)
        attended = lax.map(jax.checkpoint(attend), (queries.reshape(N_FSDP, GRP, HD), keys.reshape(N_FSDP, GRP, HD), values.reshape(N_FSDP, GRP, HD), segment))
        attended = low(low_back(attended.reshape(TOKENS, HD)))
        branch = low_back(jnp.dot(attended, wo.T, precision=highest))
        middle = inputs + branch
        hidden_two = low(middle * rms_scale(middle) * gain_two)
        logits = low_back(jnp.dot(hidden_two, wr, precision=highest))
        router_probs = jax.nn.softmax(logits, axis=-1)
        gate_value = lax.optimization_barrier(jnp.sum(router_probs * onehot, axis=1)) * kept_rows
        row_blocks = hidden_two.reshape(device_blocks, TOK_DEV, D)
        outbox = jax.vmap(lambda row_block, places_block: jnp.zeros((EXPERTS * CAP, D), row_block.dtype).at[places_block].set(row_block, mode='drop'))(row_blocks, slot_place)
        slot_inbox = outbox.reshape(device_blocks, EXPERTS, CAP, D).transpose(1, 0, 2, 3).reshape(EXPERTS, slot_count, D)
        copies = low_back(jnp.broadcast_to(slot_inbox[:, None], (EXPERTS, SPLIT, slot_count, D)))
        win_parts = win.reshape(EXPERTS, SPLIT, D, FF // SPLIT)
        wout_parts = wout.reshape(EXPERTS, SPLIT, FF // SPLIT, D)
        pre_act = low_back(jnp.einsum('esrd,esdf->esrf', copies, win_parts, precision=highest))
        activity = low(jax.nn.gelu(pre_act, approximate=True))
        part_out = low(jnp.einsum('esrf,esfd->esrd', activity, wout_parts, precision=highest))
        expert_out = low_back(lax.optimization_barrier(jnp.sum(part_out, axis=1)))
        returned = expert_out.reshape(EXPERTS, device_blocks, CAP, D).transpose(1, 0, 2, 3).reshape(device_blocks, EXPERTS * CAP, D)
        picked = jax.vmap(lambda slot_box, places_block: jnp.take(slot_box, places_block, axis=0, mode='fill', fill_value=0.0))(returned, slot_place)
        return middle + gate_value[:, None] * picked.reshape(TOKENS, D)
    primals = (tokens.astype(jnp.float32), w_query.astype(jnp.float32), w_key.astype(jnp.float32), w_value.astype(jnp.float32), w_output.astype(jnp.float32), w_router.astype(jnp.float32), gain_attn.astype(jnp.float32), gain_moe.astype(jnp.float32), rel_table.astype(jnp.float32), w_in.astype(jnp.float32), w_out.astype(jnp.float32))
    output, pullback = jax.vjp(forward, *primals)
    gradients = pullback(cotangent.astype(jnp.float32))
    return (output, gradients[0], gradients[1], gradients[2], gradients[3], gradients[4], gradients[5], gradients[6], gradients[7], gradients[8], gradients[9], gradients[10])
```

```python
import functools

import jax
import jax.numpy as jnp
import numpy as np
from jax import lax
from jax.experimental import pallas as pl
from jax.experimental.pallas import tpu as pltpu
from jax.sharding import PartitionSpec as P

epsilon = 1e-06
masked_value = -1e30
bucket_edges = (12, 16, 23, 32, 46, 64, 91)
highest = lax.Precision.HIGHEST
LANES = 128
STRIP = 128
HEAD_SIZE = 64
VMEM_BYTES = 50 * 1024 * 1024
f32 = jnp.float32
bf16 = jnp.bfloat16
vmem = pl.BlockSpec(memory_space=pltpu.VMEM)
smem = pl.BlockSpec(memory_space=pltpu.SMEM)


def mm(left, right):
    return jnp.dot(left, right, preferred_element_type=f32)


def mm_nt(left, right):
    return lax.dot_general(left, right, (((1,), (1,)), ((), ())), preferred_element_type=f32)


def mm_tn(left, right):
    return lax.dot_general(left, right, (((0,), (0,)), ((), ())), preferred_element_type=f32)


def rms_scale(values):
    return lax.rsqrt(jnp.mean(values * values, axis=-1, keepdims=True) + epsilon)


def iota(shape, dim):
    return lax.broadcasted_iota(jnp.int32, shape, dim)


def bucket_index(offset):
    side = jnp.where(offset > 0, 16, 0).astype(jnp.int32)
    distance = jnp.abs(offset)
    far_bucket = 8 + sum(((distance >= edge).astype(jnp.int32) for edge in bucket_edges))
    return side + jnp.where(distance < 8, distance, far_bucket)


def kernel_call(body, outs, in_specs, out_specs=None, scratch=(), grid=None, flops=0, moved=0):
    extra = {} if grid is None else {"grid": grid}
    return pl.pallas_call(
        body,
        out_shape=outs,
        in_specs=in_specs,
        out_specs=[vmem] * len(outs) if out_specs is None else out_specs,
        scratch_shapes=list(scratch),
        compiler_params=pltpu.CompilerParams(vmem_limit_bytes=VMEM_BYTES),
        cost_estimate=pl.CostEstimate(flops=flops, bytes_accessed=moved, transcendentals=0),
        **extra,
    )


def shape(dims, dtype):
    return jax.ShapeDtypeStruct(tuple(dims), dtype)


def segments(lengths_ref, rows, dim):
    dims = (rows, 1) if dim == 0 else (1, rows)
    places = iota(dims, dim)
    total = jnp.zeros(dims, jnp.int32)
    end = 0
    for entry in range(lengths_ref.shape[1]):
        end = end + lengths_ref[0, entry]
        total = total + (places >= end).astype(jnp.int32)
    return total


def skew(values, right):
    rows, lanes = values.shape
    row = lax.rem(iota((rows, 1), 0), STRIP)
    step = 1
    while step < STRIP:
        moved = pltpu.roll(values, step if right else lanes - step, 1)
        values = jnp.where((row & step) > 0, moved, values)
        step *= 2
    return values


def bias_strips(table_ref, first_head, heads, strip_ref):
    lanes = 4 * STRIP
    bucket = bucket_index(iota((1, lanes), 1) - 2 * STRIP)
    for head in range(heads):
        line = jnp.zeros((1, lanes), f32)
        for entry in range(table_ref.shape[0]):
            line = jnp.where(bucket == entry, table_ref[entry, first_head + head], line)
        strip = skew(jnp.broadcast_to(line, (STRIP, lanes)), True)
        strip_ref[head] = strip[:, STRIP:]


def bias_row(strip_ref, table_ref, head, first_head, block, blocks):
    buckets = table_ref.shape[0]
    parts = []
    for other in range(blocks):
        gap = other - block
        if abs(gap) <= 1:
            parts.append(strip_ref[head, :, (gap + 1) * STRIP : (gap + 2) * STRIP])
        else:
            entry = buckets - 1 if gap > 0 else buckets // 2 - 1
            parts.append(jnp.full((STRIP, STRIP), table_ref[entry, first_head + head], f32))
    return jnp.concatenate(parts, axis=1)


def head_mask(head, lanes):
    lane = iota((1, lanes), 1)
    return (lane >= head * HEAD_SIZE) & (lane < (head + 1) * HEAD_SIZE)


def pick_head(values, head, lanes):
    return jnp.where(head_mask(head, lanes), values, 0.0).astype(bf16)


def attention_forward(heads, extra_rows, *refs):
    (meta, offsets, lengths, table, x_own, x_other) = refs[:6]
    pieces = refs[6 : 6 + extra_rows]
    (h1, q_out, k_out, v_out, o_own, o_other, lse, wall, gains, strips, o_all) = refs[6 + extra_rows :]
    place = meta[0]
    rows = x_own.shape[0]
    group = 2 * rows
    first_head = place * heads
    for index, piece in enumerate(pieces):
        start = pl.multiple_of(offsets[index], 16)
        wall[pl.ds(start, piece.shape[0]), :] = piece[...]
    width = wall.shape[1]
    extras = wall[:, width - LANES :].astype(f32).T
    gain_at = LANES // 2 + 32
    gains[...] = extras[gain_at : gain_at + 8]
    gain_one = gains[0:1]
    for source, start in ((x_own, place * rows), (x_other, (1 - place) * rows)):
        values = source[...].astype(f32)
        h1[pl.ds(pl.multiple_of(start, 16), rows), :] = (
            values * rms_scale(values) * gain_one
        ).astype(bf16)
    qkv = mm(h1[...], wall[...])
    lanes = q_out.shape[1]
    q_out[...] = qkv[:, :lanes].astype(bf16)
    k_out[...] = pltpu.roll(qkv[:, LANES : LANES + lanes], lanes - LANES // 2, 1).astype(bf16)
    v_out[...] = qkv[:, width - lanes :].astype(bf16)
    bias_strips(table, first_head, heads, strips)
    segment_row = segments(lengths, group, 1)
    segment_column = segments(lengths, group, 0)
    keys = k_out[...]
    lane = iota((1, LANES), 1)
    blocks = group // STRIP
    values_of = [pick_head(v_out[...], head, lanes) for head in range(heads)]
    for block in range(blocks):
        first = block * STRIP
        same = segment_column[first : first + STRIP] == segment_row
        total = jnp.zeros((STRIP, lanes), f32)
        totals = jnp.zeros((STRIP, LANES), f32)
        for head in range(heads):
            query = pick_head(q_out[first : first + STRIP, :], head, lanes)
            scores = mm_nt(query, keys) + bias_row(strips, table, head, first_head, block, blocks)
            scores = jnp.where(same, scores, masked_value)
            top = jnp.max(scores, axis=1, keepdims=True)
            raised = jnp.exp(scores - top)
            mass = jnp.sum(raised, axis=1, keepdims=True)
            chances = (raised * (1.0 / mass)).astype(bf16)
            total = total + mm(chances, values_of[head])
            totals = jnp.where(lane == head, top + jnp.log(mass), totals)
        o_all[first : first + STRIP, :] = total.astype(bf16)
        lse[first : first + STRIP, :] = totals
    o_own[...] = o_all[pl.ds(pl.multiple_of(place * rows, 16), rows), :]
    o_other[...] = o_all[pl.ds(pl.multiple_of((1 - place) * rows, 16), rows), :]


def assemble(count, *refs):
    offsets = refs[0]
    out = refs[-1]
    for index in range(count):
        piece = refs[1 + index]
        out[pl.ds(pl.multiple_of(offsets[index], 16), piece.shape[0]), :] = piece[...]


def routed(hidden, extras, routes_column, keep_column, experts):
    logits = mm(hidden, extras)
    lane = iota((1, LANES), 1) - LANES // 2
    valid = (lane >= 0) & (lane < experts)
    logits = jnp.where(valid, logits, masked_value)
    raised = jnp.where(valid, jnp.exp(logits - jnp.max(logits, axis=1, keepdims=True)), 0.0)
    probs = raised / jnp.sum(raised, axis=1, keepdims=True)
    onehot = lane == routes_column
    kept = keep_column.astype(f32)
    gate = jnp.sum(jnp.where(onehot, probs, 0.0), axis=1, keepdims=True) * kept
    return probs, onehot, kept, gate


def slots_by_row(routes_row, keep_row, experts, capacity):
    count = routes_row.shape[1]
    chosen = ((iota((experts, count), 0) == routes_row) & (keep_row == 1)).astype(f32)
    before = (iota((count, count), 0) < iota((count, count), 1)).astype(bf16)
    earlier = mm(chosen.astype(bf16), before)
    rank = jnp.sum(earlier * chosen, axis=0, keepdims=True).astype(jnp.int32)
    return jnp.where(keep_row == 1, routes_row * capacity + rank, -2)


def slots_by_column(routes_column, keep_column, experts, capacity):
    count = routes_column.shape[0]
    chosen = ((iota((count, experts), 1) == routes_column) & (keep_column == 1)).astype(f32)
    before = (iota((count, count), 1) < iota((count, count), 0)).astype(bf16)
    earlier = mm(before, chosen.astype(bf16))
    rank = jnp.sum(earlier * chosen, axis=1, keepdims=True).astype(jnp.int32)
    return jnp.where(keep_column == 1, routes_column * capacity + rank, -2)


def to_experts(experts, capacity, *refs):
    (x_own, cotangent, o_own, o_tp, o_ctx, o_far, wo_own, wo_ctx, extras, gains) = refs[:10]
    (routes_row, routes_column, keep_row, keep_column, slot_h, slot_d) = refs[10:16]
    middle_out, sends = refs[16:]
    lanes = o_own.shape[1]
    branch = None
    for near, far, weights in ((o_own, o_tp, wo_own), (o_ctx, o_far, wo_ctx)):
        shifted = pltpu.roll(far[...].astype(f32), LANES // 2, 1).astype(bf16)
        part = mm_nt(near[...], weights[:, :lanes]) + mm_nt(shifted, weights[:, LANES : LANES + lanes])
        branch = part if branch is None else branch + part
    middle = x_own[...].astype(f32) + branch
    middle_out[...] = middle
    hidden = (middle * rms_scale(middle) * gains[1:2]).astype(bf16)
    _, _, _, gate = routed(hidden, extras[...], routes_column[...], keep_column[...], experts)
    out_grad = (gate * cotangent[...].astype(f32)).astype(bf16)
    slot = slots_by_row(routes_row[...], keep_row[...], experts, capacity)
    pick_h = (slot_h[...] == slot).astype(f32).astype(bf16)
    pick_d = (slot_d[...] == slot).astype(f32).astype(bf16)
    sends[...] = (mm(pick_h, hidden) + mm(pick_d, out_grad)).astype(bf16)


def gelu_both(value):
    scale = 0.7978845608028654
    cubic = 0.044715
    square = value * value
    inner = jnp.tanh(scale * value * (1.0 + cubic * square))
    half = 0.5 * (1.0 + inner)
    slope = half + 0.5 * value * (1.0 - inner * inner) * scale * (1.0 + 3.0 * cubic * square)
    return value * half, slope


def expert_kernel(owners, kinds_rows, chunks, group_owners, *refs):
    (rows_in, base_column, base_row, w_in, w_out) = refs[:5]
    (out, x_out, dy_out, act_out, dpre_out, acc_y, acc_x, full) = refs[5:]
    piece = pl.program_id(0)
    chunk = pl.program_id(1)
    pieces = pl.num_programs(0)
    capacity = kinds_rows
    per_owner = rows_in.shape[0] // owners
    span = group_owners * per_owner
    half = group_owners * capacity
    groups = owners // group_owners

    @pl.when(chunk == 0)
    def _():
        pick = (base_column[...] + piece * capacity == iota((2 * half, span), 1)).astype(f32).astype(bf16)
        for group in range(groups):
            got = mm(pick, rows_in[group * span : (group + 1) * span, :]).astype(bf16)
            x_out[0, group * half : (group + 1) * half, :] = got[:half]
            dy_out[0, group * half : (group + 1) * half, :] = got[half:]
        acc_y[...] = jnp.zeros_like(acc_y)
        acc_x[...] = jnp.zeros_like(acc_x)

    pre = mm(x_out[0], w_in[0])
    act, slope = gelu_both(pre)
    act = act.astype(bf16)
    act_out[0] = act
    acc_y[...] += mm(act, w_out[0])
    dpre = (mm_nt(dy_out[0], w_out[0]) * slope).astype(bf16)
    dpre_out[0] = dpre
    acc_x[...] += mm_nt(dpre, w_in[0])

    @pl.when(chunk == chunks - 1)
    def _():
        pick = (base_row[...] + piece * capacity == iota((span, 2 * half), 0)).astype(f32).astype(bf16)
        for group in range(groups):
            here = slice(group * half, (group + 1) * half)
            both = jnp.concatenate([acc_y[here].astype(bf16), acc_x[here].astype(bf16)], axis=0)
            part = mm(pick, both)
            there = slice(group * span, (group + 1) * span)
            full[there] = jnp.where(piece == 0, part, full[there] + part)

    @pl.when((chunk == chunks - 1) & (piece == pieces - 1))
    def _():
        width = out.shape[2]
        shares = out.shape[0] // owners
        for owner in range(owners):
            for share in range(shares):
                out[owner * shares + share] = full[
                    owner * per_owner : (owner + 1) * per_owner, share * width : (share + 1) * width
                ].astype(bf16)


def weight_grads(x_rows, dpre, act, dy):
    w_in_grad = jnp.einsum("lrd,lrf->ldf", x_rows, dpre, preferred_element_type=f32)
    w_out_grad = jnp.einsum("lrf,lrd->lfd", act, dy, preferred_element_type=f32)
    return w_in_grad, w_out_grad


def from_experts(experts, capacity, *refs):
    rows_in, routes_column, keep_column, slot_y, slot_x, out = refs
    slot = slots_by_column(routes_column[...], keep_column[...], experts, capacity)
    width = rows_in.shape[1]
    pick_y = (slot == slot_y[...]).astype(f32).astype(bf16)
    pick_x = (slot == slot_x[...]).astype(f32).astype(bf16)
    out[:, :width] = mm(pick_y, rows_in[...]).astype(bf16)
    out[:, width:] = mm(pick_x, rows_in[...]).astype(bf16)


def middle_backward(experts, *refs):
    (meta, both_own, both_tp, middle_ref, cotangent, extras, gains, routes_column, keep_column) = refs[:9]
    (result, dmiddle_out, branch_grad, router_grad, gain_grad) = refs[9:]
    share = meta[1]
    width = both_own.shape[1] // 2
    own = both_own[...].astype(f32)
    other = both_tp[...].astype(f32)
    first = jnp.where(share == 0, own, other)
    second = jnp.where(share == 0, other, own)
    picked = jnp.concatenate([first[:, :width], second[:, :width]], axis=1)
    slot_grad = jnp.concatenate([first[:, width:], second[:, width:]], axis=1)
    middle = middle_ref[...]
    scale = rms_scale(middle)
    normed = middle * scale
    gain = gains[1:2]
    hidden = (normed * gain).astype(bf16)
    probs, onehot, kept, gate = routed(
        hidden, extras[...], routes_column[...], keep_column[...], experts
    )
    result[...] = middle + gate * picked
    upstream = cotangent[...].astype(f32)
    gate_grad = jnp.sum(upstream * picked, axis=1, keepdims=True)
    prob_grad = jnp.where(onehot, gate_grad * kept, 0.0)
    logit_grad = (
        probs * (prob_grad - jnp.sum(probs * prob_grad, axis=1, keepdims=True))
    ).astype(bf16)
    router_grad[...] = mm_tn(hidden, logit_grad).astype(bf16)
    hidden_grad = slot_grad + mm_nt(logit_grad, extras[...])
    gain_grad[...] = jnp.broadcast_to(
        jnp.sum(hidden_grad * normed, axis=0, keepdims=True), gain_grad.shape
    )
    grad = hidden_grad * gain
    dmiddle = upstream + scale * (grad - normed * jnp.mean(grad * normed, axis=1, keepdims=True))
    dmiddle_out[...] = dmiddle
    branch_grad[...] = dmiddle.astype(bf16)


def output_grads(*refs):
    (db_own, db_other, o_own, o_other, router_grad, out) = refs
    both = mm_tn(db_own[...], o_own[...]) + mm_tn(db_other[...], o_other[...])
    width = out.shape[1]
    out[:, : width - LANES] = both[:, : width - LANES].astype(bf16)
    out[:, width - LANES :] = (
        both[:, width - LANES :] + router_grad[...].astype(f32)
    ).astype(bf16)


def attention_backward(heads, heads_all, *refs):
    (meta, lengths, table, x_own, x_other, h1, q_in, k_in, v_in, lse, db_own, db_other) = refs[:12]
    (wo_own, wall, gain_two) = refs[12:15]
    (payload, dh1_own, dh1_other, small) = refs[15:19]
    (strips, sums, do_all, dq, dk, dv, dqkv, dh1) = refs[19:]
    place, share = meta[0], meta[1]
    rows = x_own.shape[0]
    group = 2 * rows
    lanes = q_in.shape[1]
    first_head = place * heads
    own_at = pl.ds(pl.multiple_of(place * rows, 16), rows)
    other_at = pl.ds(pl.multiple_of((1 - place) * rows, 16), rows)
    weights = wo_own[:, :lanes]
    do_all[own_at, :] = mm(db_own[...], weights).astype(bf16)
    do_all[other_at, :] = mm(db_other[...], weights).astype(bf16)
    bias_strips(table, first_head, heads, strips)
    segment_row = segments(lengths, group, 1)
    segment_column = segments(lengths, group, 0)
    blocks = group // STRIP
    sums[...] = jnp.zeros_like(sums)
    keys = k_in[...]
    values = v_in[...]
    ahead = [jnp.zeros((STRIP, STRIP), f32) for _ in range(heads)]
    behind = [jnp.zeros((STRIP, STRIP), f32) for _ in range(heads)]
    for block in range(blocks):
        at = slice(block * STRIP, (block + 1) * STRIP)
        same = segment_column[at] == segment_row
        dq_total = jnp.zeros((STRIP, lanes), f32)
        for head in range(heads):
            query = pick_head(q_in[at, :], head, lanes)
            scores = mm_nt(query, keys) + bias_row(strips, table, head, first_head, block, blocks)
            scores = jnp.where(same, scores, masked_value)
            chances = jnp.exp(scores - lse[at, head : head + 1])
            grad = pick_head(do_all[at, :], head, lanes)
            chance_grad = mm_nt(grad, values)
            mean = jnp.sum(chances * chance_grad, axis=1, keepdims=True)
            score_grad = (chances * (chance_grad - mean)).astype(bf16)
            dv_part = mm_tn(chances.astype(bf16), grad)
            dk_part = mm_tn(score_grad, query)
            if block == 0 and head == 0:
                dv[...] = dv_part
                dk[...] = dk_part
            else:
                dv[...] += dv_part
                dk[...] += dk_part
            dq_total = dq_total + mm(score_grad, pick_head(keys, head, lanes))
            rounded = score_grad.astype(f32)
            for other in range(blocks):
                gap = other - block
                part = rounded[:, other * STRIP : (other + 1) * STRIP]
                if abs(gap) <= 1:
                    sums[head, :, (gap + 2) * STRIP : (gap + 3) * STRIP] += part
                elif gap > 0:
                    ahead[head] = ahead[head] + part
                else:
                    behind[head] = behind[head] + part
        dq[at, :] = dq_total
    half = LANES // 2
    dqkv[:, :LANES] = dq[:, :LANES].astype(bf16)
    shifted = pltpu.roll(dk[...], half, 1)
    dqkv[:, LANES : 2 * LANES] = (dq[:, LANES:] + shifted[:, :LANES]).astype(bf16)
    dqkv[:, 2 * LANES : 3 * LANES] = shifted[:, LANES:].astype(bf16)
    dqkv[:, 3 * LANES :] = dv[...].astype(bf16)
    payload[...] = mm_tn(h1[...], dqkv[...]).astype(bf16)
    dh1[...] = mm_nt(dqkv[...], wall[...])
    gain_part = None
    for source, at, target in ((x_own, own_at, dh1_own), (x_other, other_at, dh1_other)):
        values = source[...].astype(f32)
        grad = dh1[at, :]
        target[...] = grad.astype(bf16)
        part = jnp.sum(grad * (values * rms_scale(values)), axis=0, keepdims=True)
        gain_part = part if gain_part is None else gain_part + part
    buckets = table.shape[0]
    spread = skew(sums[...].reshape(heads * STRIP, 4 * STRIP), False)
    diagonals = jnp.sum(spread.reshape(heads, STRIP, 4 * STRIP), axis=1)
    picks = (bucket_index(iota((4 * STRIP, 1), 0) - 2 * STRIP) == iota((1, LANES), 1)).astype(f32)
    in_buckets = jnp.dot(diagonals, picks, precision=highest, preferred_element_type=f32)
    lane = iota((1, LANES), 1)
    row = iota((16, 1), 0)
    table_grad = jnp.zeros((16, LANES), f32)
    for head in range(heads):
        line = in_buckets[head : head + 1]
        line = line + jnp.where(lane == buckets - 1, jnp.sum(ahead[head]), 0.0)
        line = line + jnp.where(lane == buckets // 2 - 1, jnp.sum(behind[head]), 0.0)
        mine = share * (heads_all // 2) + first_head + head
        table_grad = table_grad + jnp.where(row == mine, line, 0.0)
    small[...] = jnp.zeros_like(small)
    small[:16, :] = table_grad
    gain_rows = gain_part.shape[1] // LANES
    once = jnp.where(share == 0, 1.0, 0.0)
    for index in range(gain_rows):
        at = slice(index * LANES, (index + 1) * LANES)
        small[16 + index : 17 + index, :] = gain_part[:, at]
        small[24 + index : 25 + index, :] = gain_two[0:1, at] * once


def input_backward(x_own, dmiddle, gains, near, far, out):
    values = x_own[...].astype(f32)
    scale = rms_scale(values)
    normed = values * scale
    grad = (near[...].astype(f32) + far[...].astype(f32)) * gains[0:1]
    out[...] = dmiddle[...] + scale * (
        grad - normed * jnp.mean(grad * normed, axis=1, keepdims=True)
    )


def swap(value, axis):
    return lax.ppermute(value, axis, [(0, 1), (1, 0)])


def ring_order(count):
    return list(range(0, count, 2)) + list(range(count - 1, 0, -2))


def ring_steps(count):
    order = ring_order(count)
    right = [(order[i], order[(i + 1) % count]) for i in range(count)]
    return order, right, [(b, a) for a, b in right]


def ring_place(count):
    order = ring_order(count)
    inverse = np.zeros(count, np.int32)
    inverse[order] = np.arange(count)
    return jnp.asarray(np.array(order, np.int32)), jnp.asarray(inverse)[lax.axis_index("fsdp")]


def ring_gather(shard, count):
    rows = shard.shape[0]
    order, right, left = ring_steps(count)
    table, place = ring_place(count)
    pieces = [shard]
    starts = [table[place] * rows]
    going_right, going_left = shard, shard
    for step in range(1, count // 2):
        going_right = lax.ppermute(going_right, "fsdp", right)
        going_left = lax.ppermute(going_left, "fsdp", left)
        pieces += [going_right, going_left]
        starts += [table[(place - step) % count] * rows, table[(place + step) % count] * rows]
    half = rows // 2
    pieces += [
        lax.ppermute(going_right[:half], "fsdp", right),
        lax.ppermute(going_left[half:], "fsdp", left),
    ]
    across = table[(place + count // 2) % count] * rows
    starts += [across, across + half]
    return pieces, jnp.stack(starts).astype(jnp.int32)


def gather_rows(shard, count):
    rows = shard.shape[0]
    if rows % 32 == 0 and count % 2 == 0:
        return ring_gather(shard, count)
    return [lax.all_gather(shard, "fsdp", axis=0, tiled=True)], jnp.zeros((1,), jnp.int32)


def sum_rows(payload, count):
    rows = payload.shape[0] // count
    if rows % 32 or count % 2:
        return lax.psum_scatter(payload.astype(f32), "fsdp", scatter_dimension=0, tiled=True)
    order, right, left = ring_steps(count)
    table, place = ring_place(count)
    half = rows // 2

    def mine(distance):
        start = table[(place + distance) % count] * rows
        return lax.dynamic_slice_in_dim(payload, start, rows, 0).astype(f32)

    across = mine(count // 2).astype(bf16)
    going_right, going_left = across[:half], across[half:]
    for step in range(count // 2, 0, -1):
        from_left = lax.ppermute(going_right, "fsdp", right).astype(f32)
        from_right = lax.ppermute(going_left, "fsdp", left).astype(f32)
        if step == count // 2:
            none = jnp.zeros_like(from_left)
            from_left = jnp.concatenate([from_left, none], axis=0)
            from_right = jnp.concatenate([none, from_right], axis=0)
        if step == 1:
            return mine(0) + from_left + from_right
        going_right = (mine(step - 1) + from_left).astype(bf16)
        going_left = (mine(1 - step) + from_right).astype(bf16)


def sum_everywhere(value, counts):
    for axis, count in counts:
        step = 1
        while step < count:
            pairs = [(i, i ^ step) for i in range(count)]
            value = value + lax.ppermute(value, axis, pairs)
            step *= 2
    return value


def body(
    tokens,
    cotangent,
    w_query,
    w_key,
    w_value,
    w_output,
    w_router,
    gain_attn,
    gain_moe,
    rel_table,
    w_in,
    w_out,
    lengths,
    routes,
    keep_mask,
):
    rows, model_width = tokens.shape
    fsdp_count = lax.axis_size("fsdp")
    owners = lax.axis_size(("fsdp", "ctx"))
    tp_count = lax.axis_size("tp")
    place = lax.axis_index("ctx")
    share = lax.axis_index("tp")
    fsdp_place = lax.axis_index("fsdp")
    group = 2 * rows
    experts = w_router.shape[1]
    capacity = max(2, (5 * rows + 4 * experts - 1) // (4 * experts))
    pieces = w_in.shape[0]
    split_count = owners * pieces // experts
    hidden_width = w_in.shape[2]
    heads = rel_table.shape[1] // 2
    heads_all = heads * 2 * tp_count
    width = heads * HEAD_SIZE
    lanes = width + HEAD_SIZE
    shard_rows = w_query.shape[0]
    buckets = rel_table.shape[0]
    meta = jnp.stack([place, share]).astype(jnp.int32)

    def columns(weight, which):
        return lax.dynamic_slice_in_dim(weight, which * width, width, 1)

    extras_width = HEAD_SIZE - experts - 2
    extras_shard = jnp.concatenate(
        [w_router, gain_attn[:, None], gain_moe[:, None], jnp.zeros((shard_rows, extras_width), bf16)],
        axis=1,
    )

    def shard_for(which):
        return jnp.concatenate(
            [columns(w_query, which), columns(w_key, which), columns(w_value, which), extras_shard],
            axis=1,
        )

    def in_order(own, other, axis):
        return jnp.where(
            place == 0,
            jnp.concatenate([own, other], axis=axis),
            jnp.concatenate([other, own], axis=axis),
        )

    shard = in_order(shard_for(place), swap(shard_for(1 - place), "ctx"), 0)
    x_other = swap(tokens, "ctx")
    wo_shard = in_order(columns(w_output, place), swap(columns(w_output, 1 - place), "ctx"), 0)
    wo_shard = jnp.concatenate([wo_shard, swap(wo_shard, "tp")], axis=1)

    wall_pieces, wall_starts = gather_rows(shard, fsdp_count)
    wo_shard, *_ = lax.optimization_barrier((wo_shard, *wall_pieces[-2:]))
    wo_pieces, wo_starts = gather_rows(wo_shard, fsdp_count)

    def full(dims, dtype):
        return shape(dims, dtype)

    wall_width = shard.shape[1]
    h1, q, k, v, o_own, o_other, lse, wall, gains = kernel_call(
        functools.partial(attention_forward, heads, len(wall_pieces)),
        [
            full((group, model_width), bf16),
            full((group, lanes), bf16),
            full((group, lanes), bf16),
            full((group, lanes), bf16),
            full((rows, lanes), bf16),
            full((rows, lanes), bf16),
            full((group, LANES), f32),
            full((model_width, wall_width), bf16),
            full((8, model_width), f32),
        ],
        [smem] * 4 + [vmem] * (2 + len(wall_pieces)),
        scratch=[pltpu.VMEM((heads, STRIP, 3 * STRIP), f32), pltpu.VMEM((group, lanes), bf16)],
        flops=2 * group * model_width * wall_width * 8,
        moved=8 * 1024 * 1024,
    )(meta, wall_starts, lengths, rel_table, tokens, x_other, *wall_pieces)

    wo_own = kernel_call(
        functools.partial(assemble, len(wo_pieces)),
        [full((model_width, wo_shard.shape[1]), bf16)],
        [smem] + [vmem] * len(wo_pieces),
        moved=1024 * 1024,
    )(wo_starts, *wo_pieces)[0]
    wo_ctx = swap(wo_own, "ctx")

    o_tp = swap(o_own, "tp")
    o_ctx = swap(o_other, "ctx")
    o_far = lax.ppermute(o_other, ("ctx", "tp"), [(i, 3 - i) for i in range(4)])

    per_owner = 2 * pieces * capacity
    owner_of = np.repeat(np.arange(owners), per_owner)
    inside = np.tile(np.arange(per_owner), owners)
    kind = inside // (pieces * capacity)
    piece_of = owner_of * pieces + (inside // capacity) % pieces
    slot_of = (piece_of // split_count) * capacity + inside % capacity
    slot_first = np.where(kind == 0, slot_of, -1).astype(np.int32)
    slot_second = np.where(kind == 1, slot_of, -1).astype(np.int32)
    routes_row = routes.reshape(1, rows)
    keep_row = keep_mask.reshape(1, rows)
    keep_column = keep_mask.reshape(rows, 1)
    extras = wall[:, wall_width - LANES :]

    middle, sends = kernel_call(
        functools.partial(to_experts, experts, capacity),
        [full((rows, model_width), f32), full((owners * per_owner, model_width), bf16)],
        [vmem] * 16,
        flops=2 * rows * model_width * (model_width + 2 * owners * per_owner),
        moved=6 * 1024 * 1024,
    )(
        tokens, cotangent, o_own, o_tp, o_ctx, o_far, wo_own, wo_ctx, extras, gains,
        routes_row, routes, keep_row, keep_column, slot_first[:, None], slot_second[:, None],
    )

    arrived = lax.all_to_all(
        sends.reshape(owners, per_owner, model_width),
        ("fsdp", "ctx"),
        split_axis=0,
        concat_axis=0,
        tiled=True,
    ).reshape(owners * per_owner, model_width)

    group_owners = min(16, owners)
    half = group_owners * capacity
    spot = np.arange(2 * half) % half
    base = (
        (spot // capacity) * per_owner
        + (np.arange(2 * half) // half) * pieces * capacity
        + spot % capacity
    ).astype(np.int32)
    chunk_width = 512 if hidden_width % 512 == 0 else hidden_width
    chunks = hidden_width // chunk_width
    slot_rows = owners * capacity
    part_width = model_width // tp_count
    whole = lambda *dims: pl.BlockSpec(dims, lambda i, j: (0,) * len(dims))
    outgoing, x_rows, dy_rows, act, dpre = kernel_call(
        functools.partial(expert_kernel, owners, capacity, chunks, group_owners),
        [
            full((owners * tp_count, per_owner, part_width), bf16),
            full((pieces, slot_rows, model_width), bf16),
            full((pieces, slot_rows, model_width), bf16),
            full((pieces, slot_rows, hidden_width), bf16),
            full((pieces, slot_rows, hidden_width), bf16),
        ],
        [
            whole(owners * per_owner, model_width),
            whole(2 * half, 1),
            whole(1, 2 * half),
            pl.BlockSpec((1, model_width, chunk_width), lambda i, j: (i, 0, j)),
            pl.BlockSpec((1, chunk_width, model_width), lambda i, j: (i, j, 0)),
        ],
        out_specs=[
            whole(owners * tp_count, per_owner, part_width),
            pl.BlockSpec((1, slot_rows, model_width), lambda i, j: (i, 0, 0)),
            pl.BlockSpec((1, slot_rows, model_width), lambda i, j: (i, 0, 0)),
            pl.BlockSpec((1, slot_rows, chunk_width), lambda i, j: (i, 0, j)),
            pl.BlockSpec((1, slot_rows, chunk_width), lambda i, j: (i, 0, j)),
        ],
        scratch=[
            pltpu.VMEM((slot_rows, model_width), f32),
            pltpu.VMEM((slot_rows, model_width), f32),
            pltpu.VMEM((owners * per_owner, model_width), f32),
        ],
        grid=(pieces, chunks),
        flops=8 * pieces * slot_rows * model_width * hidden_width,
        moved=12 * 1024 * 1024,
    )(arrived, base[:, None], base[None, :], w_in, w_out)

    returned = lax.all_to_all(
        outgoing, ("fsdp", "ctx", "tp"), split_axis=0, concat_axis=0, tiled=True
    ).reshape(owners * tp_count * per_owner, part_width)
    w_in_grad, w_out_grad = weight_grads(x_rows, dpre, act, dy_rows)

    back_first = np.repeat(slot_first.reshape(owners, 1, per_owner), tp_count, axis=1).reshape(1, -1)
    back_second = np.repeat(slot_second.reshape(owners, 1, per_owner), tp_count, axis=1).reshape(1, -1)
    both_own = kernel_call(
        functools.partial(from_experts, experts, capacity),
        [full((rows, 2 * part_width), bf16)],
        [vmem] * 5,
        flops=4 * rows * returned.shape[0] * part_width,
        moved=2 * 1024 * 1024,
    )(returned, routes, keep_column, back_first, back_second)[0]
    both_tp = swap(both_own, "tp")

    result, middle_grad, db_own, router_grad, gain_two_part = kernel_call(
        functools.partial(middle_backward, experts),
        [
            full((rows, model_width), f32),
            full((rows, model_width), f32),
            full((rows, model_width), bf16),
            full((model_width, LANES), bf16),
            full((8, model_width), f32),
        ],
        [smem] + [vmem] * 8,
        flops=6 * rows * LANES * model_width,
        moved=6 * 1024 * 1024,
    )(meta, both_own, both_tp, middle, cotangent, extras, gains, routes, keep_column)
    db_other = swap(db_own, "ctx")

    payload_one = kernel_call(
        output_grads,
        [full((model_width, lanes), bf16)],
        [vmem] * 5,
        flops=2 * group * lanes * model_width,
        moved=2 * 1024 * 1024,
    )(db_own, db_other, o_own, o_other, router_grad)[0]
    sums_one = sum_rows(payload_one, fsdp_count)

    payload_two, dh1_own, dh1_other, small = kernel_call(
        functools.partial(attention_backward, heads, heads_all),
        [
            full((model_width, wall_width), bf16),
            full((rows, model_width), bf16),
            full((rows, model_width), bf16),
            full((32, LANES), f32),
        ],
        [smem] * 3 + [vmem] * 12,
        scratch=[
            pltpu.VMEM((heads, STRIP, 3 * STRIP), f32),
            pltpu.VMEM((heads, STRIP, 4 * STRIP), f32),
            pltpu.VMEM((group, lanes), bf16),
            pltpu.VMEM((group, lanes), f32),
            pltpu.VMEM((group, lanes), f32),
            pltpu.VMEM((group, lanes), f32),
            pltpu.VMEM((group, wall_width), bf16),
            pltpu.VMEM((group, model_width), f32),
        ],
        flops=2 * group * model_width * wall_width * 12,
        moved=8 * 1024 * 1024,
    )(
        meta, lengths, rel_table, tokens, x_other, h1, q, k, v, lse, db_own, db_other,
        wo_own, wall, gain_two_part,
    )

    dh1_sum = (dh1_own.astype(f32) + swap(dh1_other, "ctx").astype(f32)).astype(bf16)
    dh1_far = swap(dh1_sum, "tp")
    sums_two = sum_rows(payload_two[:, : 3 * width], fsdp_count)
    small = sum_everywhere(small, (("ctx", 2), ("tp", tp_count), ("fsdp", fsdp_count)))

    input_grad = kernel_call(
        input_backward,
        [full((rows, model_width), f32)],
        [vmem] * 5,
        moved=4 * 1024 * 1024,
    )(tokens, middle_grad, gains, dh1_sum, dh1_far)[0]

    def own_rows(sums):
        own = lax.dynamic_slice_in_dim(sums, place * shard_rows, shard_rows, 0)
        other = lax.dynamic_slice_in_dim(sums, (1 - place) * shard_rows, shard_rows, 0)
        return own, swap(other, "ctx")

    one_own, one_other = own_rows(sums_one)
    two_own, two_other = own_rows(sums_two)
    grads = [
        in_order(two_own[:, at : at + width], two_other[:, at : at + width], 1)
        for at in (0, width, 2 * width)
    ]
    output_grad = in_order(one_own[:, :width], one_other[:, :width], 1)
    router_total = (one_own + one_other)[:, width : width + experts]
    first_row = (fsdp_place * 2 + place) * shard_rows
    gain_rows = model_width // LANES

    def gain_of(first):
        line = small[first : first + gain_rows].reshape(model_width)
        return lax.dynamic_slice_in_dim(line, first_row, shard_rows, 0)

    table_total = lax.dynamic_slice_in_dim(small, share * 2 * heads, 2 * heads, 0)[:, :buckets].T
    return (
        result,
        input_grad,
        grads[0],
        grads[1],
        grads[2],
        output_grad,
        router_total,
        gain_of(16),
        gain_of(24),
        table_total,
        w_in_grad,
        w_out_grad,
    )


def solution(mesh):
    in_specs = (
        P(("fsdp", "ctx"), None),
        P(("fsdp", "ctx"), None),
        P(("fsdp", "ctx"), "tp"),
        P(("fsdp", "ctx"), "tp"),
        P(("fsdp", "ctx"), "tp"),
        P(("fsdp", "ctx"), "tp"),
        P(("fsdp", "ctx"), None),
        P(("fsdp", "ctx")),
        P(("fsdp", "ctx")),
        P(None, "tp"),
        P(("fsdp", "ctx"), None, "tp"),
        P(("fsdp", "ctx"), "tp", None),
        P("fsdp", None),
        P(("fsdp", "ctx"), None),
        P(("fsdp", "ctx")),
    )
    out_specs = (
        P(("fsdp", "ctx"), None),
        P(("fsdp", "ctx"), None),
        P(("fsdp", "ctx"), "tp"),
        P(("fsdp", "ctx"), "tp"),
        P(("fsdp", "ctx"), "tp"),
        P(("fsdp", "ctx"), "tp"),
        P(("fsdp", "ctx"), None),
        P(("fsdp", "ctx")),
        P(("fsdp", "ctx")),
        P(None, "tp"),
        P(("fsdp", "ctx"), None, "tp"),
        P(("fsdp", "ctx"), "tp", None),
    )
    return jax.shard_map(body, mesh=mesh, in_specs=in_specs, out_specs=out_specs, check_vma=False)
```

```python
import functools

import jax
import jax.numpy as jnp
import numpy as np
from jax import lax
from jax.experimental import pallas as pl
from jax.experimental.pallas import tpu as pltpu
from jax.sharding import PartitionSpec as P

epsilon = 1e-06
masked_value = -1e30
bucket_edges = (12, 16, 23, 32, 46, 64, 91)
highest = lax.Precision.HIGHEST
LANES = 128
STRIP = 128
HEAD_SIZE = 64
VMEM_BYTES = 60 * 1024 * 1024
f32 = jnp.float32
bf16 = jnp.bfloat16
vmem = pl.BlockSpec(memory_space=pltpu.VMEM)
smem = pl.BlockSpec(memory_space=pltpu.SMEM)


def mm(left, right):
    return jnp.dot(left, right, preferred_element_type=f32)


def mm_nt(left, right):
    return lax.dot_general(left, right, (((1,), (1,)), ((), ())), preferred_element_type=f32)


def mm_tn(left, right):
    return lax.dot_general(left, right, (((0,), (0,)), ((), ())), preferred_element_type=f32)


def rms_scale(values):
    return lax.rsqrt(jnp.mean(values * values, axis=-1, keepdims=True) + epsilon)


def iota(shape, dim):
    return lax.broadcasted_iota(jnp.int32, shape, dim)


def bucket_index(offset):
    side = jnp.where(offset > 0, 16, 0).astype(jnp.int32)
    distance = jnp.abs(offset)
    far_bucket = 8 + sum(((distance >= edge).astype(jnp.int32) for edge in bucket_edges))
    return side + jnp.where(distance < 8, distance, far_bucket)


def kernel_call(body, outs, in_specs, out_specs=None, scratch=(), grid=None, flops=0, moved=0):
    extra = {} if grid is None else {"grid": grid}
    return pl.pallas_call(
        body,
        out_shape=outs,
        in_specs=in_specs,
        out_specs=[vmem] * len(outs) if out_specs is None else out_specs,
        scratch_shapes=list(scratch),
        compiler_params=pltpu.CompilerParams(vmem_limit_bytes=VMEM_BYTES),
        cost_estimate=pl.CostEstimate(flops=flops, bytes_accessed=moved, transcendentals=0),
        **extra,
    )


def shape(dims, dtype):
    return jax.ShapeDtypeStruct(tuple(dims), dtype)


def segments(lengths_ref, rows, dim):
    dims = (rows, 1) if dim == 0 else (1, rows)
    places = iota(dims, dim)
    total = jnp.zeros(dims, jnp.int32)
    end = 0
    for entry in range(lengths_ref.shape[1]):
        end = end + lengths_ref[0, entry]
        total = total + (places >= end).astype(jnp.int32)
    return total


def skew(values, right):
    rows, lanes = values.shape
    row = lax.rem(iota((rows, 1), 0), STRIP)
    step = 1
    while step < STRIP:
        moved = pltpu.roll(values, step if right else lanes - step, 1)
        values = jnp.where((row & step) > 0, moved, values)
        step *= 2
    return values


def bias_strips(table_ref, first_head, heads, strip_ref):
    lanes = 4 * STRIP
    bucket = bucket_index(iota((1, lanes), 1) - 2 * STRIP)
    for head in range(heads):
        line = jnp.zeros((1, lanes), f32)
        for entry in range(table_ref.shape[0]):
            line = jnp.where(bucket == entry, table_ref[entry, first_head + head], line)
        strip = skew(jnp.broadcast_to(line, (STRIP, lanes)), True)
        strip_ref[head] = strip[:, STRIP:]


def bias_row(strip_ref, table_ref, head, first_head, block, blocks):
    buckets = table_ref.shape[0]
    parts = []
    for other in range(blocks):
        gap = other - block
        if abs(gap) <= 1:
            parts.append(strip_ref[head, :, (gap + 1) * STRIP : (gap + 2) * STRIP])
        else:
            entry = buckets - 1 if gap > 0 else buckets // 2 - 1
            parts.append(jnp.full((STRIP, STRIP), table_ref[entry, first_head + head], f32))
    return jnp.concatenate(parts, axis=1)


def head_mask(head, lanes):
    lane = iota((1, lanes), 1)
    return (lane >= head * HEAD_SIZE) & (lane < (head + 1) * HEAD_SIZE)


def pick_head(values, head, lanes):
    return jnp.where(head_mask(head, lanes), values, 0.0).astype(bf16)


def half_columns(weight, which):
    values = weight[...].astype(f32)
    width = values.shape[1] // 2
    lanes = width + HEAD_SIZE
    high = pltpu.roll(values[:, LANES : LANES + lanes], lanes - HEAD_SIZE, 1)
    picked = jnp.where(which == 0, values[:, :lanes], high)
    return jnp.where(iota((1, lanes), 1) < width, picked, 0.0)


def join(first, second):
    moved = pltpu.roll(second, HEAD_SIZE, 1)
    return first[:, :LANES], first[:, LANES:] + moved[:, :LANES], moved[:, LANES:]


def pack_rows(*refs):
    (meta, w_query, w_key, w_value, w_output, w_router, gain_one, gain_two, out) = refs
    rows = w_query.shape[0]
    experts = w_router.shape[1]
    width = w_query.shape[1] // 2
    lanes = width + HEAD_SIZE
    lane = iota((1, lanes), 1)
    diagonal = iota((rows, rows), 0) == iota((rows, rows), 1)
    placing = (iota((experts, lanes), 0) + width == iota((experts, lanes), 1)).astype(f32)
    extras = mm(w_router[...], placing.astype(bf16))
    for index, gain in enumerate((gain_one, gain_two)):
        column = jnp.sum(
            jnp.where(diagonal, jnp.broadcast_to(gain[...].astype(f32), (rows, rows)), 0.0),
            axis=1,
            keepdims=True,
        )
        extras = extras + jnp.where(lane == width + experts + index, column, 0.0)
    at = 0
    for which in (meta[0], 1 - meta[0]):
        blocks = join(half_columns(w_query, which), half_columns(w_key, which))
        for block in blocks:
            out[:, at : at + LANES] = block.astype(bf16)
            at += LANES
        out[:, at : at + lanes] = (half_columns(w_value, which) + extras).astype(bf16)
        at += lanes
    out[:, at:] = w_output[...]


def interleave(out, lanes, own, other, place, count):
    rows = own.shape[0] // count
    for index in range(count):
        here = slice(index * rows, (index + 1) * rows)
        first = pl.multiple_of((2 * index + place) * rows, 16)
        second = pl.multiple_of((2 * index + 1 - place) * rows, 16)
        out[pl.ds(first, rows), lanes] = own[here, :]
        out[pl.ds(second, rows), lanes] = other[here, :]


def attention_forward(heads, experts, count, *refs):
    (meta, lengths, table, x_own, x_other, rows_own, rows_other) = refs[:7]
    (h1, q_out, k_out, v_out, o_own, o_other, lse, wall, gains, strips, o_all) = refs[7:]
    place = meta[0]
    rows = x_own.shape[0]
    group = 2 * rows
    first_head = place * heads
    interleave(wall, slice(None), rows_own, rows_other, meta[2], count)
    width = wall.shape[1]
    extras = wall[:, width - LANES :].astype(f32).T
    gain_at = HEAD_SIZE + experts
    gains[...] = extras[gain_at : gain_at + 8]
    gain_one = gains[0:1]
    for source, start in ((x_own, place * rows), (x_other, (1 - place) * rows)):
        values = source[...].astype(f32)
        h1[pl.ds(pl.multiple_of(start, 16), rows), :] = (
            values * rms_scale(values) * gain_one
        ).astype(bf16)
    qkv = mm(h1[...], wall[...])
    lanes = q_out.shape[1]
    q_out[...] = qkv[:, :lanes].astype(bf16)
    k_out[...] = pltpu.roll(qkv[:, LANES : LANES + lanes], lanes - HEAD_SIZE, 1).astype(bf16)
    v_out[...] = qkv[:, width - lanes :].astype(bf16)
    bias_strips(table, first_head, heads, strips)
    segment_row = segments(lengths, group, 1)
    segment_column = segments(lengths, group, 0)
    keys = k_out[...]
    lane = iota((1, LANES), 1)
    blocks = group // STRIP
    values_of = [pick_head(v_out[...], head, lanes) for head in range(heads)]
    for block in range(blocks):
        first = block * STRIP
        same = segment_column[first : first + STRIP] == segment_row
        total = jnp.zeros((STRIP, lanes), f32)
        totals = jnp.zeros((STRIP, LANES), f32)
        for head in range(heads):
            query = pick_head(q_out[first : first + STRIP, :], head, lanes)
            scores = mm_nt(query, keys) + bias_row(strips, table, head, first_head, block, blocks)
            scores = jnp.where(same, scores, masked_value)
            top = jnp.max(scores, axis=1, keepdims=True)
            raised = jnp.exp(scores - top)
            mass = jnp.sum(raised, axis=1, keepdims=True)
            chances = (raised * (1.0 / mass)).astype(bf16)
            total = total + mm(chances, values_of[head])
            totals = jnp.where(lane == head, top + jnp.log(mass), totals)
        o_all[first : first + STRIP, :] = total.astype(bf16)
        lse[first : first + STRIP, :] = totals
    o_own[...] = o_all[pl.ds(pl.multiple_of(place * rows, 16), rows), :]
    o_other[...] = o_all[pl.ds(pl.multiple_of((1 - place) * rows, 16), rows), :]


def routed(hidden, extras, routes_column, keep_column, experts):
    logits = mm(hidden, extras)
    lane = iota((1, LANES), 1) - HEAD_SIZE
    valid = (lane >= 0) & (lane < experts)
    logits = jnp.where(valid, logits, masked_value)
    raised = jnp.where(valid, jnp.exp(logits - jnp.max(logits, axis=1, keepdims=True)), 0.0)
    probs = raised / jnp.sum(raised, axis=1, keepdims=True)
    onehot = lane == routes_column
    kept = keep_column.astype(f32)
    gate = jnp.sum(jnp.where(onehot, probs, 0.0), axis=1, keepdims=True) * kept
    return probs, onehot, kept, gate


def slots_by_row(routes_row, keep_row, experts, capacity):
    count = routes_row.shape[1]
    chosen = ((iota((experts, count), 0) == routes_row) & (keep_row == 1)).astype(f32)
    before = (iota((count, count), 0) < iota((count, count), 1)).astype(bf16)
    earlier = mm(chosen.astype(bf16), before)
    rank = jnp.sum(earlier * chosen, axis=0, keepdims=True).astype(jnp.int32)
    return jnp.where(keep_row == 1, routes_row * capacity + rank, -2)


def slots_by_column(routes_column, keep_column, experts, capacity):
    count = routes_column.shape[0]
    chosen = ((iota((count, experts), 1) == routes_column) & (keep_column == 1)).astype(f32)
    before = (iota((count, count), 1) < iota((count, count), 0)).astype(bf16)
    earlier = mm(before, chosen.astype(bf16))
    rank = jnp.sum(earlier * chosen, axis=1, keepdims=True).astype(jnp.int32)
    return jnp.where(keep_column == 1, routes_column * capacity + rank, -2)


def heads_of(own, other, place):
    own = own[...].astype(f32)
    other = other[...].astype(f32)
    first = jnp.where(place == 0, own, other)
    second = jnp.where(place == 0, other, own)
    return jnp.concatenate(join(first, second), axis=1).astype(bf16)


def to_experts(experts, capacity, count, *refs):
    (meta, x_own, cotangent, o_own, o_tp, o_ctx, o_far, wo_own, wo_tp, wo_ctx, wo_far) = refs[:11]
    (extras, gains, routes_row, routes_column, keep_row, keep_column, slot_h, slot_d) = refs[11:19]
    middle_out, sends, wo_out, wo_other = refs[19:]
    place, start = meta[0], meta[2]
    interleave(wo_out, slice(None), wo_own, wo_ctx, start, count)
    interleave(wo_other, slice(None), wo_tp, wo_far, start, count)
    branch = mm_nt(heads_of(o_own, o_ctx, place), wo_out[...])
    branch = branch + mm_nt(heads_of(o_tp, o_far, place), wo_other[...])
    middle = x_own[...].astype(f32) + branch
    middle_out[...] = middle
    hidden = (middle * rms_scale(middle) * gains[1:2]).astype(bf16)
    _, _, _, gate = routed(hidden, extras[...], routes_column[...], keep_column[...], experts)
    out_grad = (gate * cotangent[...].astype(f32)).astype(bf16)
    slot = slots_by_row(routes_row[...], keep_row[...], experts, capacity)
    pick_h = (slot_h[...] == slot).astype(f32).astype(bf16)
    pick_d = (slot_d[...] == slot).astype(f32).astype(bf16)
    sends[...] = (mm(pick_h, hidden) + mm(pick_d, out_grad)).astype(bf16)


def gelu_both(value):
    scale = 0.7978845608028654
    cubic = 0.044715
    square = value * value
    inner = jnp.tanh(scale * value * (1.0 + cubic * square))
    half = 0.5 * (1.0 + inner)
    slope = half + 0.5 * value * (1.0 - inner * inner) * scale * (1.0 + 3.0 * cubic * square)
    return value * half, slope


def expert_kernel(owners, kinds_rows, chunks, group_owners, *refs):
    (rows_in, base_column, base_row, w_in, w_out) = refs[:5]
    (out, x_out, dy_out, act_out, dpre_out, acc_y, acc_x, full) = refs[5:]
    piece = pl.program_id(0)
    chunk = pl.program_id(1)
    pieces = pl.num_programs(0)
    capacity = kinds_rows
    per_owner = rows_in.shape[0] // owners
    span = group_owners * per_owner
    half = group_owners * capacity
    groups = owners // group_owners

    @pl.when(chunk == 0)
    def _():
        pick = (base_column[...] + piece * capacity == iota((2 * half, span), 1)).astype(f32).astype(bf16)
        for group in range(groups):
            got = mm(pick, rows_in[group * span : (group + 1) * span, :]).astype(bf16)
            x_out[0, group * half : (group + 1) * half, :] = got[:half]
            dy_out[0, group * half : (group + 1) * half, :] = got[half:]
        acc_y[...] = jnp.zeros_like(acc_y)
        acc_x[...] = jnp.zeros_like(acc_x)

    pre = mm(x_out[0], w_in[0])
    act, slope = gelu_both(pre)
    act = act.astype(bf16)
    act_out[0] = act
    acc_y[...] += mm(act, w_out[0])
    dpre = (mm_nt(dy_out[0], w_out[0]) * slope).astype(bf16)
    dpre_out[0] = dpre
    acc_x[...] += mm_nt(dpre, w_in[0])

    @pl.when(chunk == chunks - 1)
    def _():
        pick = (base_row[...] + piece * capacity == iota((span, 2 * half), 0)).astype(f32).astype(bf16)
        for group in range(groups):
            here = slice(group * half, (group + 1) * half)
            both = jnp.concatenate([acc_y[here].astype(bf16), acc_x[here].astype(bf16)], axis=0)
            part = mm(pick, both)
            there = slice(group * span, (group + 1) * span)
            full[there] = jnp.where(piece == 0, part, full[there] + part)

    @pl.when((chunk == chunks - 1) & (piece == pieces - 1))
    def _():
        width = out.shape[2]
        shares = out.shape[0] // owners
        for owner in range(owners):
            for share in range(shares):
                out[owner * shares + share] = full[
                    owner * per_owner : (owner + 1) * per_owner, share * width : (share + 1) * width
                ].astype(bf16)


def weight_grads(x_rows, dpre, act, dy):
    w_in_grad = jnp.einsum("lrd,lrf->ldf", x_rows, dpre, preferred_element_type=f32)
    w_out_grad = jnp.einsum("lrf,lrd->lfd", act, dy, preferred_element_type=f32)
    return w_in_grad, w_out_grad


def from_experts(experts, capacity, *refs):
    rows_in, routes_column, keep_column, slot_y, slot_x, out = refs
    slot = slots_by_column(routes_column[...], keep_column[...], experts, capacity)
    width = rows_in.shape[1]
    pick_y = (slot == slot_y[...]).astype(f32).astype(bf16)
    pick_x = (slot == slot_x[...]).astype(f32).astype(bf16)
    out[:, :width] = mm(pick_y, rows_in[...]).astype(bf16)
    out[:, width:] = mm(pick_x, rows_in[...]).astype(bf16)


def column_of(line):
    return jnp.broadcast_to(line, (LANES, line.shape[1])).T[:, :1]


def middle_backward(experts, *refs):
    (meta, both_own, both_tp, middle_ref, cotangent, extras, gains, routes_column, keep_column) = refs[:9]
    (result, dmiddle_out, branch_grad, router_grad) = refs[9:]
    share = meta[1]
    width = both_own.shape[1] // 2
    own = both_own[...].astype(f32)
    other = both_tp[...].astype(f32)
    first = jnp.where(share == 0, own, other)
    second = jnp.where(share == 0, other, own)
    picked = jnp.concatenate([first[:, :width], second[:, :width]], axis=1)
    slot_grad = jnp.concatenate([first[:, width:], second[:, width:]], axis=1)
    middle = middle_ref[...]
    scale = rms_scale(middle)
    normed = middle * scale
    gain = gains[1:2]
    hidden = (normed * gain).astype(bf16)
    probs, onehot, kept, gate = routed(
        hidden, extras[...], routes_column[...], keep_column[...], experts
    )
    result[...] = middle + gate * picked
    upstream = cotangent[...].astype(f32)
    gate_grad = jnp.sum(upstream * picked, axis=1, keepdims=True)
    prob_grad = jnp.where(onehot, gate_grad * kept, 0.0)
    logit_grad = (
        probs * (prob_grad - jnp.sum(probs * prob_grad, axis=1, keepdims=True))
    ).astype(bf16)
    hidden_grad = slot_grad + mm_nt(logit_grad, extras[...])
    gain_grad = column_of(jnp.sum(hidden_grad * normed, axis=0, keepdims=True))
    lane = iota((1, LANES), 1)
    router_grad[...] = jnp.where(
        lane == HEAD_SIZE + experts, gain_grad, mm_tn(hidden, logit_grad)
    ).astype(bf16)
    grad = hidden_grad * gain
    dmiddle = upstream + scale * (grad - normed * jnp.mean(grad * normed, axis=1, keepdims=True))
    dmiddle_out[...] = dmiddle
    branch_grad[...] = dmiddle.astype(bf16)


def attention_backward(heads, shard, *refs):
    (meta, lengths, table, x_own, x_other, h1, q_in, k_in, v_in, lse, db_own, db_other) = refs[:12]
    (o_own, o_other, wo_ref, wall, router_grad) = refs[12:17]
    (payload, dh1_own, dh1_other) = refs[17:20]
    (strips, sums, do_all, dq, dk, dv, dqkv, dh1) = refs[20:]
    place = meta[0]
    rows = x_own.shape[0]
    group = 2 * rows
    lanes = q_in.shape[1]
    first_head = place * heads
    own_at = pl.ds(pl.multiple_of(place * rows, 16), rows)
    other_at = pl.ds(pl.multiple_of((1 - place) * rows, 16), rows)
    for source, at in ((db_own, own_at), (db_other, other_at)):
        both = mm(source[...], wo_ref[...])
        high = pltpu.roll(both[:, LANES : LANES + lanes], lanes - HEAD_SIZE, 1)
        do_all[at, :] = jnp.where(place == 0, both[:, :lanes], high).astype(bf16)
    bias_strips(table, first_head, heads, strips)
    segment_row = segments(lengths, group, 1)
    segment_column = segments(lengths, group, 0)
    blocks = group // STRIP
    sums[...] = jnp.zeros_like(sums)
    keys = k_in[...]
    values = v_in[...]
    ahead = [jnp.zeros((STRIP, STRIP), f32) for _ in range(heads)]
    behind = [jnp.zeros((STRIP, STRIP), f32) for _ in range(heads)]
    for block in range(blocks):
        at = slice(block * STRIP, (block + 1) * STRIP)
        same = segment_column[at] == segment_row
        dq_total = jnp.zeros((STRIP, lanes), f32)
        for head in range(heads):
            query = pick_head(q_in[at, :], head, lanes)
            scores = mm_nt(query, keys) + bias_row(strips, table, head, first_head, block, blocks)
            scores = jnp.where(same, scores, masked_value)
            chances = jnp.exp(scores - lse[at, head : head + 1])
            grad = pick_head(do_all[at, :], head, lanes)
            chance_grad = mm_nt(grad, values)
            mean = jnp.sum(chances * chance_grad, axis=1, keepdims=True)
            score_grad = (chances * (chance_grad - mean)).astype(bf16)
            dv_part = mm_tn(chances.astype(bf16), grad)
            dk_part = mm_tn(score_grad, query)
            if block == 0 and head == 0:
                dv[...] = dv_part
                dk[...] = dk_part
            else:
                dv[...] += dv_part
                dk[...] += dk_part
            dq_total = dq_total + mm(score_grad, pick_head(keys, head, lanes))
            rounded = score_grad.astype(f32)
            for other in range(blocks):
                gap = other - block
                part = rounded[:, other * STRIP : (other + 1) * STRIP]
                if abs(gap) <= 1:
                    sums[head, :, (gap + 2) * STRIP : (gap + 3) * STRIP] += part
                elif gap > 0:
                    ahead[head] = ahead[head] + part
                else:
                    behind[head] = behind[head] + part
        dq[at, :] = dq_total
    half = HEAD_SIZE
    dqkv[:, :LANES] = dq[:, :LANES].astype(bf16)
    shifted = pltpu.roll(dk[...], half, 1)
    dqkv[:, LANES : 2 * LANES] = (dq[:, LANES:] + shifted[:, :LANES]).astype(bf16)
    dqkv[:, 2 * LANES : 3 * LANES] = shifted[:, LANES:].astype(bf16)
    dqkv[:, 3 * LANES :] = dv[...].astype(bf16)
    dh1[...] = mm_nt(dqkv[...], wall[...])
    gain_part = None
    for source, at, target in ((x_own, own_at, dh1_own), (x_other, other_at, dh1_other)):
        values = source[...].astype(f32)
        grad = dh1[at, :]
        target[...] = grad.astype(bf16)
        part = jnp.sum(grad * (values * rms_scale(values)), axis=0, keepdims=True)
        gain_part = part if gain_part is None else gain_part + part
    buckets = table.shape[0]
    spread = skew(sums[...].reshape(heads * STRIP, 4 * STRIP), False)
    diagonals = jnp.sum(spread.reshape(heads, STRIP, 4 * STRIP), axis=1)
    picks = (bucket_index(iota((4 * STRIP, 1), 0) - 2 * STRIP) == iota((1, LANES), 1)).astype(f32)
    in_buckets = jnp.dot(diagonals, picks, precision=highest, preferred_element_type=f32)
    lane = iota((1, LANES), 1)
    row = lax.rem(iota((wall.shape[0], 1), 0), shard)
    riders = jnp.where(lane == HEAD_SIZE, column_of(gain_part), 0.0)
    for head in range(heads):
        line = in_buckets[head : head + 1]
        line = line + jnp.where(lane == buckets - 1, jnp.sum(ahead[head]), 0.0)
        line = line + jnp.where(lane == buckets // 2 - 1, jnp.sum(behind[head]), 0.0)
        riders = riders + jnp.where(row == head, pltpu.roll(line, HEAD_SIZE + 1, 1), 0.0)
    width = wall.shape[1]
    grads = mm_tn(h1[...], dqkv[...])
    payload[:, : width - LANES] = grads[:, : width - LANES].astype(bf16)
    payload[:, width - LANES : width] = (grads[:, width - LANES :] + riders).astype(bf16)
    grads = mm_tn(db_own[...], o_own[...]) + mm_tn(db_other[...], o_other[...])
    payload[:, width : width + lanes - LANES] = grads[:, : lanes - LANES].astype(bf16)
    payload[:, width + lanes - LANES :] = (
        grads[:, lanes - LANES :] + router_grad[...].astype(f32)
    ).astype(bf16)


def shards_of_sums(experts, buckets, heads, *refs):
    (meta, sums, other, from_tp, from_far) = refs[:5]
    (query_out, key_out, value_out, output_out, router_out, gain_one, gain_two, table) = refs[5:]
    place = meta[0]
    rows, width = query_out.shape[0], query_out.shape[1] // 2
    lanes = width + HEAD_SIZE
    wide = 3 * width + HEAD_SIZE
    own = jnp.where(place == 0, sums[:rows, :], sums[rows : 2 * rows, :])
    more = other[:rows, :]
    lane = iota((1, lanes), 1)
    for at, moved, out in (
        (0, False, query_out),
        (LANES, True, key_out),
        (2 * width, False, value_out),
        (wide, False, output_out),
    ):
        parts = [values[:, at : at + lanes] for values in (own, more)]
        if moved:
            parts = [pltpu.roll(part, lanes - HEAD_SIZE, 1) for part in parts]
        parts = [jnp.where(lane < width, part, 0.0) for part in parts]
        first = jnp.where(place == 0, parts[0], parts[1])
        second = jnp.where(place == 0, parts[1], parts[0])
        for index, block in enumerate(join(first, second)):
            out[:, index * LANES : (index + 1) * LANES] = block
    total = (own + more)[:, wide + lanes - LANES :]
    router_out[...] = total
    gain_two[...] = total.T[HEAD_SIZE + experts : HEAD_SIZE + experts + 1, :]
    line = (own + more)[:, wide - LANES : wide] + (from_tp[...] + from_far[...])
    gain_one[...] = line.T[HEAD_SIZE : HEAD_SIZE + 1, :]
    own_lines = pltpu.roll(sums[:8, wide - LANES : wide], LANES - HEAD_SIZE - 1, 1)
    other_lines = pltpu.roll(other[rows : rows + 8, wide - LANES : wide], LANES - HEAD_SIZE - 1, 1)
    table[...] = jnp.zeros_like(table)
    table[:heads, :] = jnp.where(place == 0, own_lines, other_lines)[:heads]
    table[heads : 2 * heads, :] = jnp.where(place == 0, other_lines, own_lines)[:heads]


def input_backward(x_own, dmiddle, gains, near, far, out):
    values = x_own[...].astype(f32)
    scale = rms_scale(values)
    normed = values * scale
    grad = (near[...].astype(f32) + far[...].astype(f32)) * gains[0:1]
    out[...] = dmiddle[...] + scale * (
        grad - normed * jnp.mean(grad * normed, axis=1, keepdims=True)
    )


def swap(value, axis):
    return lax.ppermute(value, axis, [(0, 1), (1, 0)])


def ring_order(count):
    return list(range(0, count, 2)) + list(range(count - 1, 0, -2))


def ring_steps(count):
    order = ring_order(count)
    right = [(order[i], order[(i + 1) % count]) for i in range(count)]
    return order, right, [(b, a) for a, b in right]


def ring_place(count):
    order = ring_order(count)
    inverse = np.zeros(count, np.int32)
    inverse[order] = np.arange(count)
    return jnp.asarray(np.array(order, np.int32)), jnp.asarray(inverse)[lax.axis_index("fsdp")]


def sum_rows(payload, count):
    rows = payload.shape[0] // count
    if rows % 32 or count % 2:
        return lax.psum_scatter(payload.astype(f32), "fsdp", scatter_dimension=0, tiled=True)
    order, right, left = ring_steps(count)
    table, place = ring_place(count)
    half = rows // 2

    def mine(distance):
        start = table[(place + distance) % count] * rows
        return lax.dynamic_slice_in_dim(payload, start, rows, 0).astype(f32)

    across = mine(count // 2).astype(bf16)
    going_right, going_left = across[:half], across[half:]
    for step in range(count // 2, 0, -1):
        from_left = lax.ppermute(going_right, "fsdp", right).astype(f32)
        from_right = lax.ppermute(going_left, "fsdp", left).astype(f32)
        if step == count // 2:
            none = jnp.zeros_like(from_left)
            from_left = jnp.concatenate([from_left, none], axis=0)
            from_right = jnp.concatenate([none, from_right], axis=0)
        if step == 1:
            return mine(0) + from_left + from_right
        going_right = (mine(step - 1) + from_left).astype(bf16)
        going_left = (mine(1 - step) + from_right).astype(bf16)


def body(
    tokens,
    cotangent,
    w_query,
    w_key,
    w_value,
    w_output,
    w_router,
    gain_attn,
    gain_moe,
    rel_table,
    w_in,
    w_out,
    lengths,
    routes,
    keep_mask,
):
    rows, model_width = tokens.shape
    fsdp_count = lax.axis_size("fsdp")
    owners = lax.axis_size(("fsdp", "ctx"))
    tp_count = lax.axis_size("tp")
    place = lax.axis_index("ctx")
    share = lax.axis_index("tp")
    fsdp_place = lax.axis_index("fsdp")
    group = 2 * rows
    experts = w_router.shape[1]
    capacity = max(2, (5 * rows + 4 * experts - 1) // (4 * experts))
    pieces = w_in.shape[0]
    split_count = owners * pieces // experts
    hidden_width = w_in.shape[2]
    heads = rel_table.shape[1] // 2
    heads_all = heads * 2 * tp_count
    width = heads * HEAD_SIZE
    lanes = width + HEAD_SIZE
    shard_rows = w_query.shape[0]
    buckets = rel_table.shape[0]
    meta = jnp.stack([place, share]).astype(jnp.int32)

    def full(dims, dtype):
        return shape(dims, dtype)

    wide = 3 * width + HEAD_SIZE
    packed = kernel_call(
        pack_rows,
        [full((shard_rows, 2 * wide + 2 * width), bf16)],
        [smem] + [vmem] * 7,
        moved=512 * 1024,
    )(meta, w_query, w_key, w_value, w_output, w_router, gain_attn[None, :], gain_moe[None, :])[0]
    x_other = swap(tokens, "ctx")
    gathered = lax.all_gather(packed, "fsdp", axis=0, tiled=True)
    rows_own, rows_other = gathered[:, :wide], swap(gathered[:, wide : 2 * wide], "ctx")
    wo_own = gathered[:, 2 * wide :]
    count = fsdp_count
    start = place

    def ordered(own, other):
        if shard_rows % 16 == 0:
            return own, other
        dims = (fsdp_count, 1, shard_rows, own.shape[1])
        pair = in_order(own.reshape(dims), other.reshape(dims), 1).reshape(2 * own.shape[0], -1)
        return pair[: own.shape[0]], pair[own.shape[0] :]

    def in_order(own, other, axis):
        return jnp.where(
            place == 0,
            jnp.concatenate([own, other], axis=axis),
            jnp.concatenate([other, own], axis=axis),
        )

    if shard_rows % 16:
        count, start = 1, 0 * place
    meta = jnp.stack([place, share, start]).astype(jnp.int32)
    rows_own, rows_other = ordered(rows_own, rows_other)
    h1, q, k, v, o_own, o_other, lse, wall, gains = kernel_call(
        functools.partial(attention_forward, heads, experts, count),
        [
            full((group, model_width), bf16),
            full((group, lanes), bf16),
            full((group, lanes), bf16),
            full((group, lanes), bf16),
            full((rows, lanes), bf16),
            full((rows, lanes), bf16),
            full((group, LANES), f32),
            full((model_width, wide), bf16),
            full((8, model_width), f32),
        ],
        [smem] * 3 + [vmem] * 4,
        scratch=[pltpu.VMEM((heads, STRIP, 3 * STRIP), f32), pltpu.VMEM((group, lanes), bf16)],
        flops=2 * group * model_width * wide * 8,
        moved=8 * 1024 * 1024,
    )(meta, lengths, rel_table, tokens, x_other, rows_own, rows_other)
    wo_tp = swap(wo_own, "tp")
    wo_ctx = swap(wo_own, "ctx")
    wo_far = swap(wo_tp, "ctx")
    wo_own, wo_ctx = ordered(wo_own, wo_ctx)
    wo_tp, wo_far = ordered(wo_tp, wo_far)

    o_tp = swap(o_own, "tp")
    o_ctx = swap(o_other, "ctx")
    o_far = lax.ppermute(o_other, ("ctx", "tp"), [(i, 3 - i) for i in range(4)])

    per_owner = 2 * pieces * capacity
    owner_of = np.repeat(np.arange(owners), per_owner)
    inside = np.tile(np.arange(per_owner), owners)
    kind = inside // (pieces * capacity)
    piece_of = owner_of * pieces + (inside // capacity) % pieces
    slot_of = (piece_of // split_count) * capacity + inside % capacity
    slot_first = np.where(kind == 0, slot_of, -1).astype(np.int32)
    slot_second = np.where(kind == 1, slot_of, -1).astype(np.int32)
    routes_row = routes.reshape(1, rows)
    keep_row = keep_mask.reshape(1, rows)
    keep_column = keep_mask.reshape(rows, 1)
    extras = wall[:, wide - LANES :]

    middle, sends, wo_full = kernel_call(
        functools.partial(to_experts, experts, capacity, count),
        [
            full((rows, model_width), f32),
            full((owners * per_owner, model_width), bf16),
            full((model_width, 2 * width), bf16),
        ],
        [smem] + [vmem] * 18,
        scratch=[pltpu.VMEM((model_width, 2 * width), bf16)],
        flops=2 * rows * model_width * (model_width + 2 * owners * per_owner),
        moved=6 * 1024 * 1024,
    )(
        meta, tokens, cotangent, o_own, o_tp, o_ctx, o_far, wo_own, wo_tp, wo_ctx, wo_far, extras,
        gains, routes_row, routes, keep_row, keep_column, slot_first[:, None], slot_second[:, None],
    )

    arrived = lax.all_to_all(
        sends.reshape(owners, per_owner, model_width),
        ("fsdp", "ctx"),
        split_axis=0,
        concat_axis=0,
        tiled=True,
    ).reshape(owners * per_owner, model_width)

    group_owners = min(16, owners)
    half = group_owners * capacity
    spot = np.arange(2 * half) % half
    base = (
        (spot // capacity) * per_owner
        + (np.arange(2 * half) // half) * pieces * capacity
        + spot % capacity
    ).astype(np.int32)
    chunk_width = 512 if hidden_width % 512 == 0 else hidden_width
    chunks = hidden_width // chunk_width
    slot_rows = owners * capacity
    part_width = model_width // tp_count
    whole = lambda *dims: pl.BlockSpec(dims, lambda i, j: (0,) * len(dims))
    outgoing, x_rows, dy_rows, act, dpre = kernel_call(
        functools.partial(expert_kernel, owners, capacity, chunks, group_owners),
        [
            full((owners * tp_count, per_owner, part_width), bf16),
            full((pieces, slot_rows, model_width), bf16),
            full((pieces, slot_rows, model_width), bf16),
            full((pieces, slot_rows, hidden_width), bf16),
            full((pieces, slot_rows, hidden_width), bf16),
        ],
        [
            whole(owners * per_owner, model_width),
            whole(2 * half, 1),
            whole(1, 2 * half),
            pl.BlockSpec((1, model_width, chunk_width), lambda i, j: (i, 0, j)),
            pl.BlockSpec((1, chunk_width, model_width), lambda i, j: (i, j, 0)),
        ],
        out_specs=[
            whole(owners * tp_count, per_owner, part_width),
            pl.BlockSpec((1, slot_rows, model_width), lambda i, j: (i, 0, 0)),
            pl.BlockSpec((1, slot_rows, model_width), lambda i, j: (i, 0, 0)),
            pl.BlockSpec((1, slot_rows, chunk_width), lambda i, j: (i, 0, j)),
            pl.BlockSpec((1, slot_rows, chunk_width), lambda i, j: (i, 0, j)),
        ],
        scratch=[
            pltpu.VMEM((slot_rows, model_width), f32),
            pltpu.VMEM((slot_rows, model_width), f32),
            pltpu.VMEM((owners * per_owner, model_width), f32),
        ],
        grid=(pieces, chunks),
        flops=8 * pieces * slot_rows * model_width * hidden_width,
        moved=12 * 1024 * 1024,
    )(arrived, base[:, None], base[None, :], w_in, w_out)

    returned = lax.all_to_all(
        outgoing, ("fsdp", "ctx", "tp"), split_axis=0, concat_axis=0, tiled=True
    ).reshape(owners * tp_count * per_owner, part_width)
    w_in_grad, w_out_grad = weight_grads(x_rows, dpre, act, dy_rows)
    returned, w_in_grad, w_out_grad = lax.optimization_barrier((returned, w_in_grad, w_out_grad))

    back_first = np.repeat(slot_first.reshape(owners, 1, per_owner), tp_count, axis=1).reshape(1, -1)
    back_second = np.repeat(slot_second.reshape(owners, 1, per_owner), tp_count, axis=1).reshape(1, -1)
    both_own = kernel_call(
        functools.partial(from_experts, experts, capacity),
        [full((rows, 2 * part_width), bf16)],
        [vmem] * 5,
        flops=4 * rows * returned.shape[0] * part_width,
        moved=2 * 1024 * 1024,
    )(returned, routes, keep_column, back_first, back_second)[0]
    both_tp = swap(both_own, "tp")

    result, middle_grad, db_own, router_grad = kernel_call(
        functools.partial(middle_backward, experts),
        [
            full((rows, model_width), f32),
            full((rows, model_width), f32),
            full((rows, model_width), bf16),
            full((model_width, LANES), bf16),
        ],
        [smem] + [vmem] * 8,
        flops=6 * rows * LANES * model_width,
        moved=6 * 1024 * 1024,
    )(meta, both_own, both_tp, middle, cotangent, extras, gains, routes, keep_column)
    db_other = swap(db_own, "ctx")

    payload, dh1_own, dh1_other = kernel_call(
        functools.partial(attention_backward, heads, model_width // fsdp_count),
        [
            full((model_width, wide + lanes), bf16),
            full((rows, model_width), bf16),
            full((rows, model_width), bf16),
        ],
        [smem] * 3 + [vmem] * 14,
        scratch=[
            pltpu.VMEM((heads, STRIP, 3 * STRIP), f32),
            pltpu.VMEM((heads, STRIP, 4 * STRIP), f32),
            pltpu.VMEM((group, lanes), bf16),
            pltpu.VMEM((group, lanes), f32),
            pltpu.VMEM((group, lanes), f32),
            pltpu.VMEM((group, lanes), f32),
            pltpu.VMEM((group, wide), bf16),
            pltpu.VMEM((group, model_width), f32),
        ],
        flops=2 * group * model_width * wide * 12,
        moved=8 * 1024 * 1024,
    )(
        meta, lengths, rel_table, tokens, x_other, h1, q, k, v, lse, db_own, db_other,
        o_own, o_other, wo_full, wall, router_grad,
    )

    dh1_sum = (dh1_own.astype(f32) + swap(dh1_other, "ctx").astype(f32)).astype(bf16)
    dh1_far = swap(dh1_sum, "tp")
    sums = sum_rows(payload, fsdp_count)
    input_grad = kernel_call(
        input_backward,
        [full((rows, model_width), f32)],
        [vmem] * 5,
        moved=4 * 1024 * 1024,
    )(tokens, middle_grad, gains, dh1_sum, dh1_far)[0]

    not_own = lax.dynamic_slice_in_dim(sums, (1 - place) * shard_rows, shard_rows, 0)
    riders = slice(wide - LANES, wide)
    own_riders = lax.dynamic_slice_in_dim(sums, place * shard_rows, shard_rows, 0)[:, riders]
    other = swap(jnp.concatenate([not_own, sums[:8]], axis=0), "ctx")
    from_tp = swap(own_riders, "tp")
    from_far = lax.ppermute(not_own[:, riders], ("ctx", "tp"), [(i, 3 - i) for i in range(4)])
    shard = full((shard_rows, 2 * width), f32)
    query_grad, key_grad, value_grad, output_grad, router_sum, gain_one, gain_two, table_grad = kernel_call(
        functools.partial(shards_of_sums, experts, buckets, heads),
        [shard] * 4
        + [
            full((shard_rows, LANES), f32),
            full((1, shard_rows), f32),
            full((1, shard_rows), f32),
            full((8, LANES), f32),
        ],
        [smem] + [vmem] * 4,
        moved=1024 * 1024,
    )(meta, sums, other, from_tp, from_far)
    return (
        result,
        input_grad,
        query_grad,
        key_grad,
        value_grad,
        output_grad,
        router_sum[:, HEAD_SIZE : HEAD_SIZE + experts],
        gain_one.reshape(shard_rows),
        gain_two.reshape(shard_rows),
        table_grad[: 2 * heads, :buckets].T,
        w_in_grad,
        w_out_grad,
    )


def solution(mesh):
    in_specs = (
        P(("fsdp", "ctx"), None),
        P(("fsdp", "ctx"), None),
        P(("fsdp", "ctx"), "tp"),
        P(("fsdp", "ctx"), "tp"),
        P(("fsdp", "ctx"), "tp"),
        P(("fsdp", "ctx"), "tp"),
        P(("fsdp", "ctx"), None),
        P(("fsdp", "ctx")),
        P(("fsdp", "ctx")),
        P(None, "tp"),
        P(("fsdp", "ctx"), None, "tp"),
        P(("fsdp", "ctx"), "tp", None),
        P("fsdp", None),
        P(("fsdp", "ctx"), None),
        P(("fsdp", "ctx")),
    )
    out_specs = (
        P(("fsdp", "ctx"), None),
        P(("fsdp", "ctx"), None),
        P(("fsdp", "ctx"), "tp"),
        P(("fsdp", "ctx"), "tp"),
        P(("fsdp", "ctx"), "tp"),
        P(("fsdp", "ctx"), "tp"),
        P(("fsdp", "ctx"), None),
        P(("fsdp", "ctx")),
        P(("fsdp", "ctx")),
        P(None, "tp"),
        P(("fsdp", "ctx"), None, "tp"),
        P(("fsdp", "ctx"), "tp", None),
    )
    return jax.shard_map(body, mesh=mesh, in_specs=in_specs, out_specs=out_specs, check_vma=False)
```

```python
import functools

import jax
import jax.numpy as jnp
import numpy as np
from jax import lax
from jax.experimental import pallas as pl
from jax.experimental.pallas import tpu as pltpu
from jax.sharding import PartitionSpec as P

epsilon = 1e-06
masked_value = -1e30
bucket_edges = (12, 16, 23, 32, 46, 64, 91)
highest = lax.Precision.HIGHEST
LANES = 128
STRIP = 128
HEAD_SIZE = 64
VMEM_BYTES = 60 * 1024 * 1024
f32 = jnp.float32
bf16 = jnp.bfloat16
vmem = pl.BlockSpec(memory_space=pltpu.VMEM)
smem = pl.BlockSpec(memory_space=pltpu.SMEM)


def mm(left, right):
    return jnp.dot(left, right, preferred_element_type=f32)


def mm_nt(left, right):
    return lax.dot_general(left, right, (((1,), (1,)), ((), ())), preferred_element_type=f32)


def mm_tn(left, right):
    return lax.dot_general(left, right, (((0,), (0,)), ((), ())), preferred_element_type=f32)


def rms_scale(values):
    return lax.rsqrt(jnp.mean(values * values, axis=-1, keepdims=True) + epsilon)


def iota(shape, dim):
    return lax.broadcasted_iota(jnp.int32, shape, dim)


def bucket_index(offset):
    side = jnp.where(offset > 0, 16, 0).astype(jnp.int32)
    distance = jnp.abs(offset)
    far_bucket = 8 + sum(((distance >= edge).astype(jnp.int32) for edge in bucket_edges))
    return side + jnp.where(distance < 8, distance, far_bucket)


def kernel_call(body, outs, in_specs, out_specs=None, scratch=(), grid=None, flops=0, moved=0):
    extra = {} if grid is None else {"grid": grid}
    return pl.pallas_call(
        body,
        out_shape=outs,
        in_specs=in_specs,
        out_specs=[vmem] * len(outs) if out_specs is None else out_specs,
        scratch_shapes=list(scratch),
        compiler_params=pltpu.CompilerParams(vmem_limit_bytes=VMEM_BYTES),
        cost_estimate=pl.CostEstimate(flops=flops, bytes_accessed=moved, transcendentals=0),
        **extra,
    )


def shape(dims, dtype):
    return jax.ShapeDtypeStruct(tuple(dims), dtype)


def segments(lengths_ref, rows, dim):
    dims = (rows, 1) if dim == 0 else (1, rows)
    places = iota(dims, dim)
    total = jnp.zeros(dims, jnp.int32)
    end = 0
    for entry in range(lengths_ref.shape[1]):
        end = end + lengths_ref[0, entry]
        total = total + (places >= end).astype(jnp.int32)
    return total


def skew(values, right):
    rows, lanes = values.shape
    row = lax.rem(iota((rows, 1), 0), STRIP)
    step = 1
    while step < STRIP:
        moved = pltpu.roll(values, step if right else lanes - step, 1)
        values = jnp.where((row & step) > 0, moved, values)
        step *= 2
    return values


def bias_strips(table_ref, first_head, heads, strip_ref):
    lanes = 4 * STRIP
    bucket = bucket_index(iota((1, lanes), 1) - 2 * STRIP)
    for head in range(heads):
        line = jnp.zeros((1, lanes), f32)
        for entry in range(table_ref.shape[1]):
            line = jnp.where(bucket == entry, table_ref[first_head + head, entry], line)
        strip = skew(jnp.broadcast_to(line, (STRIP, lanes)), True)
        strip_ref[head] = strip[:, STRIP:]


def bias_row(strip_ref, table_ref, head, first_head, block, blocks):
    buckets = table_ref.shape[1]
    parts = []
    for other in range(blocks):
        gap = other - block
        if abs(gap) <= 1:
            parts.append(strip_ref[head, :, (gap + 1) * STRIP : (gap + 2) * STRIP])
        else:
            entry = buckets - 1 if gap > 0 else buckets // 2 - 1
            parts.append(jnp.full((STRIP, STRIP), table_ref[first_head + head, entry], f32))
    return jnp.concatenate(parts, axis=1)


def head_mask(head, lanes):
    lane = iota((1, lanes), 1)
    return (lane >= head * HEAD_SIZE) & (lane < (head + 1) * HEAD_SIZE)


def pick_head(values, head, lanes):
    return jnp.where(head_mask(head, lanes), values, 0.0).astype(bf16)


def half_columns(weight, which):
    values = weight[...].astype(f32)
    width = values.shape[1] // 2
    lanes = width + HEAD_SIZE
    high = pltpu.roll(values[:, LANES : LANES + lanes], lanes - HEAD_SIZE, 1)
    picked = jnp.where(which == 0, values[:, :lanes], high)
    return jnp.where(iota((1, lanes), 1) < width, picked, 0.0)


def join(first, second):
    moved = pltpu.roll(second, HEAD_SIZE, 1)
    return first[:, :LANES], first[:, LANES:] + moved[:, :LANES], moved[:, LANES:]


def pack_rows(*refs):
    (meta, w_query, w_key, w_value, w_output, w_router, gain_one, gain_two, own, send, output) = refs
    rows = w_query.shape[0]
    experts = w_router.shape[0]
    width = w_query.shape[1] // 2
    lanes = width + HEAD_SIZE
    lane = iota((1, lanes), 1)
    diagonal = iota((rows, rows), 0) == iota((rows, rows), 1)
    placing = (iota((experts, lanes), 0) + width == iota((experts, lanes), 1)).astype(f32)
    extras = mm_tn(w_router[...], placing.astype(bf16))
    for index, gain in enumerate((gain_one, gain_two)):
        column = jnp.sum(
            jnp.where(diagonal, jnp.broadcast_to(gain[...].astype(f32), (rows, rows)), 0.0),
            axis=1,
            keepdims=True,
        )
        extras = extras + jnp.where(lane == width + experts + index, column, 0.0)
    for which, out in ((meta[0], own), (1 - meta[0], send)):
        at = 0
        for block in join(half_columns(w_query, which), half_columns(w_key, which)):
            out[:, at : at + LANES] = block.astype(bf16)
            at += LANES
        out[:, at:] = (half_columns(w_value, which) + extras).astype(bf16)
    output[:rows, :] = half_columns(w_output, 0).astype(bf16)
    output[rows:, :] = half_columns(w_output, 1).astype(bf16)


def put_in_rows(count, *refs):
    starts, meta = refs[:2]
    shards = refs[2 : 2 + count]
    wall, output = refs[2 + count :]
    wide = wall.shape[1]
    place = meta[0]
    for index, shard in enumerate(shards):
        rows = shard.shape[0] // 2
        first = starts[index]
        for half, core in ((0, place), (1, 1 - place)):
            at = pl.multiple_of((2 * first + core) * rows, 16)
            wall[pl.ds(at, rows), :] = shard[half * rows : (half + 1) * rows, :wide]
        blocks = join(shard[:rows, wide:].astype(f32), shard[rows:, wide:].astype(f32))
        at = pl.multiple_of(first * rows, 16)
        for block, values in enumerate(blocks):
            output[pl.ds(at, rows), block * LANES : (block + 1) * LANES] = values.astype(bf16)


def interleave(out, lanes, own, other, place, count):
    rows = own.shape[0] // count
    for index in range(count):
        here = slice(index * rows, (index + 1) * rows)
        first = pl.multiple_of((2 * index + place) * rows, 16)
        second = pl.multiple_of((2 * index + 1 - place) * rows, 16)
        out[pl.ds(first, rows), lanes] = own[here, :]
        out[pl.ds(second, rows), lanes] = other[here, :]


def attention_forward(heads, experts, *refs):
    (meta, lengths, table, x_own, x_other, wall) = refs[:6]
    (h1, q_out, k_out, v_out, o_own, o_other, o_all, lse, gains, strips) = refs[6:]
    place = meta[0]
    rows = x_own.shape[0]
    group = 2 * rows
    first_head = place * heads
    width = wall.shape[1]
    extras = wall[:, width - LANES :].astype(f32).T
    gain_at = HEAD_SIZE + experts
    gains[...] = extras[gain_at : gain_at + 8]
    gain_one = gains[0:1]
    for source, start in ((x_own, place * rows), (x_other, (1 - place) * rows)):
        values = source[...].astype(f32)
        h1[pl.ds(pl.multiple_of(start, 16), rows), :] = (
            values * rms_scale(values) * gain_one
        ).astype(bf16)
    qkv = mm(h1[...], wall[...])
    lanes = q_out.shape[1]
    q_out[...] = qkv[:, :lanes].astype(bf16)
    k_out[...] = pltpu.roll(qkv[:, LANES : LANES + lanes], lanes - HEAD_SIZE, 1).astype(bf16)
    v_out[...] = qkv[:, width - lanes :].astype(bf16)
    bias_strips(table, first_head, heads, strips)
    segment_row = segments(lengths, group, 1)
    segment_column = segments(lengths, group, 0)
    keys = k_out[...]
    lane = iota((1, LANES), 1)
    blocks = group // STRIP
    values_of = [pick_head(v_out[...], head, lanes) for head in range(heads)]
    for block in range(blocks):
        first = block * STRIP
        same = segment_column[first : first + STRIP] == segment_row
        total = jnp.zeros((STRIP, lanes), f32)
        totals = jnp.zeros((STRIP, LANES), f32)
        for head in range(heads):
            query = pick_head(q_out[first : first + STRIP, :], head, lanes)
            scores = mm_nt(query, keys) + bias_row(strips, table, head, first_head, block, blocks)
            scores = jnp.where(same, scores, masked_value)
            top = jnp.max(scores, axis=1, keepdims=True)
            raised = jnp.exp(scores - top)
            mass = jnp.sum(raised, axis=1, keepdims=True)
            chances = (raised * (1.0 / mass)).astype(bf16)
            total = total + mm(chances, values_of[head])
            totals = jnp.where(lane == head, top + jnp.log(mass), totals)
        o_all[first : first + STRIP, :] = total.astype(bf16)
        lse[first : first + STRIP, :] = totals
    o_own[...] = o_all[pl.ds(pl.multiple_of(place * rows, 16), rows), :]
    o_other[...] = o_all[pl.ds(pl.multiple_of((1 - place) * rows, 16), rows), :]


def column_of(line):
    return jnp.broadcast_to(line, (LANES, line.shape[1])).T[:, :1]


def columns_of(*lines):
    return [column_of(line[...].astype(f32)).astype(jnp.int32) for line in lines]


def routed(hidden, extras, routes_column, keep_column, experts):
    logits = mm(hidden, extras)
    lane = iota((1, LANES), 1) - HEAD_SIZE
    valid = (lane >= 0) & (lane < experts)
    logits = jnp.where(valid, logits, masked_value)
    raised = jnp.where(valid, jnp.exp(logits - jnp.max(logits, axis=1, keepdims=True)), 0.0)
    probs = raised / jnp.sum(raised, axis=1, keepdims=True)
    onehot = lane == routes_column
    kept = keep_column.astype(f32)
    gate = jnp.sum(jnp.where(onehot, probs, 0.0), axis=1, keepdims=True) * kept
    return probs, onehot, kept, gate


def slots_by_row(routes_row, keep_row, experts, capacity):
    count = routes_row.shape[1]
    chosen = ((iota((experts, count), 0) == routes_row) & (keep_row == 1)).astype(f32)
    before = (iota((count, count), 0) < iota((count, count), 1)).astype(bf16)
    earlier = mm(chosen.astype(bf16), before)
    rank = jnp.sum(earlier * chosen, axis=0, keepdims=True).astype(jnp.int32)
    return jnp.where(keep_row == 1, routes_row * capacity + rank, -2)


def heads_of(own, other, place):
    own = own[...].astype(f32)
    other = other[...].astype(f32)
    first = jnp.where(place == 0, own, other)
    second = jnp.where(place == 0, other, own)
    return jnp.concatenate(join(first, second), axis=1).astype(bf16)


def to_experts(experts, capacity, count, *refs):
    (meta, x_own, cotangent, o_own, o_tp, o_ctx, o_far, wo_own, wo_tp, wo_ctx, wo_far) = refs[:11]
    (extras, gains, routes_row, keep_row, slot_h, slot_d) = refs[11:17]
    middle_out, sends, wo_out, wo_other = refs[17:]
    routes_column, keep_column = columns_of(routes_row, keep_row)
    place, start = meta[0], meta[2]
    interleave(wo_out, slice(None), wo_own, wo_ctx, start, count)
    interleave(wo_other, slice(None), wo_tp, wo_far, start, count)
    branch = mm_nt(heads_of(o_own, o_ctx, place), wo_out[...])
    branch = branch + mm_nt(heads_of(o_tp, o_far, place), wo_other[...])
    middle = x_own[...].astype(f32) + branch
    middle_out[...] = middle
    hidden = (middle * rms_scale(middle) * gains[1:2]).astype(bf16)
    _, _, _, gate = routed(hidden, extras[...], routes_column, keep_column, experts)
    out_grad = (gate * cotangent[...].astype(f32)).astype(bf16)
    slot = slots_by_row(routes_row[...], keep_row[...], experts, capacity)
    pick_h = (slot_h[...] == slot).astype(f32).astype(bf16)
    pick_d = (slot_d[...] == slot).astype(f32).astype(bf16)
    sends[...] = (mm(pick_h, hidden) + mm(pick_d, out_grad)).astype(bf16)


def gelu_both(value):
    scale = 0.7978845608028654
    cubic = 0.044715
    square = value * value
    inner = jnp.tanh(scale * value * (1.0 + cubic * square))
    half = 0.5 * (1.0 + inner)
    slope = half + 0.5 * value * (1.0 - inner * inner) * scale * (1.0 + 3.0 * cubic * square)
    return value * half, slope


def expert_kernel(owners, kinds_rows, chunks, group_owners, *refs):
    (rows_in, base_column, base_row, w_in, w_out) = refs[:5]
    (out, x_out, dy_out, act_out, dpre_out, acc_y, acc_x, full) = refs[5:]
    piece = pl.program_id(0)
    chunk = pl.program_id(1)
    pieces = pl.num_programs(0)
    capacity = kinds_rows
    per_owner = rows_in.shape[0] // owners
    span = group_owners * per_owner
    half = group_owners * capacity
    groups = owners // group_owners

    @pl.when(chunk == 0)
    def _():
        pick = (base_column[...] + piece * capacity == iota((2 * half, span), 1)).astype(f32).astype(bf16)
        for group in range(groups):
            got = mm(pick, rows_in[group * span : (group + 1) * span, :]).astype(bf16)
            x_out[0, group * half : (group + 1) * half, :] = got[:half]
            dy_out[0, group * half : (group + 1) * half, :] = got[half:]
        acc_y[...] = jnp.zeros_like(acc_y)
        acc_x[...] = jnp.zeros_like(acc_x)

    pre = mm(x_out[0], w_in[0])
    act, slope = gelu_both(pre)
    act = act.astype(bf16)
    act_out[0] = act
    acc_y[...] += mm(act, w_out[0])
    dpre = (mm_nt(dy_out[0], w_out[0]) * slope).astype(bf16)
    dpre_out[0] = dpre
    acc_x[...] += mm_nt(dpre, w_in[0])

    @pl.when(chunk == chunks - 1)
    def _():
        pick = (base_row[...] + piece * capacity == iota((span, 2 * half), 0)).astype(f32).astype(bf16)
        for group in range(groups):
            here = slice(group * half, (group + 1) * half)
            both = jnp.concatenate([acc_y[here].astype(bf16), acc_x[here].astype(bf16)], axis=0)
            part = mm(pick, both)
            there = slice(group * span, (group + 1) * span)
            full[there] = jnp.where(piece == 0, part, full[there] + part)

    @pl.when((chunk == chunks - 1) & (piece == pieces - 1))
    def _():
        width = out.shape[2]
        shares = out.shape[0] // owners
        for owner in range(owners):
            for share in range(shares):
                out[owner * shares + share] = full[
                    owner * per_owner : (owner + 1) * per_owner, share * width : (share + 1) * width
                ].astype(bf16)


def weight_grads(x_rows, dpre, act, dy):
    w_in_grad = jnp.einsum("lrd,lrf->ldf", x_rows, dpre, preferred_element_type=f32)
    w_out_grad = jnp.einsum("lrf,lrd->lfd", act, dy, preferred_element_type=f32)
    return w_in_grad, w_out_grad


def from_experts(experts, capacity, *refs):
    rows_in, routes_row, keep_row, slot_y, slot_x, out = refs
    slot = column_of(slots_by_row(routes_row[...], keep_row[...], experts, capacity).astype(f32))
    slot = slot.astype(jnp.int32)
    width = rows_in.shape[1]
    pick_y = (slot == slot_y[...]).astype(f32).astype(bf16)
    pick_x = (slot == slot_x[...]).astype(f32).astype(bf16)
    out[:, :width] = mm(pick_y, rows_in[...]).astype(bf16)
    out[:, width:] = mm(pick_x, rows_in[...]).astype(bf16)


def middle_backward(experts, *refs):
    (meta, both_own, both_tp, middle_ref, cotangent, extras, gains, routes_row, keep_row) = refs[:9]
    routes_column, keep_column = columns_of(routes_row, keep_row)
    (result, dmiddle_out, branch_grad, router_grad) = refs[9:]
    share = meta[1]
    width = both_own.shape[1] // 2
    own = both_own[...].astype(f32)
    other = both_tp[...].astype(f32)
    first = jnp.where(share == 0, own, other)
    second = jnp.where(share == 0, other, own)
    picked = jnp.concatenate([first[:, :width], second[:, :width]], axis=1)
    slot_grad = jnp.concatenate([first[:, width:], second[:, width:]], axis=1)
    middle = middle_ref[...]
    scale = rms_scale(middle)
    normed = middle * scale
    gain = gains[1:2]
    hidden = (normed * gain).astype(bf16)
    probs, onehot, kept, gate = routed(hidden, extras[...], routes_column, keep_column, experts)
    result[...] = middle + gate * picked
    upstream = cotangent[...].astype(f32)
    gate_grad = jnp.sum(upstream * picked, axis=1, keepdims=True)
    prob_grad = jnp.where(onehot, gate_grad * kept, 0.0)
    logit_grad = (
        probs * (prob_grad - jnp.sum(probs * prob_grad, axis=1, keepdims=True))
    ).astype(bf16)
    hidden_grad = slot_grad + mm_nt(logit_grad, extras[...])
    gain_grad = column_of(jnp.sum(hidden_grad * normed, axis=0, keepdims=True))
    lane = iota((1, LANES), 1)
    router_grad[...] = jnp.where(
        lane == HEAD_SIZE + experts, gain_grad, mm_tn(hidden, logit_grad)
    ).astype(bf16)
    grad = hidden_grad * gain
    dmiddle = upstream + scale * (grad - normed * jnp.mean(grad * normed, axis=1, keepdims=True))
    dmiddle_out[...] = dmiddle
    branch_grad[...] = dmiddle.astype(bf16)


def attention_backward(heads, shard, *refs):
    (meta, lengths, table, x_own, x_other, h1, q_in, k_in, v_in, lse, db) = refs[:11]
    (o_all, wo_ref, wall, router_grad) = refs[11:15]
    (payload, top_out, bottom_out, dh1_own, dh1_other) = refs[15:20]
    (strips, sums, do_all, dq, dk, dv, dqkv, dh1) = refs[20:]
    place = meta[0]
    rows = x_own.shape[0]
    group = 2 * rows
    lanes = q_in.shape[1]
    first_head = place * heads
    own_at = pl.ds(pl.multiple_of(place * rows, 16), rows)
    other_at = pl.ds(pl.multiple_of((1 - place) * rows, 16), rows)
    both = mm(db[...], wo_ref[...])
    high = pltpu.roll(both[:, LANES : LANES + lanes], lanes - HEAD_SIZE, 1)
    do_all[...] = jnp.where(place == 0, both[:, :lanes], high).astype(bf16)
    bias_strips(table, first_head, heads, strips)
    segment_row = segments(lengths, group, 1)
    segment_column = segments(lengths, group, 0)
    blocks = group // STRIP
    sums[...] = jnp.zeros_like(sums)
    keys = k_in[...]
    values = v_in[...]
    ahead = [jnp.zeros((STRIP, STRIP), f32) for _ in range(heads)]
    behind = [jnp.zeros((STRIP, STRIP), f32) for _ in range(heads)]
    for block in range(blocks):
        at = slice(block * STRIP, (block + 1) * STRIP)
        same = segment_column[at] == segment_row
        dq_total = jnp.zeros((STRIP, lanes), f32)
        for head in range(heads):
            query = pick_head(q_in[at, :], head, lanes)
            scores = mm_nt(query, keys) + bias_row(strips, table, head, first_head, block, blocks)
            scores = jnp.where(same, scores, masked_value)
            chances = jnp.exp(scores - lse[at, head : head + 1])
            grad = pick_head(do_all[at, :], head, lanes)
            chance_grad = mm_nt(grad, values)
            mean = jnp.sum(chances * chance_grad, axis=1, keepdims=True)
            score_grad = (chances * (chance_grad - mean)).astype(bf16)
            dv_part = mm_tn(chances.astype(bf16), grad)
            dk_part = mm_tn(score_grad, query)
            if block == 0 and head == 0:
                dv[...] = dv_part
                dk[...] = dk_part
            else:
                dv[...] += dv_part
                dk[...] += dk_part
            dq_total = dq_total + mm(score_grad, pick_head(keys, head, lanes))
            rounded = score_grad.astype(f32)
            for other in range(blocks):
                gap = other - block
                part = rounded[:, other * STRIP : (other + 1) * STRIP]
                if abs(gap) <= 1:
                    sums[head, :, (gap + 2) * STRIP : (gap + 3) * STRIP] += part
                elif gap > 0:
                    ahead[head] = ahead[head] + part
                else:
                    behind[head] = behind[head] + part
        dq[at, :] = dq_total
    half = HEAD_SIZE
    dqkv[:, :LANES] = dq[:, :LANES].astype(bf16)
    shifted = pltpu.roll(dk[...], half, 1)
    dqkv[:, LANES : 2 * LANES] = (dq[:, LANES:] + shifted[:, :LANES]).astype(bf16)
    dqkv[:, 2 * LANES : 3 * LANES] = shifted[:, LANES:].astype(bf16)
    dqkv[:, 3 * LANES :] = dv[...].astype(bf16)
    dh1[...] = mm_nt(dqkv[...], wall[...])
    gain_part = None
    for source, at, target in ((x_own, own_at, dh1_own), (x_other, other_at, dh1_other)):
        values = source[...].astype(f32)
        grad = dh1[at, :]
        target[...] = grad.astype(bf16)
        part = jnp.sum(grad * (values * rms_scale(values)), axis=0, keepdims=True)
        gain_part = part if gain_part is None else gain_part + part
    buckets = table.shape[1]
    spread = skew(sums[...].reshape(heads * STRIP, 4 * STRIP), False)
    diagonals = jnp.sum(spread.reshape(heads, STRIP, 4 * STRIP), axis=1)
    picks = (bucket_index(iota((4 * STRIP, 1), 0) - 2 * STRIP) == iota((1, LANES), 1)).astype(f32)
    in_buckets = jnp.dot(diagonals, picks, precision=highest, preferred_element_type=f32)
    lane = iota((1, LANES), 1)
    row = lax.rem(iota((wall.shape[0], 1), 0), shard)
    riders = jnp.where(lane == HEAD_SIZE, column_of(gain_part), 0.0)
    for head in range(heads):
        line = in_buckets[head : head + 1]
        line = line + jnp.where(lane == buckets - 1, jnp.sum(ahead[head]), 0.0)
        line = line + jnp.where(lane == buckets // 2 - 1, jnp.sum(behind[head]), 0.0)
        riders = riders + jnp.where(row == head, pltpu.roll(line, HEAD_SIZE + 1, 1), 0.0)
    width = wall.shape[1]
    grads = mm_tn(h1[...], dqkv[...])
    payload[:, : width - LANES] = grads[:, : width - LANES].astype(bf16)
    payload[:, width - LANES : width] = (grads[:, width - LANES :] + riders).astype(bf16)
    grads = mm_tn(db[...], o_all[...])
    payload[:, width : width + lanes - LANES] = grads[:, : lanes - LANES].astype(bf16)
    payload[:, width + lanes - LANES :] = (
        grads[:, lanes - LANES :] + router_grad[...].astype(f32)
    ).astype(bf16)
    half = top_out.shape[0]
    across = pl.multiple_of(meta[3] * shard if 2 * half == shard else 0 * meta[3], 16)
    top_out[...] = payload[pl.ds(across, half), :]
    bottom_out[...] = payload[pl.ds(across + half, half), :]


def ring_add(places, right_mine, left_mine, from_left, from_right, right_out, left_out):
    rows = right_mine.shape[0]
    span = from_left.shape[0]
    right_out[...] = right_mine[...]
    left_out[...] = left_mine[...]
    top, bottom = slice(0, span), slice(rows - span, rows)
    right_out[top] = (right_mine[top].astype(f32) + from_left[...].astype(f32)).astype(bf16)
    left_out[bottom] = (left_mine[bottom].astype(f32) + from_right[...].astype(f32)).astype(bf16)


def ring_end(at, place, sums, own, send, table, riders_own, riders_other):
    rows = own.shape[0]
    first, second = sums[:rows, :], sums[rows : 2 * rows, :]
    mine = jnp.where(place == 0, first, second)
    other = jnp.where(place == 0, second, first)
    own[...] = mine
    send[:rows, :] = other
    send[rows:, :] = sums[:8, :]
    table[...] = sums[:8, at : at + LANES]
    riders_own[...] = mine[:, at : at + LANES]
    riders_other[...] = other[:, at : at + LANES]


def ring_last(at, places, mine, from_left, from_right, own, send, table, riders_own, riders_other):
    total = mine[...].astype(f32) + from_left[...].astype(f32) + from_right[...].astype(f32)
    ring_end(at, places[2], total, own, send, table, riders_own, riders_other)


def ring_whole(at, places, sums, own, send, table, riders_own, riders_other):
    ring_end(at, places[2], sums[...], own, send, table, riders_own, riders_other)


def shards_of_sums(experts, buckets, heads, *refs):
    (meta, own_ref, other, own_top, from_tp, from_far) = refs[:6]
    (query_out, key_out, value_out, output_out, router_out, gain_one, gain_two, table) = refs[6:]
    place = meta[0]
    rows, width = query_out.shape[0], query_out.shape[1] // 2
    lanes = width + HEAD_SIZE
    wide = 3 * width + HEAD_SIZE
    own = own_ref[...]
    more = other[:rows, :]
    lane = iota((1, lanes), 1)
    for at, moved, out in (
        (0, False, query_out),
        (LANES, True, key_out),
        (2 * width, False, value_out),
        (wide, False, output_out),
    ):
        parts = [values[:, at : at + lanes] for values in (own, more)]
        if moved:
            parts = [pltpu.roll(part, lanes - HEAD_SIZE, 1) for part in parts]
        parts = [jnp.where(lane < width, part, 0.0) for part in parts]
        first = jnp.where(place == 0, parts[0], parts[1])
        second = jnp.where(place == 0, parts[1], parts[0])
        for index, block in enumerate(join(first, second)):
            out[:, index * LANES : (index + 1) * LANES] = block
    total = (own + more)[:, wide + lanes - LANES :].T
    router_out[...] = total[HEAD_SIZE : HEAD_SIZE + experts, :]
    gain_two[...] = total[HEAD_SIZE + experts : HEAD_SIZE + experts + 1, :]
    line = (own + more)[:, wide - LANES : wide] + (from_tp[...] + from_far[...])
    gain_one[...] = line.T[HEAD_SIZE : HEAD_SIZE + 1, :]
    own_lines = own_top[...]
    other_lines = other[rows : rows + 8, wide - LANES : wide]
    own_lines = pltpu.roll(own_lines, LANES - HEAD_SIZE - 1, 1)
    other_lines = pltpu.roll(other_lines, LANES - HEAD_SIZE - 1, 1)
    table[:heads, :] = jnp.where(place == 0, own_lines, other_lines)[:heads, :buckets]
    table[heads : 2 * heads, :] = jnp.where(place == 0, other_lines, own_lines)[:heads, :buckets]


def input_backward(x_own, dmiddle, gains, near, far, out):
    values = x_own[...].astype(f32)
    scale = rms_scale(values)
    normed = values * scale
    grad = (near[...].astype(f32) + far[...].astype(f32)) * gains[0:1]
    out[...] = dmiddle[...] + scale * (
        grad - normed * jnp.mean(grad * normed, axis=1, keepdims=True)
    )


def swap(value, axis):
    return lax.ppermute(value, axis, [(0, 1), (1, 0)])


def ring_order(count):
    return list(range(0, count, 2)) + list(range(count - 1, 0, -2))


def ring_steps(count):
    order = ring_order(count)
    right = [(order[i], order[(i + 1) % count]) for i in range(count)]
    return order, right, [(b, a) for a, b in right]


def ring_place(count):
    order = ring_order(count)
    inverse = np.zeros(count, np.int32)
    inverse[order] = np.arange(count)
    return jnp.asarray(np.array(order, np.int32)), jnp.asarray(inverse)[lax.axis_index("fsdp")]


def ring_gather(shard, count):
    order, right, left = ring_steps(count)
    table, place = ring_place(count)
    shards = [shard]
    places = [table[place]]
    going_right, going_left = shard, shard
    for step in range(1, count // 2):
        going_right = lax.ppermute(going_right, "fsdp", right)
        going_left = lax.ppermute(going_left, "fsdp", left)
        shards += [going_right, going_left]
        places += [table[(place - step) % count], table[(place + step) % count]]
    shards.append(lax.ppermute(going_right, "fsdp", right))
    places.append(table[(place + count // 2) % count])
    return shards, jnp.stack(places).astype(jnp.int32)


def ring_sums(payload, top, bottom, count, at, place, side):
    rows = payload.shape[0] // count
    lanes = payload.shape[1]
    half = rows // 2
    outs = [
        shape((half, lanes), f32),
        shape((half + 8, lanes), f32),
        shape((8, LANES), f32),
        shape((half, LANES), f32),
        shape((half, LANES), f32),
    ]
    zero = jnp.zeros((), jnp.int32)
    if rows % 32 or count % 2:
        sums = lax.psum_scatter(payload.astype(f32), "fsdp", scatter_dimension=0, tiled=True)
        places = jnp.stack([zero, zero, place]).astype(jnp.int32)
        return kernel_call(functools.partial(ring_whole, at), outs, [smem, vmem])(places, sums)
    order, right, left = ring_steps(count)
    table, spot = ring_place(count)
    going_right, going_left = top, bottom
    spec = lambda which: pl.BlockSpec((rows, lanes), lambda i, places: (places[which], 0))
    params = pltpu.CompilerParams(vmem_limit_bytes=VMEM_BYTES)
    for step in range(count // 2, 0, -1):
        from_left = lax.ppermute(going_right, "fsdp", right)
        from_right = lax.ppermute(going_left, "fsdp", left)
        places = [table[(spot + step - 1) % count], table[(spot + 1 - step) % count], place]
        places = jnp.stack(places).astype(jnp.int32)
        whole = lambda dims: pl.BlockSpec(dims, lambda i, places: (0, 0))
        last = step == 1
        if last:
            side, from_left, from_right = lax.optimization_barrier((side, from_left, from_right))
        step_outs = outs if last else [shape((rows, lanes), bf16)] * 2
        out = pl.pallas_call(
            functools.partial(ring_last, at) if last else ring_add,
            grid_spec=pltpu.PrefetchScalarGridSpec(
                num_scalar_prefetch=1,
                grid=(1,),
                in_specs=([spec(0)] if last else [spec(0), spec(1)])
                + [whole(from_left.shape), whole(from_right.shape)],
                out_specs=[whole(o.shape) for o in step_outs],
            ),
            out_shape=step_outs,
            compiler_params=params,
            cost_estimate=pl.CostEstimate(flops=0, bytes_accessed=1024 * 1024, transcendentals=0),
        )(places, *([payload] if last else [payload, payload]), from_left, from_right)
        if last:
            return out
        going_right, going_left = out


def body(
    tokens,
    cotangent,
    w_query,
    w_key,
    w_value,
    w_output,
    w_router,
    gain_attn,
    gain_moe,
    rel_table,
    w_in,
    w_out,
    lengths,
    routes,
    keep_mask,
):
    rows, model_width = tokens.shape
    fsdp_count = lax.axis_size("fsdp")
    owners = lax.axis_size(("fsdp", "ctx"))
    tp_count = lax.axis_size("tp")
    place = lax.axis_index("ctx")
    share = lax.axis_index("tp")
    fsdp_place = lax.axis_index("fsdp")
    group = 2 * rows
    experts = w_router.shape[1]
    capacity = max(2, (5 * rows + 4 * experts - 1) // (4 * experts))
    pieces = w_in.shape[0]
    split_count = owners * pieces // experts
    hidden_width = w_in.shape[2]
    heads = rel_table.shape[1] // 2
    heads_all = heads * 2 * tp_count
    width = heads * HEAD_SIZE
    lanes = width + HEAD_SIZE
    shard_rows = w_query.shape[0]
    buckets = rel_table.shape[0]

    def full(dims, dtype):
        return shape(dims, dtype)

    wide = 3 * width + HEAD_SIZE
    aligned = shard_rows % 16 == 0 and fsdp_count % 2 == 0
    count = fsdp_count if aligned else 1
    start = place if aligned else 0 * place
    across = ring_place(fsdp_count)[1] + fsdp_count // 2
    across = ring_place(fsdp_count)[0][across % fsdp_count]
    meta = jnp.stack([place, share, start, across]).astype(jnp.int32)
    table_rows = rel_table.T
    shard_own, shard_send, wo_shard = kernel_call(
        pack_rows,
        [full((shard_rows, wide), bf16), full((shard_rows, wide), bf16), full((2 * shard_rows, lanes), bf16)],
        [smem] + [vmem] * 7,
        moved=512 * 1024,
    )(meta, w_query, w_key, w_value, w_output, w_router.T, gain_attn[None, :], gain_moe[None, :])
    shard_other = swap(shard_send, "ctx")
    shard = jnp.concatenate(
        [jnp.concatenate([shard_own, shard_other], axis=0), wo_shard], axis=1
    )
    x_other = swap(tokens, "ctx")

    def ordered(own, other):
        if aligned:
            return own, other
        dims = (fsdp_count, 1, shard_rows, own.shape[1])
        pair = in_order(own.reshape(dims), other.reshape(dims), 1).reshape(2 * own.shape[0], -1)
        return pair[: own.shape[0]], pair[own.shape[0] :]

    def in_order(own, other, axis):
        return jnp.where(
            place == 0,
            jnp.concatenate([own, other], axis=axis),
            jnp.concatenate([other, own], axis=axis),
        )

    if aligned:
        shards, places = ring_gather(shard, fsdp_count)
        wall, wo_own = kernel_call(
            functools.partial(put_in_rows, len(shards)),
            [full((model_width, wide), bf16), full((model_width // 2, 2 * width), bf16)],
            [smem, smem] + [vmem] * len(shards),
            moved=4 * 1024 * 1024,
        )(places, meta, *shards)
    else:
        both = lax.all_gather(shard, "fsdp", axis=0, tiled=False)
        near, far = both[:, :shard_rows], both[:, shard_rows:]
        wall = jnp.concatenate(
            ordered(near[:, :, :wide].reshape(-1, wide), far[:, :, :wide].reshape(-1, wide)), axis=0
        )
        wo_own = jnp.concatenate([near[:, :, wide : wide + width], far[:, :, wide : wide + width]], axis=2)
        wo_own = wo_own.reshape(-1, 2 * width)

    h1, q, k, v, o_own, o_other, o_all, lse, gains = kernel_call(
        functools.partial(attention_forward, heads, experts),
        [
            full((group, model_width), bf16),
            full((group, lanes), bf16),
            full((group, lanes), bf16),
            full((group, lanes), bf16),
            full((rows, lanes), bf16),
            full((rows, lanes), bf16),
            full((group, lanes), bf16),
            full((group, LANES), f32),
            full((8, model_width), f32),
        ],
        [smem] * 3 + [vmem] * 3,
        scratch=[pltpu.VMEM((heads, STRIP, 3 * STRIP), f32)],
        flops=2 * group * model_width * wide * 8,
        moved=8 * 1024 * 1024,
    )(meta, lengths, table_rows, tokens, x_other, wall)
    wo_tp = swap(wo_own, "tp")
    wo_ctx = swap(wo_own, "ctx")
    wo_far = swap(wo_tp, "ctx")
    wo_own, wo_ctx = ordered(wo_own, wo_ctx)
    wo_tp, wo_far = ordered(wo_tp, wo_far)

    o_tp = swap(o_own, "tp")
    o_ctx = swap(o_other, "ctx")
    o_far = lax.ppermute(o_other, ("ctx", "tp"), [(i, 3 - i) for i in range(4)])

    per_owner = 2 * pieces * capacity
    owner_of = np.repeat(np.arange(owners), per_owner)
    inside = np.tile(np.arange(per_owner), owners)
    kind = inside // (pieces * capacity)
    piece_of = owner_of * pieces + (inside // capacity) % pieces
    slot_of = (piece_of // split_count) * capacity + inside % capacity
    slot_first = np.where(kind == 0, slot_of, -1).astype(np.int32)
    slot_second = np.where(kind == 1, slot_of, -1).astype(np.int32)
    routes_row = routes.reshape(1, rows)
    keep_row = keep_mask.reshape(1, rows)
    extras = wall[:, wide - LANES :]

    middle, sends, wo_full = kernel_call(
        functools.partial(to_experts, experts, capacity, count),
        [
            full((rows, model_width), f32),
            full((owners * per_owner, model_width), bf16),
            full((model_width, 2 * width), bf16),
        ],
        [smem] + [vmem] * 16,
        scratch=[pltpu.VMEM((model_width, 2 * width), bf16)],
        flops=2 * rows * model_width * (model_width + 2 * owners * per_owner),
        moved=6 * 1024 * 1024,
    )(
        meta, tokens, cotangent, o_own, o_tp, o_ctx, o_far, wo_own, wo_tp, wo_ctx, wo_far, extras,
        gains, routes_row, keep_row, slot_first[:, None], slot_second[:, None],
    )

    arrived = lax.all_to_all(
        sends.reshape(owners, per_owner, model_width),
        ("fsdp", "ctx"),
        split_axis=0,
        concat_axis=0,
        tiled=True,
    ).reshape(owners * per_owner, model_width)

    group_owners = min(16, owners)
    half = group_owners * capacity
    spot = np.arange(2 * half) % half
    base = (
        (spot // capacity) * per_owner
        + (np.arange(2 * half) // half) * pieces * capacity
        + spot % capacity
    ).astype(np.int32)
    chunk_width = 512 if hidden_width % 512 == 0 else hidden_width
    chunks = hidden_width // chunk_width
    slot_rows = owners * capacity
    part_width = model_width // tp_count
    whole = lambda *dims: pl.BlockSpec(dims, lambda i, j: (0,) * len(dims))
    outgoing, x_rows, dy_rows, act, dpre = kernel_call(
        functools.partial(expert_kernel, owners, capacity, chunks, group_owners),
        [
            full((owners * tp_count, per_owner, part_width), bf16),
            full((pieces, slot_rows, model_width), bf16),
            full((pieces, slot_rows, model_width), bf16),
            full((pieces, slot_rows, hidden_width), bf16),
            full((pieces, slot_rows, hidden_width), bf16),
        ],
        [
            whole(owners * per_owner, model_width),
            whole(2 * half, 1),
            whole(1, 2 * half),
            pl.BlockSpec((1, model_width, chunk_width), lambda i, j: (i, 0, j)),
            pl.BlockSpec((1, chunk_width, model_width), lambda i, j: (i, j, 0)),
        ],
        out_specs=[
            whole(owners * tp_count, per_owner, part_width),
            pl.BlockSpec((1, slot_rows, model_width), lambda i, j: (i, 0, 0)),
            pl.BlockSpec((1, slot_rows, model_width), lambda i, j: (i, 0, 0)),
            pl.BlockSpec((1, slot_rows, chunk_width), lambda i, j: (i, 0, j)),
            pl.BlockSpec((1, slot_rows, chunk_width), lambda i, j: (i, 0, j)),
        ],
        scratch=[
            pltpu.VMEM((slot_rows, model_width), f32),
            pltpu.VMEM((slot_rows, model_width), f32),
            pltpu.VMEM((owners * per_owner, model_width), f32),
        ],
        grid=(pieces, chunks),
        flops=8 * pieces * slot_rows * model_width * hidden_width,
        moved=12 * 1024 * 1024,
    )(arrived, base[:, None], base[None, :], w_in, w_out)

    returned = lax.all_to_all(
        outgoing, ("fsdp", "ctx", "tp"), split_axis=0, concat_axis=0, tiled=True
    ).reshape(owners * tp_count * per_owner, part_width)
    w_in_grad, w_out_grad = weight_grads(x_rows, dpre, act, dy_rows)
    returned, w_in_grad, w_out_grad = lax.optimization_barrier((returned, w_in_grad, w_out_grad))

    back_first = np.repeat(slot_first.reshape(owners, 1, per_owner), tp_count, axis=1).reshape(1, -1)
    back_second = np.repeat(slot_second.reshape(owners, 1, per_owner), tp_count, axis=1).reshape(1, -1)
    both_own = kernel_call(
        functools.partial(from_experts, experts, capacity),
        [full((rows, 2 * part_width), bf16)],
        [vmem] * 5,
        flops=4 * rows * returned.shape[0] * part_width,
        moved=2 * 1024 * 1024,
    )(returned, routes_row, keep_row, back_first, back_second)[0]
    both_tp = swap(both_own, "tp")

    result, middle_grad, db_own, router_grad = kernel_call(
        functools.partial(middle_backward, experts),
        [
            full((rows, model_width), f32),
            full((rows, model_width), f32),
            full((rows, model_width), bf16),
            full((model_width, LANES), bf16),
        ],
        [smem] + [vmem] * 8,
        flops=6 * rows * LANES * model_width,
        moved=6 * 1024 * 1024,
    )(meta, both_own, both_tp, middle, cotangent, extras, gains, routes_row, keep_row)
    db = lax.all_gather(db_own, "ctx", axis=0, tiled=True)

    half = model_width // fsdp_count // 2
    payload, top, bottom, dh1_own, dh1_other = kernel_call(
        functools.partial(attention_backward, heads, model_width // fsdp_count),
        [
            full((model_width, wide + lanes), bf16),
            full((half if aligned else 16, wide + lanes), bf16),
            full((half if aligned else 16, wide + lanes), bf16),
            full((rows, model_width), bf16),
            full((rows, model_width), bf16),
        ],
        [smem] * 3 + [vmem] * 12,
        scratch=[
            pltpu.VMEM((heads, STRIP, 3 * STRIP), f32),
            pltpu.VMEM((heads, STRIP, 4 * STRIP), f32),
            pltpu.VMEM((group, lanes), bf16),
            pltpu.VMEM((group, lanes), f32),
            pltpu.VMEM((group, lanes), f32),
            pltpu.VMEM((group, lanes), f32),
            pltpu.VMEM((group, wide), bf16),
            pltpu.VMEM((group, model_width), f32),
        ],
        flops=2 * group * model_width * wide * 12,
        moved=8 * 1024 * 1024,
    )(
        meta, lengths, table_rows, tokens, x_other, h1, q, k, v, lse, db,
        o_all, wo_full, wall, router_grad,
    )

    dh1_sum = (dh1_own.astype(f32) + swap(dh1_other, "ctx").astype(f32)).astype(bf16)
    dh1_far = swap(dh1_sum, "tp")
    own, send, own_lines, riders_own, riders_other = ring_sums(
        payload, top, bottom, fsdp_count, wide - LANES, place, dh1_far
    )
    other = swap(send, "ctx")
    from_tp = swap(riders_own, "tp")
    from_far = lax.ppermute(riders_other, ("ctx", "tp"), [(i, 3 - i) for i in range(4)])
    input_grad = kernel_call(
        input_backward,
        [full((rows, model_width), f32)],
        [vmem] * 5,
        moved=4 * 1024 * 1024,
    )(tokens, middle_grad, gains, dh1_sum, dh1_far)[0]
    other, input_grad = lax.optimization_barrier((other, input_grad))

    shard = full((shard_rows, 2 * width), f32)
    query_grad, key_grad, value_grad, output_grad, router_sum, gain_one, gain_two, table_grad = kernel_call(
        functools.partial(shards_of_sums, experts, buckets, heads),
        [shard] * 4
        + [
            full((experts, shard_rows), f32),
            full((1, shard_rows), f32),
            full((1, shard_rows), f32),
            full((2 * heads, buckets), f32),
        ],
        [smem] + [vmem] * 5,
        moved=1024 * 1024,
    )(meta, own, other, own_lines, from_tp, from_far)
    return (
        result,
        input_grad,
        query_grad,
        key_grad,
        value_grad,
        output_grad,
        router_sum.T,
        gain_one.reshape(shard_rows),
        gain_two.reshape(shard_rows),
        table_grad.T,
        w_in_grad,
        w_out_grad,
    )


def solution(mesh):
    in_specs = (
        P(("fsdp", "ctx"), None),
        P(("fsdp", "ctx"), None),
        P(("fsdp", "ctx"), "tp"),
        P(("fsdp", "ctx"), "tp"),
        P(("fsdp", "ctx"), "tp"),
        P(("fsdp", "ctx"), "tp"),
        P(("fsdp", "ctx"), None),
        P(("fsdp", "ctx")),
        P(("fsdp", "ctx")),
        P(None, "tp"),
        P(("fsdp", "ctx"), None, "tp"),
        P(("fsdp", "ctx"), "tp", None),
        P("fsdp", None),
        P(("fsdp", "ctx"), None),
        P(("fsdp", "ctx")),
    )
    out_specs = (
        P(("fsdp", "ctx"), None),
        P(("fsdp", "ctx"), None),
        P(("fsdp", "ctx"), "tp"),
        P(("fsdp", "ctx"), "tp"),
        P(("fsdp", "ctx"), "tp"),
        P(("fsdp", "ctx"), "tp"),
        P(("fsdp", "ctx"), None),
        P(("fsdp", "ctx")),
        P(("fsdp", "ctx")),
        P(None, "tp"),
        P(("fsdp", "ctx"), None, "tp"),
        P(("fsdp", "ctx"), "tp", None),
    )
    return jax.shard_map(body, mesh=mesh, in_specs=in_specs, out_specs=out_specs, check_vma=False)
```

```python
import functools

import jax
import jax.numpy as jnp
import numpy as np
from jax import lax
from jax.experimental import pallas as pl
from jax.experimental.pallas import tpu as pltpu
from jax.sharding import PartitionSpec as P

epsilon = 1e-06
masked_value = -1e30
bucket_edges = (12, 16, 23, 32, 46, 64, 91)
highest = lax.Precision.HIGHEST
LANES = 128
STRIP = 128
HEAD_SIZE = 64
VMEM_BYTES = 40 * 1024 * 1024
SMALL_VMEM_BYTES = 16 * 1024 * 1024
f32 = jnp.float32
bf16 = jnp.bfloat16
vmem = pl.BlockSpec(memory_space=pltpu.VMEM)
smem = pl.BlockSpec(memory_space=pltpu.SMEM)


def mm(left, right):
    return jnp.dot(left, right, preferred_element_type=f32)


def mm_nt(left, right):
    return lax.dot_general(left, right, (((1,), (1,)), ((), ())), preferred_element_type=f32)


def mm_tn(left, right):
    return lax.dot_general(left, right, (((0,), (0,)), ((), ())), preferred_element_type=f32)


def rms_scale(values):
    return lax.rsqrt(jnp.mean(values * values, axis=-1, keepdims=True) + epsilon)


def iota(shape, dim):
    return lax.broadcasted_iota(jnp.int32, shape, dim)


def bucket_index(offset):
    side = jnp.where(offset > 0, 16, 0).astype(jnp.int32)
    distance = jnp.abs(offset)
    far_bucket = 8 + sum(((distance >= edge).astype(jnp.int32) for edge in bucket_edges))
    return side + jnp.where(distance < 8, distance, far_bucket)


def kernel_call(body, outs, in_specs, out_specs=None, scratch=(), grid=None, flops=0, moved=0, small=False):
    extra = {} if grid is None else {"grid": grid}
    return pl.pallas_call(
        body,
        out_shape=outs,
        in_specs=in_specs,
        out_specs=[vmem] * len(outs) if out_specs is None else out_specs,
        scratch_shapes=list(scratch),
        compiler_params=pltpu.CompilerParams(vmem_limit_bytes=SMALL_VMEM_BYTES if small else VMEM_BYTES),
        cost_estimate=pl.CostEstimate(flops=flops, bytes_accessed=moved, transcendentals=0),
        **extra,
    )


def shape(dims, dtype):
    return jax.ShapeDtypeStruct(tuple(dims), dtype)


def segments(lengths_ref, rows, dim):
    dims = (rows, 1) if dim == 0 else (1, rows)
    places = iota(dims, dim)
    total = jnp.zeros(dims, jnp.int32)
    end = 0
    for entry in range(lengths_ref.shape[1]):
        end = end + lengths_ref[0, entry]
        total = total + (places >= end).astype(jnp.int32)
    return total


def skew(values, right):
    rows, lanes = values.shape
    row = lax.rem(iota((rows, 1), 0), STRIP)
    step = 1
    while step < STRIP:
        moved = pltpu.roll(values, step if right else lanes - step, 1)
        values = jnp.where((row & step) > 0, moved, values)
        step *= 2
    return values


def bias_strips(table_ref, first_head, heads, strip_ref):
    lanes = 4 * STRIP
    bucket = bucket_index(iota((1, lanes), 1) - 2 * STRIP)
    for head in range(heads):
        line = jnp.zeros((1, lanes), f32)
        for entry in range(table_ref.shape[1]):
            line = jnp.where(bucket == entry, table_ref[first_head + head, entry], line)
        strip = skew(jnp.broadcast_to(line, (STRIP, lanes)), True)
        strip_ref[head] = strip[:, STRIP:]


def bias_row(strip_ref, table_ref, head, first_head, block, blocks):
    buckets = table_ref.shape[1]
    parts = []
    for other in range(blocks):
        gap = other - block
        if abs(gap) <= 1:
            parts.append(strip_ref[head, :, (gap + 1) * STRIP : (gap + 2) * STRIP])
        else:
            entry = buckets - 1 if gap > 0 else buckets // 2 - 1
            parts.append(jnp.full((STRIP, STRIP), table_ref[first_head + head, entry], f32))
    return jnp.concatenate(parts, axis=1)


def head_mask(head, lanes):
    lane = iota((1, lanes), 1)
    return (lane >= head * HEAD_SIZE) & (lane < (head + 1) * HEAD_SIZE)


def pick_head(values, head, lanes):
    return jnp.where(head_mask(head, lanes), values, 0.0).astype(bf16)


def half_columns(weight, which):
    values = weight[...].astype(f32)
    width = values.shape[1] // 2
    lanes = width + HEAD_SIZE
    high = pltpu.roll(values[:, LANES : LANES + lanes], lanes - HEAD_SIZE, 1)
    picked = jnp.where(which == 0, values[:, :lanes], high)
    return jnp.where(iota((1, lanes), 1) < width, picked, 0.0)


def join(first, second):
    moved = pltpu.roll(second, HEAD_SIZE, 1)
    return first[:, :LANES], first[:, LANES:] + moved[:, :LANES], moved[:, LANES:]


def pack_rows(*refs):
    (meta, w_query, w_key, w_value, w_output, w_router, gain_one, gain_two, own, send, output) = refs
    rows = w_query.shape[0]
    experts = w_router.shape[0]
    width = w_query.shape[1] // 2
    lanes = width + HEAD_SIZE
    lane = iota((1, lanes), 1)
    diagonal = iota((rows, rows), 0) == iota((rows, rows), 1)
    placing = (iota((experts, lanes), 0) + width == iota((experts, lanes), 1)).astype(f32)
    extras = mm_tn(w_router[...], placing.astype(bf16))
    for index, gain in enumerate((gain_one, gain_two)):
        column = jnp.sum(
            jnp.where(diagonal, jnp.broadcast_to(gain[...].astype(f32), (rows, rows)), 0.0),
            axis=1,
            keepdims=True,
        )
        extras = extras + jnp.where(lane == width + experts + index, column, 0.0)
    for which, out in ((meta[0], own), (1 - meta[0], send)):
        at = 0
        for block in join(half_columns(w_query, which), half_columns(w_key, which)):
            out[:, at : at + LANES] = block.astype(bf16)
            at += LANES
        out[:, at:] = (half_columns(w_value, which) + extras).astype(bf16)
    output[:rows, :] = half_columns(w_output, 0).astype(bf16)
    output[rows:, :] = half_columns(w_output, 1).astype(bf16)


def put_in_rows(count, *refs):
    meta = refs[0]
    shards = refs[1 : 1 + count]
    wall, output = refs[1 + count :]
    wide = wall.shape[1]
    place = meta[0]
    for index, shard in enumerate(shards):
        rows = shard.shape[0] // 2
        first = meta[4 + index]
        for half, core in ((0, place), (1, 1 - place)):
            at = pl.multiple_of((2 * first + core) * rows, 16)
            wall[pl.ds(at, rows), :] = shard[half * rows : (half + 1) * rows, :wide]
        blocks = join(shard[:rows, wide:].astype(f32), shard[rows:, wide:].astype(f32))
        at = pl.multiple_of(first * rows, 16)
        for block, values in enumerate(blocks):
            output[pl.ds(at, rows), block * LANES : (block + 1) * LANES] = values.astype(bf16)


def interleave(out, lanes, own, other, place, count):
    rows = own.shape[0] // count
    for index in range(count):
        here = slice(index * rows, (index + 1) * rows)
        first = pl.multiple_of((2 * index + place) * rows, 16)
        second = pl.multiple_of((2 * index + 1 - place) * rows, 16)
        out[pl.ds(first, rows), lanes] = own[here, :]
        out[pl.ds(second, rows), lanes] = other[here, :]


def attention_forward(heads, experts, *refs):
    (meta, lengths, table, x_own, x_other, wall) = refs[:6]
    (h1, q_out, k_out, v_out, o_own, o_other, o_all, lse, gains, strips) = refs[6:]
    place = meta[0]
    rows = x_own.shape[0]
    group = 2 * rows
    first_head = place * heads
    width = wall.shape[1]
    extras = wall[:, width - LANES :].astype(f32).T
    gain_at = HEAD_SIZE + experts
    gains[...] = extras[gain_at : gain_at + 8]
    gain_one = gains[0:1]
    for source, start in ((x_own, place * rows), (x_other, (1 - place) * rows)):
        values = source[...].astype(f32)
        h1[pl.ds(pl.multiple_of(start, 16), rows), :] = (
            values * rms_scale(values) * gain_one
        ).astype(bf16)
    qkv = mm(h1[...], wall[...])
    lanes = q_out.shape[1]
    q_out[...] = qkv[:, :lanes].astype(bf16)
    k_out[...] = pltpu.roll(qkv[:, LANES : LANES + lanes], lanes - HEAD_SIZE, 1).astype(bf16)
    v_out[...] = qkv[:, width - lanes :].astype(bf16)
    bias_strips(table, first_head, heads, strips)
    segment_row = segments(lengths, group, 1)
    segment_column = segments(lengths, group, 0)
    keys = k_out[...]
    lane = iota((1, LANES), 1)
    blocks = group // STRIP
    values_of = [pick_head(v_out[...], head, lanes) for head in range(heads)]
    for block in range(blocks):
        first = block * STRIP
        same = segment_column[first : first + STRIP] == segment_row
        total = jnp.zeros((STRIP, lanes), f32)
        totals = jnp.zeros((STRIP, LANES), f32)
        for head in range(heads):
            query = pick_head(q_out[first : first + STRIP, :], head, lanes)
            scores = mm_nt(query, keys) + bias_row(strips, table, head, first_head, block, blocks)
            scores = jnp.where(same, scores, masked_value)
            top = jnp.max(scores, axis=1, keepdims=True)
            raised = jnp.exp(scores - top)
            mass = jnp.sum(raised, axis=1, keepdims=True)
            chances = (raised * (1.0 / mass)).astype(bf16)
            total = total + mm(chances, values_of[head])
            totals = jnp.where(lane == head, top + jnp.log(mass), totals)
        o_all[first : first + STRIP, :] = total.astype(bf16)
        lse[first : first + STRIP, :] = totals
    for out, start in ((o_own, place * rows), (o_other, (1 - place) * rows)):
        values = o_all[pl.ds(pl.multiple_of(start, 16), rows), :].astype(f32)
        for index, part in enumerate(join(values[: rows // 2], values[rows // 2 :])):
            out[:, index * LANES : (index + 1) * LANES] = part.astype(bf16)


def column_of(line):
    return jnp.broadcast_to(line, (LANES, line.shape[1])).T[:, :1]


def columns_of(*lines):
    return [column_of(line[...].astype(f32)).astype(jnp.int32) for line in lines]


def routed(hidden, extras, routes_column, keep_column, experts):
    logits = mm(hidden, extras)
    lane = iota((1, LANES), 1) - HEAD_SIZE
    valid = (lane >= 0) & (lane < experts)
    logits = jnp.where(valid, logits, masked_value)
    raised = jnp.where(valid, jnp.exp(logits - jnp.max(logits, axis=1, keepdims=True)), 0.0)
    probs = raised / jnp.sum(raised, axis=1, keepdims=True)
    onehot = lane == routes_column
    kept = keep_column.astype(f32)
    gate = jnp.sum(jnp.where(onehot, probs, 0.0), axis=1, keepdims=True) * kept
    return probs, onehot, kept, gate


def slots_by_row(routes_row, keep_row, experts, capacity):
    count = routes_row.shape[1]
    chosen = ((iota((experts, count), 0) == routes_row) & (keep_row == 1)).astype(f32)
    before = (iota((count, count), 0) < iota((count, count), 1)).astype(bf16)
    earlier = mm(chosen.astype(bf16), before)
    rank = jnp.sum(earlier * chosen, axis=0, keepdims=True).astype(jnp.int32)
    return jnp.where(keep_row == 1, routes_row * capacity + rank, -2)


def unpacked(pair):
    values = pair[...].astype(f32)
    lanes = values.shape[1] - LANES
    upper = jnp.where(iota((1, lanes), 1) < lanes - HEAD_SIZE, values[:, :lanes], 0.0)
    lower = pltpu.roll(values[:, LANES:], lanes - HEAD_SIZE, 1)
    lower = jnp.where(iota((1, lanes), 1) < lanes - HEAD_SIZE, lower, 0.0)
    return jnp.concatenate([upper, lower], axis=0)


def heads_of(own, other, place):
    own = unpacked(own)
    other = unpacked(other)
    first = jnp.where(place == 0, own, other)
    second = jnp.where(place == 0, other, own)
    return jnp.concatenate(join(first, second), axis=1).astype(bf16)


def to_experts(experts, capacity, count, *refs):
    (meta, x_own, cotangent, o_own, o_tp, o_ctx, o_far, wo_own, wo_tp, wo_ctx, wo_far) = refs[:11]
    (extras, gains, routes_row, keep_row, slot_h, slot_d) = refs[11:17]
    middle_out, sends, wo_out, wo_other = refs[17:]
    routes_column, keep_column = columns_of(routes_row, keep_row)
    extras = extras[:, extras.shape[1] - LANES :]
    place, start = meta[0], meta[2]
    interleave(wo_out, slice(None), wo_own, wo_ctx, start, count)
    interleave(wo_other, slice(None), wo_tp, wo_far, start, count)
    branch = mm_nt(heads_of(o_own, o_ctx, place), wo_out[...])
    branch = branch + mm_nt(heads_of(o_tp, o_far, place), wo_other[...])
    middle = x_own[...].astype(f32) + branch
    middle_out[...] = middle
    hidden = (middle * rms_scale(middle) * gains[1:2]).astype(bf16)
    _, _, _, gate = routed(hidden, extras, routes_column, keep_column, experts)
    out_grad = (gate * cotangent[...].astype(f32)).astype(bf16)
    slot = slots_by_row(routes_row[...], keep_row[...], experts, capacity)
    pick_h = (slot_h[...] == slot).astype(f32).astype(bf16)
    pick_d = (slot_d[...] == slot).astype(f32).astype(bf16)
    sends[...] = (mm(pick_h, hidden) + mm(pick_d, out_grad)).astype(bf16)


def gelu_both(value):
    scale = 0.7978845608028654
    cubic = 0.044715
    square = value * value
    inner = jnp.tanh(scale * value * (1.0 + cubic * square))
    half = 0.5 * (1.0 + inner)
    slope = half + 0.5 * value * (1.0 - inner * inner) * scale * (1.0 + 3.0 * cubic * square)
    return value * half, slope


def expert_kernel(owners, kinds_rows, chunks, group_owners, *refs):
    (rows_in, base_column, base_row, w_in, w_out) = refs[:5]
    (out, x_out, dy_out, act_out, dpre_out, acc_y, acc_x, full) = refs[5:]
    piece = pl.program_id(0)
    chunk = pl.program_id(1)
    pieces = pl.num_programs(0)
    capacity = kinds_rows
    per_owner = rows_in.shape[0] // owners
    span = group_owners * per_owner
    half = group_owners * capacity
    groups = owners // group_owners

    @pl.when(chunk == 0)
    def _():
        pick = (base_column[...] + piece * capacity == iota((2 * half, span), 1)).astype(f32).astype(bf16)
        for group in range(groups):
            got = mm(pick, rows_in[group * span : (group + 1) * span, :]).astype(bf16)
            x_out[0, group * half : (group + 1) * half, :] = got[:half]
            dy_out[0, group * half : (group + 1) * half, :] = got[half:]
        acc_y[...] = jnp.zeros_like(acc_y)
        acc_x[...] = jnp.zeros_like(acc_x)

    pre = mm(x_out[0], w_in[0])
    act, slope = gelu_both(pre)
    act = act.astype(bf16)
    act_out[0] = act
    acc_y[...] += mm(act, w_out[0])
    dpre = (mm_nt(dy_out[0], w_out[0]) * slope).astype(bf16)
    dpre_out[0] = dpre
    acc_x[...] += mm_nt(dpre, w_in[0])

    @pl.when(chunk == chunks - 1)
    def _():
        pick = (base_row[...] + piece * capacity == iota((span, 2 * half), 0)).astype(f32).astype(bf16)
        for group in range(groups):
            here = slice(group * half, (group + 1) * half)
            both = jnp.concatenate([acc_y[here].astype(bf16), acc_x[here].astype(bf16)], axis=0)
            part = mm(pick, both)
            there = slice(group * span, (group + 1) * span)
            full[there] = jnp.where(piece == 0, part, full[there] + part)

    @pl.when((chunk == chunks - 1) & (piece == pieces - 1))
    def _():
        width = out.shape[2]
        shares = out.shape[0] // owners
        for owner in range(owners):
            for share in range(shares):
                out[owner * shares + share] = full[
                    owner * per_owner : (owner + 1) * per_owner, share * width : (share + 1) * width
                ].astype(bf16)


def weight_grads(x_rows, dpre, act, dy):
    w_in_grad = jnp.einsum("lrd,lrf->ldf", x_rows, dpre, preferred_element_type=f32)
    w_out_grad = jnp.einsum("lrf,lrd->lfd", act, dy, preferred_element_type=f32)
    return w_in_grad, w_out_grad


def from_experts(experts, capacity, *refs):
    rows_in, routes_row, keep_row, slot_y, slot_x, out = refs
    slot = column_of(slots_by_row(routes_row[...], keep_row[...], experts, capacity).astype(f32))
    slot = slot.astype(jnp.int32)
    width = rows_in.shape[1]
    pick_y = (slot == slot_y[...]).astype(f32).astype(bf16)
    pick_x = (slot == slot_x[...]).astype(f32).astype(bf16)
    out[:, :width] = mm(pick_y, rows_in[...]).astype(bf16)
    out[:, width:] = mm(pick_x, rows_in[...]).astype(bf16)


def middle_backward(experts, *refs):
    (meta, both_own, both_tp, middle_ref, cotangent, extras, gains, routes_row, keep_row) = refs[:9]
    routes_column, keep_column = columns_of(routes_row, keep_row)
    extras = extras[:, extras.shape[1] - LANES :]
    (result, dmiddle_out, branch_grad, router_grad) = refs[9:]
    share = meta[1]
    width = both_own.shape[1] // 2
    own = both_own[...].astype(f32)
    other = both_tp[...].astype(f32)
    first = jnp.where(share == 0, own, other)
    second = jnp.where(share == 0, other, own)
    picked = jnp.concatenate([first[:, :width], second[:, :width]], axis=1)
    slot_grad = jnp.concatenate([first[:, width:], second[:, width:]], axis=1)
    middle = middle_ref[...]
    scale = rms_scale(middle)
    normed = middle * scale
    gain = gains[1:2]
    hidden = (normed * gain).astype(bf16)
    probs, onehot, kept, gate = routed(hidden, extras, routes_column, keep_column, experts)
    result[...] = middle + gate * picked
    upstream = cotangent[...].astype(f32)
    gate_grad = jnp.sum(upstream * picked, axis=1, keepdims=True)
    prob_grad = jnp.where(onehot, gate_grad * kept, 0.0)
    logit_grad = (
        probs * (prob_grad - jnp.sum(probs * prob_grad, axis=1, keepdims=True))
    ).astype(bf16)
    hidden_grad = slot_grad + mm_nt(logit_grad, extras)
    gain_grad = column_of(jnp.sum(hidden_grad * normed, axis=0, keepdims=True))
    lane = iota((1, LANES), 1)
    router_grad[...] = jnp.where(
        lane == HEAD_SIZE + experts, gain_grad, mm_tn(hidden, logit_grad)
    ).astype(bf16)
    grad = hidden_grad * gain
    dmiddle = upstream + scale * (grad - normed * jnp.mean(grad * normed, axis=1, keepdims=True))
    dmiddle_out[...] = dmiddle
    branch_grad[...] = dmiddle.astype(bf16)


def attention_backward(heads, shard, *refs):
    (meta, lengths, table, x_own, x_other, h1, q_in, k_in, v_in, lse, db) = refs[:11]
    (o_all, wo_ref, wall, router_grad) = refs[11:15]
    (payload, top_out, bottom_out, dh1_own, dh1_other) = refs[15:20]
    (strips, sums, do_all, dq, dk, dv, dqkv, dh1) = refs[20:]
    place = meta[0]
    rows = x_own.shape[0]
    group = 2 * rows
    lanes = q_in.shape[1]
    first_head = place * heads
    own_at = pl.ds(pl.multiple_of(place * rows, 16), rows)
    other_at = pl.ds(pl.multiple_of((1 - place) * rows, 16), rows)
    both = mm(db[...], wo_ref[...])
    high = pltpu.roll(both[:, LANES : LANES + lanes], lanes - HEAD_SIZE, 1)
    do_all[...] = jnp.where(place == 0, both[:, :lanes], high).astype(bf16)
    bias_strips(table, first_head, heads, strips)
    segment_row = segments(lengths, group, 1)
    segment_column = segments(lengths, group, 0)
    blocks = group // STRIP
    sums[...] = jnp.zeros_like(sums)
    keys = k_in[...]
    values = v_in[...]
    ahead = [jnp.zeros((STRIP, STRIP), f32) for _ in range(heads)]
    behind = [jnp.zeros((STRIP, STRIP), f32) for _ in range(heads)]
    for block in range(blocks):
        at = slice(block * STRIP, (block + 1) * STRIP)
        same = segment_column[at] == segment_row
        dq_total = jnp.zeros((STRIP, lanes), f32)
        for head in range(heads):
            query = pick_head(q_in[at, :], head, lanes)
            scores = mm_nt(query, keys) + bias_row(strips, table, head, first_head, block, blocks)
            scores = jnp.where(same, scores, masked_value)
            chances = jnp.exp(scores - lse[at, head : head + 1])
            grad = pick_head(do_all[at, :], head, lanes)
            chance_grad = mm_nt(grad, values)
            mean = jnp.sum(chances * chance_grad, axis=1, keepdims=True)
            score_grad = (chances * (chance_grad - mean)).astype(bf16)
            dv_part = mm_tn(chances.astype(bf16), grad)
            dk_part = mm_tn(score_grad, query)
            if block == 0 and head == 0:
                dv[...] = dv_part
                dk[...] = dk_part
            else:
                dv[...] += dv_part
                dk[...] += dk_part
            dq_total = dq_total + mm(score_grad, pick_head(keys, head, lanes))
            rounded = score_grad.astype(f32)
            for other in range(blocks):
                gap = other - block
                part = rounded[:, other * STRIP : (other + 1) * STRIP]
                if abs(gap) <= 1:
                    sums[head, :, (gap + 2) * STRIP : (gap + 3) * STRIP] += part
                elif gap > 0:
                    ahead[head] = ahead[head] + part
                else:
                    behind[head] = behind[head] + part
        dq[at, :] = dq_total
    half = HEAD_SIZE
    dqkv[:, :LANES] = dq[:, :LANES].astype(bf16)
    shifted = pltpu.roll(dk[...], half, 1)
    dqkv[:, LANES : 2 * LANES] = (dq[:, LANES:] + shifted[:, :LANES]).astype(bf16)
    dqkv[:, 2 * LANES : 3 * LANES] = shifted[:, LANES:].astype(bf16)
    dqkv[:, 3 * LANES :] = dv[...].astype(bf16)
    dh1[...] = mm_nt(dqkv[...], wall[...])
    gain_part = None
    for source, at, target in ((x_own, own_at, dh1_own), (x_other, other_at, dh1_other)):
        values = source[...].astype(f32)
        grad = dh1[at, :]
        target[...] = grad.astype(bf16)
        part = jnp.sum(grad * (values * rms_scale(values)), axis=0, keepdims=True)
        gain_part = part if gain_part is None else gain_part + part
    buckets = table.shape[1]
    spread = skew(sums[...].reshape(heads * STRIP, 4 * STRIP), False)
    diagonals = jnp.sum(spread.reshape(heads, STRIP, 4 * STRIP), axis=1)
    picks = (bucket_index(iota((4 * STRIP, 1), 0) - 2 * STRIP) == iota((1, LANES), 1)).astype(f32)
    in_buckets = jnp.dot(diagonals, picks, precision=highest, preferred_element_type=f32)
    lane = iota((1, LANES), 1)
    row = lax.rem(iota((wall.shape[0], 1), 0), shard)
    riders = jnp.where(lane == HEAD_SIZE, column_of(gain_part), 0.0)
    for head in range(heads):
        line = in_buckets[head : head + 1]
        line = line + jnp.where(lane == buckets - 1, jnp.sum(ahead[head]), 0.0)
        line = line + jnp.where(lane == buckets // 2 - 1, jnp.sum(behind[head]), 0.0)
        riders = riders + jnp.where(row == head, pltpu.roll(line, HEAD_SIZE + 1, 1), 0.0)
    width = wall.shape[1]
    grads = mm_tn(h1[...], dqkv[...])
    payload[:, : width - LANES] = grads[:, : width - LANES].astype(bf16)
    payload[:, width - LANES : width] = (grads[:, width - LANES :] + riders).astype(bf16)
    grads = mm_tn(db[...], o_all[...])
    payload[:, width : width + lanes - LANES] = grads[:, : lanes - LANES].astype(bf16)
    payload[:, width + lanes - LANES :] = (
        grads[:, lanes - LANES :] + router_grad[...].astype(f32)
    ).astype(bf16)
    half = top_out.shape[0]
    across = pl.multiple_of(meta[3] * shard if 2 * half == shard else 0 * meta[3], 16)
    top_out[...] = payload[pl.ds(across, half), :]
    bottom_out[...] = payload[pl.ds(across + half, half), :]


def ring_add(places, right_mine, left_mine, from_left, from_right, right_out, left_out):
    rows = right_mine.shape[0]
    span = from_left.shape[0]
    right_out[...] = right_mine[...]
    left_out[...] = left_mine[...]
    top, bottom = slice(0, span), slice(rows - span, rows)
    right_out[top] = (right_mine[top].astype(f32) + from_left[...].astype(f32)).astype(bf16)
    left_out[bottom] = (left_mine[bottom].astype(f32) + from_right[...].astype(f32)).astype(bf16)


def ring_end(at, place, sums, own, send, table, riders_own, riders_other):
    rows = own.shape[0]
    first, second = sums[:rows, :], sums[rows : 2 * rows, :]
    mine = jnp.where(place == 0, first, second)
    other = jnp.where(place == 0, second, first)
    own[...] = mine
    send[:rows, :] = other
    send[rows:, :] = sums[:8, :]
    table[...] = sums[:8, at : at + LANES]
    riders_own[...] = mine[:, at : at + LANES]
    riders_other[...] = other[:, at : at + LANES]


def ring_last(at, places, mine, from_left, from_right, own, send, table, riders_own, riders_other):
    total = mine[...].astype(f32) + from_left[...].astype(f32) + from_right[...].astype(f32)
    ring_end(at, places[0], total, own, send, table, riders_own, riders_other)


def ring_whole(at, places, sums, own, send, table, riders_own, riders_other):
    ring_end(at, places[0], sums[...], own, send, table, riders_own, riders_other)


def shards_of_sums(experts, buckets, heads, *refs):
    (meta, own_ref, other, own_top, from_tp, from_far) = refs[:6]
    (query_out, key_out, value_out, output_out, router_out, gain_one, gain_two, table) = refs[6:]
    place = meta[0]
    rows, width = query_out.shape[0], query_out.shape[1] // 2
    lanes = width + HEAD_SIZE
    wide = 3 * width + HEAD_SIZE
    own = own_ref[...]
    more = other[:rows, :]
    lane = iota((1, lanes), 1)
    for at, moved, out in (
        (0, False, query_out),
        (LANES, True, key_out),
        (2 * width, False, value_out),
        (wide, False, output_out),
    ):
        parts = [values[:, at : at + lanes] for values in (own, more)]
        if moved:
            parts = [pltpu.roll(part, lanes - HEAD_SIZE, 1) for part in parts]
        parts = [jnp.where(lane < width, part, 0.0) for part in parts]
        first = jnp.where(place == 0, parts[0], parts[1])
        second = jnp.where(place == 0, parts[1], parts[0])
        for index, block in enumerate(join(first, second)):
            out[:, index * LANES : (index + 1) * LANES] = block
    total = (own + more)[:, wide + lanes - LANES :].T
    router_out[...] = total[HEAD_SIZE : HEAD_SIZE + experts, :]
    gain_two[...] = total[HEAD_SIZE + experts : HEAD_SIZE + experts + 1, :]
    line = (own + more)[:, wide - LANES : wide] + (from_tp[...] + from_far[...])
    gain_one[...] = line.T[HEAD_SIZE : HEAD_SIZE + 1, :]
    own_lines = own_top[...]
    other_lines = other[rows : rows + 8, wide - LANES : wide]
    own_lines = pltpu.roll(own_lines, LANES - HEAD_SIZE - 1, 1)
    other_lines = pltpu.roll(other_lines, LANES - HEAD_SIZE - 1, 1)
    table[:heads, :] = jnp.where(place == 0, own_lines, other_lines)[:heads, :buckets]
    table[heads : 2 * heads, :] = jnp.where(place == 0, other_lines, own_lines)[:heads, :buckets]


def input_backward(x_own, dmiddle, gains, near, far, out):
    values = x_own[...].astype(f32)
    scale = rms_scale(values)
    normed = values * scale
    grad = (near[...].astype(f32) + far[...].astype(f32)) * gains[0:1]
    out[...] = dmiddle[...] + scale * (
        grad - normed * jnp.mean(grad * normed, axis=1, keepdims=True)
    )


def swap(value, axis):
    return lax.ppermute(value, axis, [(0, 1), (1, 0)])


def ring_order(count):
    return list(range(0, count, 2)) + list(range(count - 1, 0, -2))


def ring_steps(count):
    order = ring_order(count)
    right = [(order[i], order[(i + 1) % count]) for i in range(count)]
    return order, right, [(b, a) for a, b in right]


def device_table(fsdp_count, ctx_count, tp_count, aligned):
    order = ring_order(fsdp_count)
    rows = []
    for place in range(fsdp_count):
        spot = order.index(place)
        at = lambda distance: order[(spot + distance) % fsdp_count]
        half = fsdp_count // 2
        ring = [place]
        for step in range(1, half):
            ring += [at(-step), at(step)]
        ring.append(at(half))
        for step in range(half, 0, -1):
            ring += [at(step - 1), at(1 - step)]
        for core in range(ctx_count):
            for share in range(tp_count):
                rows.append([core, share, core if aligned else 0, at(half)] + (ring if aligned else []))
    return np.array(rows, np.int32)


def ring_gather(shard, count):
    _, right, left = ring_steps(count)
    shards = [shard]
    going_right, going_left = shard, shard
    for step in range(1, count // 2):
        going_right = lax.ppermute(going_right, "fsdp", right)
        going_left = lax.ppermute(going_left, "fsdp", left)
        shards += [going_right, going_left]
    shards.append(lax.ppermute(going_right, "fsdp", right))
    return shards


def ring_sums(payload, top, bottom, count, at, meta, side):
    rows = payload.shape[0] // count
    lanes = payload.shape[1]
    half = rows // 2
    outs = [
        shape((half, lanes), f32),
        shape((half + 8, lanes), f32),
        shape((8, LANES), f32),
        shape((half, LANES), f32),
        shape((half, LANES), f32),
    ]
    if rows % 32 or count % 2:
        sums = lax.psum_scatter(payload.astype(f32), "fsdp", scatter_dimension=0, tiled=True)
        return kernel_call(functools.partial(ring_whole, at), outs, [smem, vmem])(meta, sums)
    _, right, left = ring_steps(count)
    going_right, going_left = top, bottom
    spec = lambda which: pl.BlockSpec((rows, lanes), lambda i, places: (places[which], 0))
    params = pltpu.CompilerParams(vmem_limit_bytes=SMALL_VMEM_BYTES)
    for step in range(count // 2, 0, -1):
        from_left = lax.ppermute(going_right, "fsdp", right)
        from_right = lax.ppermute(going_left, "fsdp", left)
        which = 4 + count + 2 * (count // 2 - step)
        whole = lambda dims: pl.BlockSpec(dims, lambda i, places: (0, 0))
        last = step == 1
        if last:
            side, from_left, from_right = lax.optimization_barrier((side, from_left, from_right))
        step_outs = outs if last else [shape((rows, lanes), bf16)] * 2
        out = pl.pallas_call(
            functools.partial(ring_last, at) if last else ring_add,
            grid_spec=pltpu.PrefetchScalarGridSpec(
                num_scalar_prefetch=1,
                grid=(1,),
                in_specs=([spec(which)] if last else [spec(which), spec(which + 1)])
                + [whole(from_left.shape), whole(from_right.shape)],
                out_specs=[whole(o.shape) for o in step_outs],
            ),
            out_shape=step_outs,
            compiler_params=params,
            cost_estimate=pl.CostEstimate(flops=0, bytes_accessed=1024 * 1024, transcendentals=0),
        )(meta, *([payload] if last else [payload, payload]), from_left, from_right)
        if last:
            return out
        going_right, going_left = out


def body(
    tokens,
    cotangent,
    w_query,
    w_key,
    w_value,
    w_output,
    w_router,
    gain_attn,
    gain_moe,
    rel_table,
    w_in,
    w_out,
    lengths,
    routes,
    keep_mask,
):
    rows, model_width = tokens.shape
    fsdp_count = lax.axis_size("fsdp")
    owners = lax.axis_size(("fsdp", "ctx"))
    tp_count = lax.axis_size("tp")
    place = lax.axis_index("ctx")
    share = lax.axis_index("tp")
    fsdp_place = lax.axis_index("fsdp")
    group = 2 * rows
    experts = w_router.shape[1]
    capacity = max(2, (5 * rows + 4 * experts - 1) // (4 * experts))
    pieces = w_in.shape[0]
    split_count = owners * pieces // experts
    hidden_width = w_in.shape[2]
    heads = rel_table.shape[1] // 2
    heads_all = heads * 2 * tp_count
    width = heads * HEAD_SIZE
    lanes = width + HEAD_SIZE
    shard_rows = w_query.shape[0]
    buckets = rel_table.shape[0]

    def full(dims, dtype):
        return shape(dims, dtype)

    wide = 3 * width + HEAD_SIZE
    aligned = shard_rows % 16 == 0 and fsdp_count % 2 == 0
    count = fsdp_count if aligned else 1
    table = jnp.asarray(device_table(fsdp_count, 2, tp_count, aligned))
    device = lax.axis_index(("fsdp", "ctx", "tp"))
    meta = lax.dynamic_slice(table, (device, 0), (1, table.shape[1])).reshape(-1)
    table_rows = rel_table.T
    shard_own, shard_send, wo_shard = kernel_call(
        pack_rows,
        [full((shard_rows, wide), bf16), full((shard_rows, wide), bf16), full((2 * shard_rows, lanes), bf16)],
        [smem] + [vmem] * 7,
        moved=512 * 1024,
    )(meta, w_query, w_key, w_value, w_output, w_router.T, gain_attn[None, :], gain_moe[None, :])
    shard_other = swap(shard_send, "ctx")
    shard = jnp.concatenate(
        [jnp.concatenate([shard_own, shard_other], axis=0), wo_shard], axis=1
    )
    x_other = swap(tokens, "ctx")

    def ordered(own, other):
        if aligned:
            return own, other
        dims = (fsdp_count, 1, shard_rows, own.shape[1])
        pair = in_order(own.reshape(dims), other.reshape(dims), 1).reshape(2 * own.shape[0], -1)
        return pair[: own.shape[0]], pair[own.shape[0] :]

    def in_order(own, other, axis):
        return jnp.where(
            place == 0,
            jnp.concatenate([own, other], axis=axis),
            jnp.concatenate([other, own], axis=axis),
        )

    if aligned:
        shards = ring_gather(shard, fsdp_count)
        wall, wo_own = kernel_call(
            functools.partial(put_in_rows, len(shards)),
            [full((model_width, wide), bf16), full((model_width // 2, 2 * width), bf16)],
            [smem] + [vmem] * len(shards),
            moved=4 * 1024 * 1024,
        )(meta, *shards)
    else:
        both = lax.all_gather(shard, "fsdp", axis=0, tiled=False)
        near, far = both[:, :shard_rows], both[:, shard_rows:]
        wall = jnp.concatenate(
            ordered(near[:, :, :wide].reshape(-1, wide), far[:, :, :wide].reshape(-1, wide)), axis=0
        )
        wo_own = jnp.concatenate([near[:, :, wide : wide + width], far[:, :, wide : wide + width]], axis=2)
        wo_own = wo_own.reshape(-1, 2 * width)

    h1, q, k, v, o_own, o_other, o_all, lse, gains = kernel_call(
        functools.partial(attention_forward, heads, experts),
        [
            full((group, model_width), bf16),
            full((group, lanes), bf16),
            full((group, lanes), bf16),
            full((group, lanes), bf16),
            full((rows // 2, 2 * width), bf16),
            full((rows // 2, 2 * width), bf16),
            full((group, lanes), bf16),
            full((group, LANES), f32),
            full((8, model_width), f32),
        ],
        [smem] * 3 + [vmem] * 3,
        scratch=[pltpu.VMEM((heads, STRIP, 3 * STRIP), f32)],
        flops=2 * group * model_width * wide * 8,
        moved=8 * 1024 * 1024,
    )(meta, lengths, table_rows, tokens, x_other, wall)
    wo_tp = swap(wo_own, "tp")
    wo_ctx = swap(wo_own, "ctx")
    wo_tp, gains = lax.optimization_barrier((wo_tp, gains))
    wo_far = swap(wo_tp, "ctx")
    wo_own, wo_ctx = ordered(wo_own, wo_ctx)
    wo_tp, wo_far = ordered(wo_tp, wo_far)

    o_tp = swap(o_own, "tp")
    o_ctx = swap(o_other, "ctx")
    o_far = lax.ppermute(o_other, ("ctx", "tp"), [(i, 3 - i) for i in range(4)])

    per_owner = 2 * pieces * capacity
    owner_of = np.repeat(np.arange(owners), per_owner)
    inside = np.tile(np.arange(per_owner), owners)
    kind = inside // (pieces * capacity)
    piece_of = owner_of * pieces + (inside // capacity) % pieces
    slot_of = (piece_of // split_count) * capacity + inside % capacity
    slot_first = np.where(kind == 0, slot_of, -1).astype(np.int32)
    slot_second = np.where(kind == 1, slot_of, -1).astype(np.int32)
    routes_row = routes.reshape(1, rows)
    keep_row = keep_mask.reshape(1, rows)

    middle, sends, wo_full = kernel_call(
        functools.partial(to_experts, experts, capacity, count),
        [
            full((rows, model_width), f32),
            full((owners * per_owner, model_width), bf16),
            full((model_width, 2 * width), bf16),
        ],
        [smem] + [vmem] * 16,
        scratch=[pltpu.VMEM((model_width, 2 * width), bf16)],
        flops=2 * rows * model_width * (model_width + 2 * owners * per_owner),
        moved=6 * 1024 * 1024,
    )(
        meta, tokens, cotangent, o_own, o_tp, o_ctx, o_far, wo_own, wo_tp, wo_ctx, wo_far, wall,
        gains, routes_row, keep_row, slot_first[:, None], slot_second[:, None],
    )

    arrived = lax.all_to_all(
        sends.reshape(owners, per_owner, model_width),
        ("fsdp", "ctx"),
        split_axis=0,
        concat_axis=0,
        tiled=True,
    ).reshape(owners * per_owner, model_width)

    group_owners = min(16, owners)
    half = group_owners * capacity
    spot = np.arange(2 * half) % half
    base = (
        (spot // capacity) * per_owner
        + (np.arange(2 * half) // half) * pieces * capacity
        + spot % capacity
    ).astype(np.int32)
    chunk_width = 768 if hidden_width % 768 == 0 else hidden_width
    chunks = hidden_width // chunk_width
    slot_rows = owners * capacity
    part_width = model_width // tp_count
    whole = lambda *dims: pl.BlockSpec(dims, lambda i, j: (0,) * len(dims))
    outgoing, x_rows, dy_rows, act, dpre = kernel_call(
        functools.partial(expert_kernel, owners, capacity, chunks, group_owners),
        [
            full((owners * tp_count, per_owner, part_width), bf16),
            full((pieces, slot_rows, model_width), bf16),
            full((pieces, slot_rows, model_width), bf16),
            full((pieces, slot_rows, hidden_width), bf16),
            full((pieces, slot_rows, hidden_width), bf16),
        ],
        [
            whole(owners * per_owner, model_width),
            whole(2 * half, 1),
            whole(1, 2 * half),
            pl.BlockSpec((1, model_width, chunk_width), lambda i, j: (i, 0, j)),
            pl.BlockSpec((1, chunk_width, model_width), lambda i, j: (i, j, 0)),
        ],
        out_specs=[
            whole(owners * tp_count, per_owner, part_width),
            pl.BlockSpec((1, slot_rows, model_width), lambda i, j: (i, 0, 0)),
            pl.BlockSpec((1, slot_rows, model_width), lambda i, j: (i, 0, 0)),
            pl.BlockSpec((1, slot_rows, chunk_width), lambda i, j: (i, 0, j)),
            pl.BlockSpec((1, slot_rows, chunk_width), lambda i, j: (i, 0, j)),
        ],
        scratch=[
            pltpu.VMEM((slot_rows, model_width), f32),
            pltpu.VMEM((slot_rows, model_width), f32),
            pltpu.VMEM((owners * per_owner, model_width), f32),
        ],
        grid=(pieces, chunks),
        flops=8 * pieces * slot_rows * model_width * hidden_width,
        moved=12 * 1024 * 1024,
    )(arrived, base[:, None], base[None, :], w_in, w_out)

    returned = lax.all_to_all(
        outgoing, ("fsdp", "ctx", "tp"), split_axis=0, concat_axis=0, tiled=True
    ).reshape(owners * tp_count * per_owner, part_width)
    w_in_grad, w_out_grad = weight_grads(x_rows, dpre, act, dy_rows)
    returned, w_in_grad, w_out_grad = lax.optimization_barrier((returned, w_in_grad, w_out_grad))

    back_first = np.repeat(slot_first.reshape(owners, 1, per_owner), tp_count, axis=1).reshape(1, -1)
    back_second = np.repeat(slot_second.reshape(owners, 1, per_owner), tp_count, axis=1).reshape(1, -1)
    both_own = kernel_call(
        functools.partial(from_experts, experts, capacity),
        [full((rows, 2 * part_width), bf16)],
        [vmem] * 5,
        flops=4 * rows * returned.shape[0] * part_width,
        moved=2 * 1024 * 1024,
    )(returned, routes_row, keep_row, back_first, back_second)[0]
    both_tp = swap(both_own, "tp")

    result, middle_grad, db_own, router_grad = kernel_call(
        functools.partial(middle_backward, experts),
        [
            full((rows, model_width), f32),
            full((rows, model_width), f32),
            full((rows, model_width), bf16),
            full((model_width, LANES), bf16),
        ],
        [smem] + [vmem] * 8,
        flops=6 * rows * LANES * model_width,
        moved=6 * 1024 * 1024,
    )(meta, both_own, both_tp, middle, cotangent, wall, gains, routes_row, keep_row)
    db = lax.all_gather(db_own, "ctx", axis=0, tiled=True)

    half = model_width // fsdp_count // 2
    payload, top, bottom, dh1_own, dh1_other = kernel_call(
        functools.partial(attention_backward, heads, model_width // fsdp_count),
        [
            full((model_width, wide + lanes), bf16),
            full((half if aligned else 16, wide + lanes), bf16),
            full((half if aligned else 16, wide + lanes), bf16),
            full((rows, model_width), bf16),
            full((rows, model_width), bf16),
        ],
        [smem] * 3 + [vmem] * 12,
        scratch=[
            pltpu.VMEM((heads, STRIP, 3 * STRIP), f32),
            pltpu.VMEM((heads, STRIP, 4 * STRIP), f32),
            pltpu.VMEM((group, lanes), bf16),
            pltpu.VMEM((group, lanes), f32),
            pltpu.VMEM((group, lanes), f32),
            pltpu.VMEM((group, lanes), f32),
            pltpu.VMEM((group, wide), bf16),
            pltpu.VMEM((group, model_width), f32),
        ],
        flops=2 * group * model_width * wide * 12,
        moved=8 * 1024 * 1024,
    )(
        meta, lengths, table_rows, tokens, x_other, h1, q, k, v, lse, db,
        o_all, wo_full, wall, router_grad,
    )

    dh1_sum = (dh1_own.astype(f32) + swap(dh1_other, "ctx").astype(f32)).astype(bf16)
    dh1_far = swap(dh1_sum, "tp")
    own, send, own_lines, riders_own, riders_other = ring_sums(
        payload, top, bottom, fsdp_count, wide - LANES, meta, dh1_far
    )
    other = swap(send, "ctx")
    from_tp = swap(riders_own, "tp")
    from_far = lax.ppermute(riders_other, ("ctx", "tp"), [(i, 3 - i) for i in range(4)])
    input_grad = kernel_call(
        input_backward,
        [full((rows, model_width), f32)],
        [vmem] * 5,
        moved=4 * 1024 * 1024,
    )(tokens, middle_grad, gains, dh1_sum, dh1_far)[0]
    other, input_grad = lax.optimization_barrier((other, input_grad))

    shard = full((shard_rows, 2 * width), f32)
    query_grad, key_grad, value_grad, output_grad, router_sum, gain_one, gain_two, table_grad = kernel_call(
        functools.partial(shards_of_sums, experts, buckets, heads),
        [shard] * 4
        + [
            full((experts, shard_rows), f32),
            full((1, shard_rows), f32),
            full((1, shard_rows), f32),
            full((2 * heads, buckets), f32),
        ],
        [smem] + [vmem] * 5,
        moved=1024 * 1024,
    )(meta, own, other, own_lines, from_tp, from_far)
    return (
        result,
        input_grad,
        query_grad,
        key_grad,
        value_grad,
        output_grad,
        router_sum.T,
        gain_one.reshape(shard_rows),
        gain_two.reshape(shard_rows),
        table_grad.T,
        w_in_grad,
        w_out_grad,
    )


def solution(mesh):
    in_specs = (
        P(("fsdp", "ctx"), None),
        P(("fsdp", "ctx"), None),
        P(("fsdp", "ctx"), "tp"),
        P(("fsdp", "ctx"), "tp"),
        P(("fsdp", "ctx"), "tp"),
        P(("fsdp", "ctx"), "tp"),
        P(("fsdp", "ctx"), None),
        P(("fsdp", "ctx")),
        P(("fsdp", "ctx")),
        P(None, "tp"),
        P(("fsdp", "ctx"), None, "tp"),
        P(("fsdp", "ctx"), "tp", None),
        P("fsdp", None),
        P(("fsdp", "ctx"), None),
        P(("fsdp", "ctx")),
    )
    out_specs = (
        P(("fsdp", "ctx"), None),
        P(("fsdp", "ctx"), None),
        P(("fsdp", "ctx"), "tp"),
        P(("fsdp", "ctx"), "tp"),
        P(("fsdp", "ctx"), "tp"),
        P(("fsdp", "ctx"), "tp"),
        P(("fsdp", "ctx"), None),
        P(("fsdp", "ctx")),
        P(("fsdp", "ctx")),
        P(None, "tp"),
        P(("fsdp", "ctx"), None, "tp"),
        P(("fsdp", "ctx"), "tp", None),
    )
    return jax.shard_map(body, mesh=mesh, in_specs=in_specs, out_specs=out_specs, check_vma=False)
```

```python
import functools

import jax
import jax.numpy as jnp
import numpy as np
from jax import lax
from jax.experimental import pallas as pl
from jax.experimental.pallas import tpu as pltpu
from jax.sharding import PartitionSpec as P

epsilon = 1e-06
masked_value = -1e30
bucket_edges = (12, 16, 23, 32, 46, 64, 91)
highest = lax.Precision.HIGHEST
LANES = 128
STRIP = 128
HEAD_SIZE = 64
MIB = 1024 * 1024
f32 = jnp.float32
bf16 = jnp.bfloat16
vmem = pl.BlockSpec(memory_space=pltpu.VMEM)
smem = pl.BlockSpec(memory_space=pltpu.SMEM)


def mm(left, right):
    return jnp.dot(left, right, preferred_element_type=f32)


def mm_nt(left, right):
    return lax.dot_general(left, right, (((1,), (1,)), ((), ())), preferred_element_type=f32)


def mm_tn(left, right):
    return lax.dot_general(left, right, (((0,), (0,)), ((), ())), preferred_element_type=f32)


def rms_scale(values):
    return lax.rsqrt(jnp.mean(values * values, axis=-1, keepdims=True) + epsilon)


def iota(shape, dim):
    return lax.broadcasted_iota(jnp.int32, shape, dim)


def bucket_index(offset):
    side = jnp.where(offset > 0, 16, 0).astype(jnp.int32)
    distance = jnp.abs(offset)
    far_bucket = 8 + sum(((distance >= edge).astype(jnp.int32) for edge in bucket_edges))
    return side + jnp.where(distance < 8, distance, far_bucket)


def kernel_call(body, outs, in_specs, out_specs=None, scratch=(), grid=None, flops=0, moved=0, mib=16):
    extra = {} if grid is None else {"grid": grid}
    return pl.pallas_call(
        body,
        out_shape=outs,
        in_specs=in_specs,
        out_specs=[vmem] * len(outs) if out_specs is None else out_specs,
        scratch_shapes=list(scratch),
        compiler_params=pltpu.CompilerParams(vmem_limit_bytes=mib * MIB),
        cost_estimate=pl.CostEstimate(flops=flops, bytes_accessed=moved, transcendentals=0),
        **extra,
    )


def shape(dims, dtype):
    return jax.ShapeDtypeStruct(tuple(dims), dtype)


def segments(lengths_ref, columns, rows):
    places = iota((rows, columns), 1)
    total = jnp.zeros((rows, columns), jnp.int32)
    end = 0
    for entry in range(lengths_ref.shape[1]):
        end = end + lengths_ref[0, entry]
        total = total + (places >= end).astype(jnp.int32)
    return total


def column_of(line):
    return jnp.broadcast_to(line, (LANES, line.shape[1])).T[:, :1]


def skew(values, right):
    rows, lanes = values.shape
    row = lax.rem(iota((rows, 1), 0), STRIP)
    step = 1
    while step < STRIP:
        moved = pltpu.roll(values, step if right else lanes - step, 1)
        values = jnp.where((row & step) > 0, moved, values)
        step *= 2
    return values


def attention_tables(heads, meta, lengths, table, strips, far, segment):
    lanes = 4 * STRIP
    buckets = table.shape[1]
    first_head = meta[0] * heads
    bucket = bucket_index(iota((1, lanes), 1) - 2 * STRIP)
    far[...] = jnp.zeros_like(far)
    for head in range(heads):
        line = jnp.zeros((1, lanes), f32)
        for entry in range(buckets):
            line = jnp.where(bucket == entry, table[first_head + head, entry], line)
        strip = skew(jnp.broadcast_to(line, (STRIP, lanes)), True)
        strips[head] = strip[:, STRIP:]
        far[2 * head : 2 * head + 1, :] = jnp.full((1, LANES), table[first_head + head, buckets - 1], f32)
        far[2 * head + 1 : 2 * head + 2, :] = jnp.full(
            (1, LANES), table[first_head + head, buckets // 2 - 1], f32
        )
    segment[...] = segments(lengths, segment.shape[1], segment.shape[0])


def bias_row(strips, far, head, block, blocks):
    parts = []
    for other in range(blocks):
        gap = other - block
        if abs(gap) <= 1:
            parts.append(strips[head, :, (gap + 1) * STRIP : (gap + 2) * STRIP])
        else:
            row = 2 * head + (0 if gap > 0 else 1)
            parts.append(jnp.broadcast_to(far[row : row + 1, :], (STRIP, STRIP)))
    return jnp.concatenate(parts, axis=1)


def head_mask(head, lanes):
    lane = iota((1, lanes), 1)
    return (lane >= head * HEAD_SIZE) & (lane < (head + 1) * HEAD_SIZE)


def pick_head(values, head, lanes):
    return jnp.where(head_mask(head, lanes), values, 0.0).astype(bf16)


def half_columns(weight, which):
    values = weight[...].astype(f32)
    width = values.shape[1] // 2
    lanes = width + HEAD_SIZE
    high = pltpu.roll(values[:, LANES : LANES + lanes], lanes - HEAD_SIZE, 1)
    picked = jnp.where(which == 0, values[:, :lanes], high)
    return jnp.where(iota((1, lanes), 1) < width, picked, 0.0)


def join(first, second):
    moved = pltpu.roll(second, HEAD_SIZE, 1)
    return first[:, :LANES], first[:, LANES:] + moved[:, :LANES], moved[:, LANES:]


def pack_rows(*refs):
    (meta, w_query, w_key, w_value, w_output, w_router, gain_one, gain_two, own, send, output) = refs
    rows = w_query.shape[0]
    experts = w_router.shape[0]
    width = w_query.shape[1] // 2
    lanes = width + HEAD_SIZE
    lane = iota((1, lanes), 1)
    diagonal = iota((rows, rows), 0) == iota((rows, rows), 1)
    placing = (iota((experts, lanes), 0) + width == iota((experts, lanes), 1)).astype(f32)
    extras = mm_tn(w_router[...], placing.astype(bf16))
    for index, gain in enumerate((gain_one, gain_two)):
        column = jnp.sum(
            jnp.where(diagonal, jnp.broadcast_to(gain[...].astype(f32), (rows, rows)), 0.0),
            axis=1,
            keepdims=True,
        )
        extras = extras + jnp.where(lane == width + experts + index, column, 0.0)
    for which, out in ((meta[0], own), (1 - meta[0], send)):
        at = 0
        for block in join(half_columns(w_query, which), half_columns(w_key, which)):
            out[:, at : at + LANES] = block.astype(bf16)
            at += LANES
        out[:, at:] = (half_columns(w_value, which) + extras).astype(bf16)
    output[:rows, :] = half_columns(w_output, 0).astype(bf16)
    output[rows:, :] = half_columns(w_output, 1).astype(bf16)


def put_in_rows(count, *refs):
    meta = refs[0]
    shards = refs[1 : 1 + count]
    wall, output = refs[1 + count :]
    wide = wall.shape[1]
    place = meta[0]
    for index, shard in enumerate(shards):
        rows = shard.shape[0] // 2
        first = meta[4 + index]
        for half, core in ((0, place), (1, 1 - place)):
            at = pl.multiple_of((2 * first + core) * rows, 16)
            wall[pl.ds(at, rows), :] = shard[half * rows : (half + 1) * rows, :wide]
        blocks = join(shard[:rows, wide:].astype(f32), shard[rows:, wide:].astype(f32))
        at = pl.multiple_of(first * rows, 16)
        for block, values in enumerate(blocks):
            output[pl.ds(at, rows), block * LANES : (block + 1) * LANES] = values.astype(bf16)


def interleave(out, lanes, own, other, place, count):
    rows = own.shape[0] // count
    for index in range(count):
        here = slice(index * rows, (index + 1) * rows)
        first = pl.multiple_of((2 * index + place) * rows, 16)
        second = pl.multiple_of((2 * index + 1 - place) * rows, 16)
        out[pl.ds(first, rows), lanes] = own[here, :]
        out[pl.ds(second, rows), lanes] = other[here, :]


def attention_forward(heads, experts, *refs):
    (meta, x_own, x_other, wall, strips, far, segment) = refs[:7]
    (h1, q_out, k_out, v_out, o_own, o_other, o_all, probs, gains) = refs[7:]
    place = meta[0]
    rows = x_own.shape[0]
    group = 2 * rows
    width = wall.shape[1]
    extras = wall[:, width - LANES :].astype(f32).T
    gain_at = HEAD_SIZE + experts
    gains[...] = extras[gain_at : gain_at + 8]
    gain_one = gains[0:1]
    for source, start in ((x_own, place * rows), (x_other, (1 - place) * rows)):
        values = source[...].astype(f32)
        h1[pl.ds(pl.multiple_of(start, 16), rows), :] = (
            values * rms_scale(values) * gain_one
        ).astype(bf16)
    qkv = mm(h1[...], wall[...])
    lanes = q_out.shape[1]
    q_out[...] = qkv[:, :lanes].astype(bf16)
    k_out[...] = pltpu.roll(qkv[:, LANES : LANES + lanes], lanes - HEAD_SIZE, 1).astype(bf16)
    v_out[...] = qkv[:, width - lanes :].astype(bf16)
    segment_row = segment[0:1, :]
    segment_column = column_of(segment_row.astype(f32)).astype(jnp.int32)
    keys = k_out[...]
    blocks = group // STRIP
    values_of = [pick_head(v_out[...], head, lanes) for head in range(heads)]
    for block in range(blocks):
        first = block * STRIP
        same = segment_column[first : first + STRIP] == segment_row
        total = jnp.zeros((STRIP, lanes), f32)
        for head in range(heads):
            query = pick_head(q_out[first : first + STRIP, :], head, lanes)
            scores = mm_nt(query, keys) + bias_row(strips, far, head, block, blocks)
            scores = jnp.where(same, scores, masked_value)
            top = jnp.max(scores, axis=1, keepdims=True)
            raised = jnp.exp(scores - top)
            mass = jnp.sum(raised, axis=1, keepdims=True)
            chances = raised * (1.0 / mass)
            probs[head, first : first + STRIP, :] = chances
            total = total + mm(chances.astype(bf16), values_of[head])
        o_all[first : first + STRIP, :] = total.astype(bf16)
    for out, start in ((o_own, place * rows), (o_other, (1 - place) * rows)):
        values = o_all[pl.ds(pl.multiple_of(start, 16), rows), :].astype(f32)
        for index, part in enumerate(join(values[: rows // 2], values[rows // 2 :])):
            out[:, index * LANES : (index + 1) * LANES] = part.astype(bf16)


def columns_of(*lines):
    return [column_of(line[...].astype(f32)).astype(jnp.int32) for line in lines]


def routed(hidden, extras, routes_column, keep_column, experts):
    logits = mm(hidden, extras)
    lane = iota((1, LANES), 1) - HEAD_SIZE
    valid = (lane >= 0) & (lane < experts)
    logits = jnp.where(valid, logits, masked_value)
    raised = jnp.where(valid, jnp.exp(logits - jnp.max(logits, axis=1, keepdims=True)), 0.0)
    probs = raised / jnp.sum(raised, axis=1, keepdims=True)
    onehot = lane == routes_column
    kept = keep_column.astype(f32)
    gate = jnp.sum(jnp.where(onehot, probs, 0.0), axis=1, keepdims=True) * kept
    return probs, onehot, kept, gate


def slots_by_row(routes_row, keep_row, experts, capacity):
    count = routes_row.shape[1]
    chosen = ((iota((experts, count), 0) == routes_row) & (keep_row == 1)).astype(f32)
    before = (iota((count, count), 0) < iota((count, count), 1)).astype(bf16)
    earlier = mm(chosen.astype(bf16), before)
    rank = jnp.sum(earlier * chosen, axis=0, keepdims=True).astype(jnp.int32)
    return jnp.where(keep_row == 1, routes_row * capacity + rank, -2)


def unpacked(pair):
    values = pair[...].astype(f32)
    lanes = values.shape[1] - LANES
    upper = jnp.where(iota((1, lanes), 1) < lanes - HEAD_SIZE, values[:, :lanes], 0.0)
    lower = pltpu.roll(values[:, LANES:], lanes - HEAD_SIZE, 1)
    lower = jnp.where(iota((1, lanes), 1) < lanes - HEAD_SIZE, lower, 0.0)
    return jnp.concatenate([upper, lower], axis=0)


def heads_of(own, other, place):
    own = unpacked(own)
    other = unpacked(other)
    first = jnp.where(place == 0, own, other)
    second = jnp.where(place == 0, other, own)
    return jnp.concatenate(join(first, second), axis=1).astype(bf16)


def to_experts(experts, capacity, count, *refs):
    (meta, x_own, cotangent, o_own, o_tp, o_ctx, o_far, wo_own, wo_tp, wo_ctx, wo_far) = refs[:11]
    (extras, gains, routes_row, keep_row, slot_h, slot_d) = refs[11:17]
    middle_out, sends, wo_out, wo_other = refs[17:]
    routes_column, keep_column = columns_of(routes_row, keep_row)
    extras = extras[:, extras.shape[1] - LANES :]
    place, start = meta[0], meta[2]
    interleave(wo_out, slice(None), wo_own, wo_ctx, start, count)
    interleave(wo_other, slice(None), wo_tp, wo_far, start, count)
    branch = mm_nt(heads_of(o_own, o_ctx, place), wo_out[...])
    branch = branch + mm_nt(heads_of(o_tp, o_far, place), wo_other[...])
    middle = x_own[...].astype(f32) + branch
    middle_out[...] = middle
    hidden = (middle * rms_scale(middle) * gains[1:2]).astype(bf16)
    _, _, _, gate = routed(hidden, extras, routes_column, keep_column, experts)
    out_grad = (gate * cotangent[...].astype(f32)).astype(bf16)
    slot = slots_by_row(routes_row[...], keep_row[...], experts, capacity)
    pick_h = (slot_h[...] == slot).astype(f32).astype(bf16)
    pick_d = (slot_d[...] == slot).astype(f32).astype(bf16)
    sends[...] = (mm(pick_h, hidden) + mm(pick_d, out_grad)).astype(bf16)


def gelu_both(value):
    scale = 0.7978845608028654
    cubic = 0.044715
    square = value * value
    inner = jnp.tanh(scale * value * (1.0 + cubic * square))
    half = 0.5 * (1.0 + inner)
    slope = half + 0.5 * value * (1.0 - inner * inner) * scale * (1.0 + 3.0 * cubic * square)
    return value * half, slope


def expert_kernel(owners, kinds_rows, chunks, group_owners, *refs):
    (rows_in, base_column, base_row, w_in, w_out) = refs[:5]
    (out, x_out, dy_out, act_out, dpre_out, acc_y, acc_x, full) = refs[5:]
    piece = pl.program_id(0)
    chunk = pl.program_id(1)
    pieces = pl.num_programs(0)
    capacity = kinds_rows
    per_owner = rows_in.shape[0] // owners
    span = group_owners * per_owner
    half = group_owners * capacity
    groups = owners // group_owners

    @pl.when(chunk == 0)
    def _():
        pick = (base_column[...] + piece * capacity == iota((2 * half, span), 1)).astype(f32).astype(bf16)
        for group in range(groups):
            got = mm(pick, rows_in[group * span : (group + 1) * span, :]).astype(bf16)
            x_out[0, group * half : (group + 1) * half, :] = got[:half]
            dy_out[0, group * half : (group + 1) * half, :] = got[half:]
        acc_y[...] = jnp.zeros_like(acc_y)
        acc_x[...] = jnp.zeros_like(acc_x)

    pre = mm(x_out[0], w_in[0])
    act, slope = gelu_both(pre)
    act = act.astype(bf16)
    act_out[0] = act
    acc_y[...] += mm(act, w_out[0])
    dpre = (mm_nt(dy_out[0], w_out[0]) * slope).astype(bf16)
    dpre_out[0] = dpre
    acc_x[...] += mm_nt(dpre, w_in[0])

    @pl.when(chunk == chunks - 1)
    def _():
        pick = (base_row[...] + piece * capacity == iota((span, 2 * half), 0)).astype(f32).astype(bf16)
        for group in range(groups):
            here = slice(group * half, (group + 1) * half)
            both = jnp.concatenate([acc_y[here].astype(bf16), acc_x[here].astype(bf16)], axis=0)
            part = mm(pick, both)
            there = slice(group * span, (group + 1) * span)
            full[there] = jnp.where(piece == 0, part, full[there] + part)

    @pl.when((chunk == chunks - 1) & (piece == pieces - 1))
    def _():
        width = out.shape[2]
        shares = out.shape[0] // owners
        for owner in range(owners):
            for share in range(shares):
                out[owner * shares + share] = full[
                    owner * per_owner : (owner + 1) * per_owner, share * width : (share + 1) * width
                ].astype(bf16)


def weight_grads(x_rows, dpre, act, dy):
    w_in_grad = jnp.einsum("lrd,lrf->ldf", x_rows, dpre, preferred_element_type=f32)
    w_out_grad = jnp.einsum("lrf,lrd->lfd", act, dy, preferred_element_type=f32)
    return w_in_grad, w_out_grad


def from_experts(experts, capacity, *refs):
    meta, rows_in, cotangent, routes_row, keep_row, slot_y, slot_x, y_out, dx_out, gate_out = refs
    slot = column_of(slots_by_row(routes_row[...], keep_row[...], experts, capacity).astype(f32))
    slot = slot.astype(jnp.int32)
    width = rows_in.shape[1]
    pick_y = (slot == slot_y[...]).astype(f32).astype(bf16)
    pick_x = (slot == slot_x[...]).astype(f32).astype(bf16)
    dx_out[...] = mm(pick_x, rows_in[...]).astype(bf16)
    picked = mm(pick_y, rows_in[...]).astype(bf16)
    y_out[...] = picked
    upstream = jnp.where(meta[1] == 0, cotangent[:, :width], cotangent[:, width:])
    part = jnp.sum(upstream.astype(f32) * picked.astype(f32), axis=1, keepdims=True)
    gate_out[...] = jnp.broadcast_to(part, (part.shape[0], LANES)).T[:8]


def add_expert(meta, middle, gate, y_own, y_tp, result):
    width = y_own.shape[1]
    share = meta[1]
    own, other = y_own[...].astype(f32), y_tp[...].astype(f32)
    gates = gate[:, :1]
    result[:, :width] = middle[:, :width] + gates * jnp.where(share == 0, own, other)
    result[:, width:] = middle[:, width:] + gates * jnp.where(share == 0, other, own)


def middle_backward(experts, *refs):
    (meta, dx_own, dx_tp, part_own, part_tp, middle_ref, cotangent, extras) = refs[:8]
    (gains, routes_row, keep_row) = refs[8:11]
    (dmiddle_out, branch_grad, router_grad, gate_out) = refs[11:]
    routes_column, keep_column = columns_of(routes_row, keep_row)
    extras = extras[:, extras.shape[1] - LANES :]
    share = meta[1]
    own, other = dx_own[...].astype(f32), dx_tp[...].astype(f32)
    slot_grad = jnp.concatenate(
        [jnp.where(share == 0, own, other), jnp.where(share == 0, other, own)], axis=1
    )
    middle = middle_ref[...]
    scale = rms_scale(middle)
    normed = middle * scale
    gain = gains[1:2]
    hidden = (normed * gain).astype(bf16)
    probs, onehot, kept, gate = routed(hidden, extras, routes_column, keep_column, experts)
    gate_out[...] = jnp.broadcast_to(gate, gate_out.shape)
    upstream = cotangent[...].astype(f32)
    gate_grad = column_of(part_own[0:1, :] + part_tp[0:1, :])
    prob_grad = jnp.where(onehot, gate_grad * kept, 0.0)
    logit_grad = (
        probs * (prob_grad - jnp.sum(probs * prob_grad, axis=1, keepdims=True))
    ).astype(bf16)
    hidden_grad = slot_grad + mm_nt(logit_grad, extras)
    gain_grad = column_of(jnp.sum(hidden_grad * normed, axis=0, keepdims=True))
    lane = iota((1, LANES), 1)
    router_grad[...] = jnp.where(
        lane == HEAD_SIZE + experts, gain_grad, mm_tn(hidden, logit_grad)
    ).astype(bf16)
    grad = hidden_grad * gain
    dmiddle = upstream + scale * (grad - normed * jnp.mean(grad * normed, axis=1, keepdims=True))
    dmiddle_out[...] = dmiddle
    branch_grad[...] = dmiddle.astype(bf16)


def attention_backward(heads, buckets, shard, *refs):
    (meta, x_own, x_other, h1, q_in, k_in, v_in, probs, db) = refs[:9]
    (o_all, wo_ref, wall, router_grad) = refs[9:13]
    (payload, top_out, bottom_out, dh1_own, dh1_other) = refs[13:18]
    (sums, do_all, dq, dk, dv, dqkv, dh1) = refs[18:]
    place = meta[0]
    rows = x_own.shape[0]
    group = 2 * rows
    lanes = q_in.shape[1]
    own_at = pl.ds(pl.multiple_of(place * rows, 16), rows)
    other_at = pl.ds(pl.multiple_of((1 - place) * rows, 16), rows)
    both = mm(db[...], wo_ref[...])
    high = pltpu.roll(both[:, LANES : LANES + lanes], lanes - HEAD_SIZE, 1)
    do_all[...] = jnp.where(place == 0, both[:, :lanes], high).astype(bf16)
    blocks = group // STRIP
    sums[...] = jnp.zeros_like(sums)
    keys = k_in[...]
    values = v_in[...]
    ahead = [jnp.zeros((STRIP, STRIP), f32) for _ in range(heads)]
    behind = [jnp.zeros((STRIP, STRIP), f32) for _ in range(heads)]
    for block in range(blocks):
        at = slice(block * STRIP, (block + 1) * STRIP)
        dq_total = jnp.zeros((STRIP, lanes), f32)
        for head in range(heads):
            query = pick_head(q_in[at, :], head, lanes)
            chances = probs[head, at, :]
            grad = pick_head(do_all[at, :], head, lanes)
            chance_grad = mm_nt(grad, values)
            mean = jnp.sum(chances * chance_grad, axis=1, keepdims=True)
            score_grad = (chances * (chance_grad - mean)).astype(bf16)
            dv_part = mm_tn(chances.astype(bf16), grad)
            dk_part = mm_tn(score_grad, query)
            if block == 0 and head == 0:
                dv[...] = dv_part
                dk[...] = dk_part
            else:
                dv[...] += dv_part
                dk[...] += dk_part
            dq_total = dq_total + mm(score_grad, pick_head(keys, head, lanes))
            rounded = score_grad.astype(f32)
            for other in range(blocks):
                gap = other - block
                part = rounded[:, other * STRIP : (other + 1) * STRIP]
                if abs(gap) <= 1:
                    sums[head, :, (gap + 2) * STRIP : (gap + 3) * STRIP] += part
                elif gap > 0:
                    ahead[head] = ahead[head] + part
                else:
                    behind[head] = behind[head] + part
        dq[at, :] = dq_total
    half = HEAD_SIZE
    dqkv[:, :LANES] = dq[:, :LANES].astype(bf16)
    shifted = pltpu.roll(dk[...], half, 1)
    dqkv[:, LANES : 2 * LANES] = (dq[:, LANES:] + shifted[:, :LANES]).astype(bf16)
    dqkv[:, 2 * LANES : 3 * LANES] = shifted[:, LANES:].astype(bf16)
    dqkv[:, 3 * LANES :] = dv[...].astype(bf16)
    dh1[...] = mm_nt(dqkv[...], wall[...])
    gain_part = None
    for source, at, target in ((x_own, own_at, dh1_own), (x_other, other_at, dh1_other)):
        values = source[...].astype(f32)
        grad = dh1[at, :]
        target[...] = grad.astype(bf16)
        part = jnp.sum(grad * (values * rms_scale(values)), axis=0, keepdims=True)
        gain_part = part if gain_part is None else gain_part + part
    spread = skew(sums[...].reshape(heads * STRIP, 4 * STRIP), False)
    diagonals = jnp.sum(spread.reshape(heads, STRIP, 4 * STRIP), axis=1)
    picks = (bucket_index(iota((4 * STRIP, 1), 0) - 2 * STRIP) == iota((1, LANES), 1)).astype(f32)
    in_buckets = jnp.dot(diagonals, picks, precision=highest, preferred_element_type=f32)
    lane = iota((1, LANES), 1)
    row = lax.rem(iota((wall.shape[0], 1), 0), shard)
    riders = jnp.where(lane == HEAD_SIZE, column_of(gain_part), 0.0)
    for head in range(heads):
        line = in_buckets[head : head + 1]
        line = line + jnp.where(lane == buckets - 1, jnp.sum(ahead[head]), 0.0)
        line = line + jnp.where(lane == buckets // 2 - 1, jnp.sum(behind[head]), 0.0)
        riders = riders + jnp.where(row == head, pltpu.roll(line, HEAD_SIZE + 1, 1), 0.0)
    width = wall.shape[1]
    grads = mm_tn(h1[...], dqkv[...])
    payload[:, : width - LANES] = grads[:, : width - LANES].astype(bf16)
    payload[:, width - LANES : width] = (grads[:, width - LANES :] + riders).astype(bf16)
    grads = mm_tn(db[...], o_all[...])
    payload[:, width : width + lanes - LANES] = grads[:, : lanes - LANES].astype(bf16)
    payload[:, width + lanes - LANES :] = (
        grads[:, lanes - LANES :] + router_grad[...].astype(f32)
    ).astype(bf16)
    half = top_out.shape[0]
    across = pl.multiple_of(meta[3] * shard if 2 * half == shard else 0 * meta[3], 16)
    top_out[...] = payload[pl.ds(across, half), :]
    bottom_out[...] = payload[pl.ds(across + half, half), :]


def ring_add(places, right_mine, left_mine, from_left, from_right, right_out, left_out):
    rows = right_mine.shape[0]
    span = from_left.shape[0]
    right_out[...] = right_mine[...]
    left_out[...] = left_mine[...]
    top, bottom = slice(0, span), slice(rows - span, rows)
    right_out[top] = (right_mine[top].astype(f32) + from_left[...].astype(f32)).astype(bf16)
    left_out[bottom] = (left_mine[bottom].astype(f32) + from_right[...].astype(f32)).astype(bf16)


def ring_end(at, place, sums, own, send, table, riders_own, riders_other):
    rows = own.shape[0]
    first, second = sums[:rows, :], sums[rows : 2 * rows, :]
    mine = jnp.where(place == 0, first, second)
    other = jnp.where(place == 0, second, first)
    own[...] = mine
    send[:rows, :] = other
    send[rows:, :] = sums[:8, :]
    table[...] = sums[:8, at : at + LANES]
    riders_own[...] = mine[:, at : at + LANES]
    riders_other[...] = other[:, at : at + LANES]


def ring_last(at, places, mine, from_left, from_right, own, send, table, riders_own, riders_other):
    total = mine[...].astype(f32) + from_left[...].astype(f32) + from_right[...].astype(f32)
    ring_end(at, places[0], total, own, send, table, riders_own, riders_other)


def ring_whole(at, places, sums, own, send, table, riders_own, riders_other):
    ring_end(at, places[0], sums[...], own, send, table, riders_own, riders_other)


def shards_of_sums(experts, buckets, heads, *refs):
    (meta, own_ref, other, own_top, from_tp, from_far) = refs[:6]
    (query_out, key_out, value_out, output_out, router_out, gain_one, gain_two, table) = refs[6:]
    place = meta[0]
    rows, width = query_out.shape[0], query_out.shape[1] // 2
    lanes = width + HEAD_SIZE
    wide = 3 * width + HEAD_SIZE
    own = own_ref[...]
    more = other[:rows, :]
    lane = iota((1, lanes), 1)
    for at, moved, out in (
        (0, False, query_out),
        (LANES, True, key_out),
        (2 * width, False, value_out),
        (wide, False, output_out),
    ):
        parts = [values[:, at : at + lanes] for values in (own, more)]
        if moved:
            parts = [pltpu.roll(part, lanes - HEAD_SIZE, 1) for part in parts]
        parts = [jnp.where(lane < width, part, 0.0) for part in parts]
        first = jnp.where(place == 0, parts[0], parts[1])
        second = jnp.where(place == 0, parts[1], parts[0])
        for index, block in enumerate(join(first, second)):
            out[:, index * LANES : (index + 1) * LANES] = block
    total = (own + more)[:, wide + lanes - LANES :].T
    router_out[...] = total[HEAD_SIZE : HEAD_SIZE + experts, :]
    gain_two[...] = total[HEAD_SIZE + experts : HEAD_SIZE + experts + 1, :]
    line = (own + more)[:, wide - LANES : wide] + (from_tp[...] + from_far[...])
    gain_one[...] = line.T[HEAD_SIZE : HEAD_SIZE + 1, :]
    own_lines = own_top[...]
    other_lines = other[rows : rows + 8, wide - LANES : wide]
    own_lines = pltpu.roll(own_lines, LANES - HEAD_SIZE - 1, 1)
    other_lines = pltpu.roll(other_lines, LANES - HEAD_SIZE - 1, 1)
    table[:heads, :] = jnp.where(place == 0, own_lines, other_lines)[:heads, :buckets]
    table[heads : 2 * heads, :] = jnp.where(place == 0, other_lines, own_lines)[:heads, :buckets]


def input_backward(x_own, dmiddle, gains, near, far, out):
    values = x_own[...].astype(f32)
    scale = rms_scale(values)
    normed = values * scale
    grad = (near[...].astype(f32) + far[...].astype(f32)) * gains[0:1]
    out[...] = dmiddle[...] + scale * (
        grad - normed * jnp.mean(grad * normed, axis=1, keepdims=True)
    )


def swap(value, axis):
    return lax.ppermute(value, axis, [(0, 1), (1, 0)])


def ring_order(count):
    return list(range(0, count, 2)) + list(range(count - 1, 0, -2))


def ring_steps(count):
    order = ring_order(count)
    right = [(order[i], order[(i + 1) % count]) for i in range(count)]
    return order, right, [(b, a) for a, b in right]


def device_table(fsdp_count, ctx_count, tp_count, aligned):
    order = ring_order(fsdp_count)
    rows = []
    for place in range(fsdp_count):
        spot = order.index(place)
        at = lambda distance: order[(spot + distance) % fsdp_count]
        half = fsdp_count // 2
        ring = [place]
        for step in range(1, half):
            ring += [at(-step), at(step)]
        ring.append(at(half))
        for step in range(half, 0, -1):
            ring += [at(step - 1), at(1 - step)]
        for core in range(ctx_count):
            for share in range(tp_count):
                rows.append([core, share, core if aligned else 0, at(half)] + (ring if aligned else []))
    return np.array(rows, np.int32)


def ring_gather(shard, count):
    _, right, left = ring_steps(count)
    shards = [shard]
    going_right, going_left = shard, shard
    for step in range(1, count // 2):
        going_right = lax.ppermute(going_right, "fsdp", right)
        going_left = lax.ppermute(going_left, "fsdp", left)
        shards += [going_right, going_left]
    shards.append(lax.ppermute(going_right, "fsdp", right))
    return shards


def ring_sums(payload, top, bottom, count, at, meta, side):
    rows = payload.shape[0] // count
    lanes = payload.shape[1]
    half = rows // 2
    outs = [
        shape((half, lanes), f32),
        shape((half + 8, lanes), f32),
        shape((8, LANES), f32),
        shape((half, LANES), f32),
        shape((half, LANES), f32),
    ]
    if rows % 32 or count % 2:
        sums = lax.psum_scatter(payload.astype(f32), "fsdp", scatter_dimension=0, tiled=True)
        return kernel_call(functools.partial(ring_whole, at), outs, [smem, vmem])(meta, sums)
    _, right, left = ring_steps(count)
    going_right, going_left = top, bottom
    spec = lambda which: pl.BlockSpec((rows, lanes), lambda i, places: (places[which], 0))
    params = pltpu.CompilerParams(vmem_limit_bytes=8 * MIB)
    for step in range(count // 2, 0, -1):
        from_left = lax.ppermute(going_right, "fsdp", right)
        from_right = lax.ppermute(going_left, "fsdp", left)
        which = 4 + count + 2 * (count // 2 - step)
        whole = lambda dims: pl.BlockSpec(dims, lambda i, places: (0, 0))
        last = step == 1
        if last:
            side, from_left, from_right = lax.optimization_barrier((side, from_left, from_right))
        step_outs = outs if last else [shape((rows, lanes), bf16)] * 2
        out = pl.pallas_call(
            functools.partial(ring_last, at) if last else ring_add,
            grid_spec=pltpu.PrefetchScalarGridSpec(
                num_scalar_prefetch=1,
                grid=(1,),
                in_specs=([spec(which)] if last else [spec(which), spec(which + 1)])
                + [whole(from_left.shape), whole(from_right.shape)],
                out_specs=[whole(o.shape) for o in step_outs],
            ),
            out_shape=step_outs,
            compiler_params=params,
            cost_estimate=pl.CostEstimate(flops=0, bytes_accessed=1024 * 1024, transcendentals=0),
        )(meta, *([payload] if last else [payload, payload]), from_left, from_right)
        if last:
            return out
        going_right, going_left = out


def body(
    tokens,
    cotangent,
    w_query,
    w_key,
    w_value,
    w_output,
    w_router,
    gain_attn,
    gain_moe,
    rel_table,
    w_in,
    w_out,
    lengths,
    routes,
    keep_mask,
):
    rows, model_width = tokens.shape
    fsdp_count = lax.axis_size("fsdp")
    owners = lax.axis_size(("fsdp", "ctx"))
    tp_count = lax.axis_size("tp")
    place = lax.axis_index("ctx")
    share = lax.axis_index("tp")
    fsdp_place = lax.axis_index("fsdp")
    group = 2 * rows
    experts = w_router.shape[1]
    capacity = max(2, (5 * rows + 4 * experts - 1) // (4 * experts))
    pieces = w_in.shape[0]
    split_count = owners * pieces // experts
    hidden_width = w_in.shape[2]
    heads = rel_table.shape[1] // 2
    heads_all = heads * 2 * tp_count
    width = heads * HEAD_SIZE
    lanes = width + HEAD_SIZE
    shard_rows = w_query.shape[0]
    buckets = rel_table.shape[0]

    def full(dims, dtype):
        return shape(dims, dtype)

    wide = 3 * width + HEAD_SIZE
    aligned = shard_rows % 16 == 0 and fsdp_count % 2 == 0
    count = fsdp_count if aligned else 1
    table = jnp.asarray(device_table(fsdp_count, 2, tp_count, aligned))
    device = lax.axis_index(("fsdp", "ctx", "tp"))
    meta = lax.dynamic_slice(table, (device, 0), (1, table.shape[1])).reshape(-1)
    shard_own, shard_send, wo_shard = kernel_call(
        pack_rows,
        [full((shard_rows, wide), bf16), full((shard_rows, wide), bf16), full((2 * shard_rows, lanes), bf16)],
        [smem] + [vmem] * 7,
        moved=512 * 1024,
        mib=60,
    )(meta, w_query, w_key, w_value, w_output, w_router.T, gain_attn[None, :], gain_moe[None, :])
    shard_other = swap(shard_send, "ctx")
    shard = jnp.concatenate(
        [jnp.concatenate([shard_own, shard_other], axis=0), wo_shard], axis=1
    )
    x_other = swap(tokens, "ctx")

    def ordered(own, other):
        if aligned:
            return own, other
        dims = (fsdp_count, 1, shard_rows, own.shape[1])
        pair = in_order(own.reshape(dims), other.reshape(dims), 1).reshape(2 * own.shape[0], -1)
        return pair[: own.shape[0]], pair[own.shape[0] :]

    def in_order(own, other, axis):
        return jnp.where(
            place == 0,
            jnp.concatenate([own, other], axis=axis),
            jnp.concatenate([other, own], axis=axis),
        )

    strips, far, segment = kernel_call(
        functools.partial(attention_tables, heads),
        [
            full((heads, STRIP, 3 * STRIP), f32),
            full((8, LANES), f32),
            full((8, group), jnp.int32),
        ],
        [smem] * 3,
        moved=1024 * 1024,
        mib=8,
    )(meta, lengths, rel_table.T)
    if aligned:
        shards = ring_gather(shard, fsdp_count)
        wall, wo_own = kernel_call(
            functools.partial(put_in_rows, len(shards)),
            [full((model_width, wide), bf16), full((model_width // 2, 2 * width), bf16)],
            [smem] + [vmem] * len(shards),
            moved=4 * 1024 * 1024,
        )(meta, *shards)
    else:
        both = lax.all_gather(shard, "fsdp", axis=0, tiled=False)
        upper, lower = both[:, :shard_rows], both[:, shard_rows:]
        wall = jnp.concatenate(
            ordered(upper[:, :, :wide].reshape(-1, wide), lower[:, :, :wide].reshape(-1, wide)), axis=0
        )
        wo_own = jnp.concatenate([upper[:, :, wide : wide + width], lower[:, :, wide : wide + width]], axis=2)
        wo_own = wo_own.reshape(-1, 2 * width)

    h1, q, k, v, o_own, o_other, o_all, probs, gains = kernel_call(
        functools.partial(attention_forward, heads, experts),
        [
            full((group, model_width), bf16),
            full((group, lanes), bf16),
            full((group, lanes), bf16),
            full((group, lanes), bf16),
            full((rows // 2, 2 * width), bf16),
            full((rows // 2, 2 * width), bf16),
            full((group, lanes), bf16),
            full((heads, group, group), f32),
            full((8, model_width), f32),
        ],
        [smem] + [vmem] * 6,
        flops=2 * group * model_width * wide * 8,
        moved=8 * 1024 * 1024,
    )(meta, tokens, x_other, wall, strips, far, segment)
    wo_tp = swap(wo_own, "tp")
    wo_ctx = swap(wo_own, "ctx")
    wo_tp, gains = lax.optimization_barrier((wo_tp, gains))
    wo_far = swap(wo_tp, "ctx")
    wo_own, wo_ctx = ordered(wo_own, wo_ctx)
    wo_tp, wo_far = ordered(wo_tp, wo_far)

    o_tp = swap(o_own, "tp")
    o_ctx = swap(o_other, "ctx")
    o_far = lax.ppermute(o_other, ("ctx", "tp"), [(i, 3 - i) for i in range(4)])

    per_owner = 2 * pieces * capacity
    owner_of = np.repeat(np.arange(owners), per_owner)
    inside = np.tile(np.arange(per_owner), owners)
    kind = inside // (pieces * capacity)
    piece_of = owner_of * pieces + (inside // capacity) % pieces
    slot_of = (piece_of // split_count) * capacity + inside % capacity
    slot_first = np.where(kind == 0, slot_of, -1).astype(np.int32)
    slot_second = np.where(kind == 1, slot_of, -1).astype(np.int32)
    routes_row = routes.reshape(1, rows)
    keep_row = keep_mask.reshape(1, rows)

    middle, sends, wo_full = kernel_call(
        functools.partial(to_experts, experts, capacity, count),
        [
            full((rows, model_width), f32),
            full((owners * per_owner, model_width), bf16),
            full((model_width, 2 * width), bf16),
        ],
        [smem] + [vmem] * 16,
        scratch=[pltpu.VMEM((model_width, 2 * width), bf16)],
        flops=2 * rows * model_width * (model_width + 2 * owners * per_owner),
        moved=6 * 1024 * 1024,
    )(
        meta, tokens, cotangent, o_own, o_tp, o_ctx, o_far, wo_own, wo_tp, wo_ctx, wo_far, wall,
        gains, routes_row, keep_row, slot_first[:, None], slot_second[:, None],
    )

    arrived = lax.all_to_all(
        sends.reshape(owners, per_owner, model_width),
        ("fsdp", "ctx"),
        split_axis=0,
        concat_axis=0,
        tiled=True,
    ).reshape(owners * per_owner, model_width)

    group_owners = min(16, owners)
    half = group_owners * capacity
    spot = np.arange(2 * half) % half
    base = (
        (spot // capacity) * per_owner
        + (np.arange(2 * half) // half) * pieces * capacity
        + spot % capacity
    ).astype(np.int32)
    chunk_width = 768 if hidden_width % 768 == 0 else hidden_width
    chunks = hidden_width // chunk_width
    slot_rows = owners * capacity
    part_width = model_width // tp_count
    whole = lambda *dims: pl.BlockSpec(dims, lambda i, j: (0,) * len(dims))
    outgoing, x_rows, dy_rows, act, dpre = kernel_call(
        functools.partial(expert_kernel, owners, capacity, chunks, group_owners),
        [
            full((owners * tp_count, per_owner, part_width), bf16),
            full((pieces, slot_rows, model_width), bf16),
            full((pieces, slot_rows, model_width), bf16),
            full((pieces, slot_rows, hidden_width), bf16),
            full((pieces, slot_rows, hidden_width), bf16),
        ],
        [
            whole(owners * per_owner, model_width),
            whole(2 * half, 1),
            whole(1, 2 * half),
            pl.BlockSpec((1, model_width, chunk_width), lambda i, j: (i, 0, j)),
            pl.BlockSpec((1, chunk_width, model_width), lambda i, j: (i, j, 0)),
        ],
        out_specs=[
            whole(owners * tp_count, per_owner, part_width),
            pl.BlockSpec((1, slot_rows, model_width), lambda i, j: (i, 0, 0)),
            pl.BlockSpec((1, slot_rows, model_width), lambda i, j: (i, 0, 0)),
            pl.BlockSpec((1, slot_rows, chunk_width), lambda i, j: (i, 0, j)),
            pl.BlockSpec((1, slot_rows, chunk_width), lambda i, j: (i, 0, j)),
        ],
        scratch=[
            pltpu.VMEM((slot_rows, model_width), f32),
            pltpu.VMEM((slot_rows, model_width), f32),
            pltpu.VMEM((owners * per_owner, model_width), f32),
        ],
        grid=(pieces, chunks),
        mib=24,
        flops=8 * pieces * slot_rows * model_width * hidden_width,
        moved=12 * 1024 * 1024,
    )(arrived, base[:, None], base[None, :], w_in, w_out)

    returned = lax.all_to_all(
        outgoing, ("fsdp", "ctx", "tp"), split_axis=0, concat_axis=0, tiled=True
    ).reshape(owners * tp_count * per_owner, part_width)
    w_in_grad, w_out_grad = weight_grads(x_rows, dpre, act, dy_rows)
    returned, w_in_grad, w_out_grad = lax.optimization_barrier((returned, w_in_grad, w_out_grad))

    back_first = np.repeat(slot_first.reshape(owners, 1, per_owner), tp_count, axis=1).reshape(1, -1)
    back_second = np.repeat(slot_second.reshape(owners, 1, per_owner), tp_count, axis=1).reshape(1, -1)
    y_own, dx_own, part_own = kernel_call(
        functools.partial(from_experts, experts, capacity),
        [
            full((rows, part_width), bf16),
            full((rows, part_width), bf16),
            full((8, rows), f32),
        ],
        [smem] + [vmem] * 6,
        flops=4 * rows * returned.shape[0] * part_width,
        moved=2 * 1024 * 1024,
    )(meta, returned, cotangent, routes_row, keep_row, back_first, back_second)
    dx_tp = swap(dx_own, "tp")
    part_tp = swap(part_own, "tp")

    middle_grad, db_own, router_grad, gate = kernel_call(
        functools.partial(middle_backward, experts),
        [
            full((rows, model_width), f32),
            full((rows, model_width), bf16),
            full((model_width, LANES), bf16),
            full((rows, LANES), f32),
        ],
        [smem] + [vmem] * 10,
        flops=6 * rows * LANES * model_width,
        moved=6 * 1024 * 1024,
    )(meta, dx_own, dx_tp, part_own, part_tp, middle, cotangent, wall, gains, routes_row, keep_row)
    y_own, gate = lax.optimization_barrier((y_own, gate))
    y_tp = swap(y_own, "tp")
    result = kernel_call(
        add_expert,
        [full((rows, model_width), f32)],
        [smem] + [vmem] * 4,
        moved=4 * 1024 * 1024,
    )(meta, middle, gate, y_own, y_tp)[0]
    db = lax.all_gather(db_own, "ctx", axis=0, tiled=True)

    half = model_width // fsdp_count // 2
    payload, top, bottom, dh1_own, dh1_other = kernel_call(
        functools.partial(attention_backward, heads, buckets, model_width // fsdp_count),
        [
            full((model_width, wide + lanes), bf16),
            full((half if aligned else 16, wide + lanes), bf16),
            full((half if aligned else 16, wide + lanes), bf16),
            full((rows, model_width), bf16),
            full((rows, model_width), bf16),
        ],
        [smem] + [vmem] * 12,
        scratch=[
            pltpu.VMEM((heads, STRIP, 4 * STRIP), f32),
            pltpu.VMEM((group, lanes), bf16),
            pltpu.VMEM((group, lanes), f32),
            pltpu.VMEM((group, lanes), f32),
            pltpu.VMEM((group, lanes), f32),
            pltpu.VMEM((group, wide), bf16),
            pltpu.VMEM((group, model_width), f32),
        ],
        flops=2 * group * model_width * wide * 12,
        mib=20,
        moved=8 * 1024 * 1024,
    )(
        meta, tokens, x_other, h1, q, k, v, probs, db, o_all, wo_full, wall, router_grad,
    )

    dh1_sum = (dh1_own.astype(f32) + swap(dh1_other, "ctx").astype(f32)).astype(bf16)
    dh1_far = swap(dh1_sum, "tp")
    own, send, own_lines, riders_own, riders_other = ring_sums(
        payload, top, bottom, fsdp_count, wide - LANES, meta, dh1_far
    )
    other = swap(send, "ctx")
    from_tp = swap(riders_own, "tp")
    from_far = lax.ppermute(riders_other, ("ctx", "tp"), [(i, 3 - i) for i in range(4)])
    input_grad = kernel_call(
        input_backward,
        [full((rows, model_width), f32)],
        [vmem] * 5,
        moved=4 * 1024 * 1024,
    )(tokens, middle_grad, gains, dh1_sum, dh1_far)[0]
    other, input_grad, result = lax.optimization_barrier((other, input_grad, result))

    shard = full((shard_rows, 2 * width), f32)
    query_grad, key_grad, value_grad, output_grad, router_sum, gain_one, gain_two, table_grad = kernel_call(
        functools.partial(shards_of_sums, experts, buckets, heads),
        [shard] * 4
        + [
            full((experts, shard_rows), f32),
            full((1, shard_rows), f32),
            full((1, shard_rows), f32),
            full((2 * heads, buckets), f32),
        ],
        [smem] + [vmem] * 5,
        moved=1024 * 1024,
    )(meta, own, other, own_lines, from_tp, from_far)
    return (
        result,
        input_grad,
        query_grad,
        key_grad,
        value_grad,
        output_grad,
        router_sum.T,
        gain_one.reshape(shard_rows),
        gain_two.reshape(shard_rows),
        table_grad.T,
        w_in_grad,
        w_out_grad,
    )


def solution(mesh):
    in_specs = (
        P(("fsdp", "ctx"), None),
        P(("fsdp", "ctx"), None),
        P(("fsdp", "ctx"), "tp"),
        P(("fsdp", "ctx"), "tp"),
        P(("fsdp", "ctx"), "tp"),
        P(("fsdp", "ctx"), "tp"),
        P(("fsdp", "ctx"), None),
        P(("fsdp", "ctx")),
        P(("fsdp", "ctx")),
        P(None, "tp"),
        P(("fsdp", "ctx"), None, "tp"),
        P(("fsdp", "ctx"), "tp", None),
        P("fsdp", None),
        P(("fsdp", "ctx"), None),
        P(("fsdp", "ctx")),
    )
    out_specs = (
        P(("fsdp", "ctx"), None),
        P(("fsdp", "ctx"), None),
        P(("fsdp", "ctx"), "tp"),
        P(("fsdp", "ctx"), "tp"),
        P(("fsdp", "ctx"), "tp"),
        P(("fsdp", "ctx"), "tp"),
        P(("fsdp", "ctx"), None),
        P(("fsdp", "ctx")),
        P(("fsdp", "ctx")),
        P(None, "tp"),
        P(("fsdp", "ctx"), None, "tp"),
        P(("fsdp", "ctx"), "tp", None),
    )
    return jax.shard_map(body, mesh=mesh, in_specs=in_specs, out_specs=out_specs, check_vma=False)
```

```python
import functools

import jax
import jax.numpy as jnp
import numpy as np
from jax import lax
from jax.experimental import pallas as pl
from jax.experimental.pallas import tpu as pltpu
from jax.sharding import PartitionSpec as P

epsilon = 1e-06
masked_value = -1e30
bucket_edges = (12, 16, 23, 32, 46, 64, 91)
highest = lax.Precision.HIGHEST
LANES = 128
STRIP = 128
HEAD_SIZE = 64
MIB = 1024 * 1024
f32 = jnp.float32
bf16 = jnp.bfloat16
vmem = pl.BlockSpec(memory_space=pltpu.VMEM)
smem = pl.BlockSpec(memory_space=pltpu.SMEM)


def mm(left, right):
    return jnp.dot(left, right, preferred_element_type=f32)


def mm_nt(left, right):
    return lax.dot_general(left, right, (((1,), (1,)), ((), ())), preferred_element_type=f32)


def mm_tn(left, right):
    return lax.dot_general(left, right, (((0,), (0,)), ((), ())), preferred_element_type=f32)


def rms_scale(values):
    return lax.rsqrt(jnp.mean(values * values, axis=-1, keepdims=True) + epsilon)


def iota(shape, dim):
    return lax.broadcasted_iota(jnp.int32, shape, dim)


def bucket_index(offset):
    side = jnp.where(offset > 0, 16, 0).astype(jnp.int32)
    distance = jnp.abs(offset)
    far_bucket = 8 + sum(((distance >= edge).astype(jnp.int32) for edge in bucket_edges))
    return side + jnp.where(distance < 8, distance, far_bucket)


def kernel_call(body, outs, in_specs, out_specs=None, scratch=(), grid=None, flops=0, moved=0, mib=16):
    extra = {} if grid is None else {"grid": grid}
    return pl.pallas_call(
        body,
        out_shape=outs,
        in_specs=in_specs,
        out_specs=[vmem] * len(outs) if out_specs is None else out_specs,
        scratch_shapes=list(scratch),
        compiler_params=pltpu.CompilerParams(vmem_limit_bytes=mib * MIB),
        cost_estimate=pl.CostEstimate(flops=flops, bytes_accessed=moved, transcendentals=0),
        **extra,
    )


def shape(dims, dtype):
    return jax.ShapeDtypeStruct(tuple(dims), dtype)


def segments(lengths_ref, columns, rows):
    places = iota((rows, columns), 1)
    total = jnp.zeros((rows, columns), jnp.int32)
    end = 0
    for entry in range(lengths_ref.shape[1]):
        end = end + lengths_ref[0, entry]
        total = total + (places >= end).astype(jnp.int32)
    return total


def column_of(line):
    return jnp.broadcast_to(line, (LANES, line.shape[1])).T[:, :1]


def skew(values, right):
    rows, lanes = values.shape
    row = lax.rem(iota((rows, 1), 0), STRIP)
    step = 1
    while step < STRIP:
        moved = pltpu.roll(values, step if right else lanes - step, 1)
        values = jnp.where((row & step) > 0, moved, values)
        step *= 2
    return values


def attention_tables(heads, meta, lengths, table, strips, far, segment):
    lanes = 4 * STRIP
    buckets = table.shape[1]
    first_head = meta[0] * heads
    bucket = bucket_index(iota((1, lanes), 1) - 2 * STRIP)
    far[...] = jnp.zeros_like(far)
    for head in range(heads):
        line = jnp.zeros((1, lanes), f32)
        for entry in range(buckets):
            line = jnp.where(bucket == entry, table[first_head + head, entry], line)
        strip = skew(jnp.broadcast_to(line, (STRIP, lanes)), True)
        strips[head] = strip[:, STRIP:]
        far[2 * head : 2 * head + 1, :] = jnp.full((1, LANES), table[first_head + head, buckets - 1], f32)
        far[2 * head + 1 : 2 * head + 2, :] = jnp.full(
            (1, LANES), table[first_head + head, buckets // 2 - 1], f32
        )
    segment[...] = segments(lengths, segment.shape[1], segment.shape[0])


def bias_row(strips, far, head, block, blocks):
    parts = []
    for other in range(blocks):
        gap = other - block
        if abs(gap) <= 1:
            parts.append(strips[head, :, (gap + 1) * STRIP : (gap + 2) * STRIP])
        else:
            row = 2 * head + (0 if gap > 0 else 1)
            parts.append(jnp.broadcast_to(far[row : row + 1, :], (STRIP, STRIP)))
    return jnp.concatenate(parts, axis=1)


def head_mask(head, lanes):
    lane = iota((1, lanes), 1)
    return (lane >= head * HEAD_SIZE) & (lane < (head + 1) * HEAD_SIZE)


def pick_head(values, head, lanes):
    return jnp.where(head_mask(head, lanes), values, 0.0).astype(bf16)


def half_columns(weight, which):
    values = weight[...].astype(f32)
    width = values.shape[1] // 2
    lanes = width + HEAD_SIZE
    high = pltpu.roll(values[:, LANES : LANES + lanes], lanes - HEAD_SIZE, 1)
    picked = jnp.where(which == 0, values[:, :lanes], high)
    return jnp.where(iota((1, lanes), 1) < width, picked, 0.0)


def join(first, second):
    moved = pltpu.roll(second, HEAD_SIZE, 1)
    return first[:, :LANES], first[:, LANES:] + moved[:, :LANES], moved[:, LANES:]


def pack_rows(*refs):
    (meta, w_query, w_key, w_value, w_output, w_router, gain_one, gain_two, own, send, output) = refs
    rows = w_query.shape[0]
    experts = w_router.shape[0]
    width = w_query.shape[1] // 2
    lanes = width + HEAD_SIZE
    lane = iota((1, lanes), 1)
    diagonal = iota((rows, rows), 0) == iota((rows, rows), 1)
    placing = (iota((experts, lanes), 0) + width == iota((experts, lanes), 1)).astype(f32)
    extras = mm_tn(w_router[...], placing.astype(bf16))
    for index, gain in enumerate((gain_one, gain_two)):
        column = jnp.sum(
            jnp.where(diagonal, jnp.broadcast_to(gain[...].astype(f32), (rows, rows)), 0.0),
            axis=1,
            keepdims=True,
        )
        extras = extras + jnp.where(lane == width + experts + index, column, 0.0)
    for which, out in ((meta[0], own), (1 - meta[0], send)):
        at = 0
        for block in join(half_columns(w_query, which), half_columns(w_key, which)):
            out[:, at : at + LANES] = block.astype(bf16)
            at += LANES
        out[:, at:] = (half_columns(w_value, which) + extras).astype(bf16)
    output[:rows, :] = half_columns(w_output, 0).astype(bf16)
    output[rows:, :] = half_columns(w_output, 1).astype(bf16)


def put_in_rows(count, *refs):
    meta = refs[0]
    shards = refs[1 : 1 + count]
    wall, output = refs[1 + count :]
    wide = wall.shape[1]
    place = meta[0]
    for index, shard in enumerate(shards):
        rows = shard.shape[0] // 2
        first = meta[4 + index]
        for half, core in ((0, place), (1, 1 - place)):
            at = pl.multiple_of((2 * first + core) * rows, 16)
            wall[pl.ds(at, rows), :] = shard[half * rows : (half + 1) * rows, :wide]
        blocks = join(shard[:rows, wide:].astype(f32), shard[rows:, wide:].astype(f32))
        at = pl.multiple_of(first * rows, 16)
        for block, values in enumerate(blocks):
            output[pl.ds(at, rows), block * LANES : (block + 1) * LANES] = values.astype(bf16)


def interleave(out, lanes, own, other, place, count):
    rows = own.shape[0] // count
    for index in range(count):
        here = slice(index * rows, (index + 1) * rows)
        first = pl.multiple_of((2 * index + place) * rows, 16)
        second = pl.multiple_of((2 * index + 1 - place) * rows, 16)
        out[pl.ds(first, rows), lanes] = own[here, :]
        out[pl.ds(second, rows), lanes] = other[here, :]


def attention_forward(heads, experts, *refs):
    (meta, x_own, x_other, wall, strips, far, segment) = refs[:7]
    (h1, q_out, k_out, v_out, o_own, o_other, o_all, probs, gains) = refs[7:]
    place = meta[0]
    rows = x_own.shape[0]
    group = 2 * rows
    width = wall.shape[1]
    extras = wall[:, width - LANES :].astype(f32).T
    gain_at = HEAD_SIZE + experts
    gains[...] = extras[gain_at : gain_at + 8]
    gain_one = gains[0:1]
    for source, start in ((x_own, place * rows), (x_other, (1 - place) * rows)):
        values = source[...].astype(f32)
        h1[pl.ds(pl.multiple_of(start, 16), rows), :] = (
            values * rms_scale(values) * gain_one
        ).astype(bf16)
    qkv = mm(h1[...], wall[...])
    lanes = q_out.shape[1]
    q_out[...] = qkv[:, :lanes].astype(bf16)
    k_out[...] = pltpu.roll(qkv[:, LANES : LANES + lanes], lanes - HEAD_SIZE, 1).astype(bf16)
    v_out[...] = qkv[:, width - lanes :].astype(bf16)
    segment_row = segment[0:1, :]
    segment_column = column_of(segment_row.astype(f32)).astype(jnp.int32)
    keys = k_out[...]
    blocks = group // STRIP
    values_of = [pick_head(v_out[...], head, lanes) for head in range(heads)]
    for block in range(blocks):
        first = block * STRIP
        same = segment_column[first : first + STRIP] == segment_row
        total = jnp.zeros((STRIP, lanes), f32)
        for head in range(heads):
            query = pick_head(q_out[first : first + STRIP, :], head, lanes)
            scores = mm_nt(query, keys) + bias_row(strips, far, head, block, blocks)
            scores = jnp.where(same, scores, masked_value)
            top = jnp.max(scores, axis=1, keepdims=True)
            raised = jnp.exp(scores - top)
            mass = jnp.sum(raised, axis=1, keepdims=True)
            chances = raised * (1.0 / mass)
            probs[head, first : first + STRIP, :] = chances
            total = total + mm(chances.astype(bf16), values_of[head])
        o_all[first : first + STRIP, :] = total.astype(bf16)
    for out, start in ((o_own, place * rows), (o_other, (1 - place) * rows)):
        values = o_all[pl.ds(pl.multiple_of(start, 16), rows), :].astype(f32)
        for index, part in enumerate(join(values[: rows // 2], values[rows // 2 :])):
            out[:, index * LANES : (index + 1) * LANES] = part.astype(bf16)


def columns_of(*lines):
    return [column_of(line[...].astype(f32)).astype(jnp.int32) for line in lines]


def routed(hidden, extras, routes_column, keep_column, experts):
    logits = mm(hidden, extras)
    lane = iota((1, LANES), 1) - HEAD_SIZE
    valid = (lane >= 0) & (lane < experts)
    logits = jnp.where(valid, logits, masked_value)
    raised = jnp.where(valid, jnp.exp(logits - jnp.max(logits, axis=1, keepdims=True)), 0.0)
    probs = raised / jnp.sum(raised, axis=1, keepdims=True)
    onehot = lane == routes_column
    kept = keep_column.astype(f32)
    gate = jnp.sum(jnp.where(onehot, probs, 0.0), axis=1, keepdims=True) * kept
    return probs, onehot, kept, gate


def slots_by_row(routes_row, keep_row, experts, capacity):
    count = routes_row.shape[1]
    chosen = ((iota((experts, count), 0) == routes_row) & (keep_row == 1)).astype(f32)
    before = (iota((count, count), 0) < iota((count, count), 1)).astype(bf16)
    earlier = mm(chosen.astype(bf16), before)
    rank = jnp.sum(earlier * chosen, axis=0, keepdims=True).astype(jnp.int32)
    return jnp.where(keep_row == 1, routes_row * capacity + rank, -2)


def unpacked(pair):
    values = pair[...].astype(f32)
    lanes = values.shape[1] - LANES
    upper = jnp.where(iota((1, lanes), 1) < lanes - HEAD_SIZE, values[:, :lanes], 0.0)
    lower = pltpu.roll(values[:, LANES:], lanes - HEAD_SIZE, 1)
    lower = jnp.where(iota((1, lanes), 1) < lanes - HEAD_SIZE, lower, 0.0)
    return jnp.concatenate([upper, lower], axis=0)


def heads_of(own, other, place):
    own = unpacked(own)
    other = unpacked(other)
    first = jnp.where(place == 0, own, other)
    second = jnp.where(place == 0, other, own)
    return jnp.concatenate(join(first, second), axis=1).astype(bf16)


def to_experts(experts, capacity, count, *refs):
    (meta, x_own, cotangent, o_own, o_tp, o_ctx, o_far, wo_own, wo_tp, wo_ctx, wo_far) = refs[:11]
    (extras, gains, routes_row, keep_row, slot_h, slot_d) = refs[11:17]
    middle_out, sends, wo_out, wo_other = refs[17:]
    routes_column, keep_column = columns_of(routes_row, keep_row)
    extras = extras[:, extras.shape[1] - LANES :]
    place, start = meta[0], meta[2]
    interleave(wo_out, slice(None), wo_own, wo_ctx, start, count)
    interleave(wo_other, slice(None), wo_tp, wo_far, start, count)
    branch = mm_nt(heads_of(o_own, o_ctx, place), wo_out[...])
    branch = branch + mm_nt(heads_of(o_tp, o_far, place), wo_other[...])
    middle = x_own[...].astype(f32) + branch
    middle_out[...] = middle
    hidden = (middle * rms_scale(middle) * gains[1:2]).astype(bf16)
    _, _, _, gate = routed(hidden, extras, routes_column, keep_column, experts)
    out_grad = (gate * cotangent[...].astype(f32)).astype(bf16)
    slot = slots_by_row(routes_row[...], keep_row[...], experts, capacity)
    pick_h = (slot_h[...] == slot).astype(f32).astype(bf16)
    pick_d = (slot_d[...] == slot).astype(f32).astype(bf16)
    sends[...] = (mm(pick_h, hidden) + mm(pick_d, out_grad)).astype(bf16)


def gelu_both(value):
    scale = 0.7978845608028654
    cubic = 0.044715
    square = value * value
    inner = jnp.tanh(scale * value * (1.0 + cubic * square))
    half = 0.5 * (1.0 + inner)
    slope = half + 0.5 * value * (1.0 - inner * inner) * scale * (1.0 + 3.0 * cubic * square)
    return value * half, slope


def expert_kernel(owners, kinds_rows, chunks, group_owners, *refs):
    (rows_in, base_column, base_row, w_in, w_out) = refs[:5]
    (out, x_out, dy_out, act_out, dpre_out, acc_y, acc_x, full) = refs[5:]
    piece = pl.program_id(0)
    chunk = pl.program_id(1)
    pieces = pl.num_programs(0)
    capacity = kinds_rows
    per_owner = rows_in.shape[0] // owners
    span = group_owners * per_owner
    half = group_owners * capacity
    groups = owners // group_owners

    @pl.when(chunk == 0)
    def _():
        pick = (base_column[...] + piece * capacity == iota((2 * half, span), 1)).astype(f32).astype(bf16)
        for group in range(groups):
            got = mm(pick, rows_in[group * span : (group + 1) * span, :]).astype(bf16)
            x_out[0, group * half : (group + 1) * half, :] = got[:half]
            dy_out[0, group * half : (group + 1) * half, :] = got[half:]
        acc_y[...] = jnp.zeros_like(acc_y)
        acc_x[...] = jnp.zeros_like(acc_x)

    pre = mm(x_out[0], w_in[0])
    act, slope = gelu_both(pre)
    act = act.astype(bf16)
    act_out[0] = act
    acc_y[...] += mm(act, w_out[0])
    dpre = (mm_nt(dy_out[0], w_out[0]) * slope).astype(bf16)
    dpre_out[0] = dpre
    acc_x[...] += mm_nt(dpre, w_in[0])

    @pl.when(chunk == chunks - 1)
    def _():
        pick = (base_row[...] + piece * capacity == iota((span, 2 * half), 0)).astype(f32).astype(bf16)
        for group in range(groups):
            here = slice(group * half, (group + 1) * half)
            both = jnp.concatenate([acc_y[here].astype(bf16), acc_x[here].astype(bf16)], axis=0)
            part = mm(pick, both)
            there = slice(group * span, (group + 1) * span)
            full[there] = jnp.where(piece == 0, part, full[there] + part)

    @pl.when((chunk == chunks - 1) & (piece == pieces - 1))
    def _():
        width = out.shape[2]
        shares = out.shape[0] // owners
        for owner in range(owners):
            for share in range(shares):
                out[owner * shares + share] = full[
                    owner * per_owner : (owner + 1) * per_owner, share * width : (share + 1) * width
                ].astype(bf16)


def expert_grads(x_rows, dpre, act, dy, w_in_grad, w_out_grad):
    w_in_grad[0] = mm_tn(x_rows[0], dpre[0])
    w_out_grad[0] = mm_tn(act[0], dy[0])


def from_experts(experts, capacity, *refs):
    meta, rows_in, cotangent, routes_row, keep_row, slot_y, slot_x, y_out, dx_out, gate_out = refs
    slot = column_of(slots_by_row(routes_row[...], keep_row[...], experts, capacity).astype(f32))
    slot = slot.astype(jnp.int32)
    width = rows_in.shape[1]
    pick_y = (slot == slot_y[...]).astype(f32).astype(bf16)
    pick_x = (slot == slot_x[...]).astype(f32).astype(bf16)
    dx_out[...] = mm(pick_x, rows_in[...]).astype(bf16)
    picked = mm(pick_y, rows_in[...]).astype(bf16)
    y_out[...] = picked
    upstream = jnp.where(meta[1] == 0, cotangent[:, :width], cotangent[:, width:])
    part = jnp.sum(upstream.astype(f32) * picked.astype(f32), axis=1, keepdims=True)
    gate_out[...] = jnp.broadcast_to(part, (part.shape[0], LANES)).T[:8]


def add_expert(meta, middle, gate, y_own, y_tp, result):
    width = y_own.shape[1]
    share = meta[1]
    own, other = y_own[...].astype(f32), y_tp[...].astype(f32)
    gates = gate[:, :1]
    result[:, :width] = middle[:, :width] + gates * jnp.where(share == 0, own, other)
    result[:, width:] = middle[:, width:] + gates * jnp.where(share == 0, other, own)


def middle_backward(experts, *refs):
    (meta, dx_own, dx_tp, part_own, part_tp, middle_ref, cotangent, extras) = refs[:8]
    (gains, routes_row, keep_row) = refs[8:11]
    (dmiddle_out, branch_grad, router_grad, gate_out) = refs[11:]
    routes_column, keep_column = columns_of(routes_row, keep_row)
    extras = extras[:, extras.shape[1] - LANES :]
    share = meta[1]
    own, other = dx_own[...].astype(f32), dx_tp[...].astype(f32)
    slot_grad = jnp.concatenate(
        [jnp.where(share == 0, own, other), jnp.where(share == 0, other, own)], axis=1
    )
    middle = middle_ref[...]
    scale = rms_scale(middle)
    normed = middle * scale
    gain = gains[1:2]
    hidden = (normed * gain).astype(bf16)
    probs, onehot, kept, gate = routed(hidden, extras, routes_column, keep_column, experts)
    gate_out[...] = jnp.broadcast_to(gate, gate_out.shape)
    upstream = cotangent[...].astype(f32)
    gate_grad = column_of(part_own[0:1, :] + part_tp[0:1, :])
    prob_grad = jnp.where(onehot, gate_grad * kept, 0.0)
    logit_grad = (
        probs * (prob_grad - jnp.sum(probs * prob_grad, axis=1, keepdims=True))
    ).astype(bf16)
    hidden_grad = slot_grad + mm_nt(logit_grad, extras)
    gain_grad = column_of(jnp.sum(hidden_grad * normed, axis=0, keepdims=True))
    lane = iota((1, LANES), 1)
    router_grad[...] = jnp.where(
        lane == HEAD_SIZE + experts, gain_grad, mm_tn(hidden, logit_grad)
    ).astype(bf16)
    grad = hidden_grad * gain
    dmiddle = upstream + scale * (grad - normed * jnp.mean(grad * normed, axis=1, keepdims=True))
    dmiddle_out[...] = dmiddle
    branch_grad[...] = dmiddle.astype(bf16)


def attention_backward(heads, buckets, shard, *refs):
    (meta, x_own, x_other, h1, q_in, k_in, v_in, probs, db) = refs[:9]
    (o_all, wo_ref, wall, router_grad) = refs[9:13]
    (payload, top_out, bottom_out, dh1_own, dh1_other) = refs[13:18]
    (sums, do_all, dq, dk, dv, dqkv, dh1) = refs[18:]
    place = meta[0]
    rows = x_own.shape[0]
    group = 2 * rows
    lanes = q_in.shape[1]
    own_at = pl.ds(pl.multiple_of(place * rows, 16), rows)
    other_at = pl.ds(pl.multiple_of((1 - place) * rows, 16), rows)
    both = mm(db[...], wo_ref[...])
    high = pltpu.roll(both[:, LANES : LANES + lanes], lanes - HEAD_SIZE, 1)
    do_all[...] = jnp.where(place == 0, both[:, :lanes], high).astype(bf16)
    blocks = group // STRIP
    sums[...] = jnp.zeros_like(sums)
    keys = k_in[...]
    values = v_in[...]
    ahead = [jnp.zeros((STRIP, STRIP), f32) for _ in range(heads)]
    behind = [jnp.zeros((STRIP, STRIP), f32) for _ in range(heads)]
    for block in range(blocks):
        at = slice(block * STRIP, (block + 1) * STRIP)
        dq_total = jnp.zeros((STRIP, lanes), f32)
        for head in range(heads):
            query = pick_head(q_in[at, :], head, lanes)
            chances = probs[head, at, :]
            grad = pick_head(do_all[at, :], head, lanes)
            chance_grad = mm_nt(grad, values)
            mean = jnp.sum(chances * chance_grad, axis=1, keepdims=True)
            score_grad = (chances * (chance_grad - mean)).astype(bf16)
            dv_part = mm_tn(chances.astype(bf16), grad)
            dk_part = mm_tn(score_grad, query)
            if block == 0 and head == 0:
                dv[...] = dv_part
                dk[...] = dk_part
            else:
                dv[...] += dv_part
                dk[...] += dk_part
            dq_total = dq_total + mm(score_grad, pick_head(keys, head, lanes))
            rounded = score_grad.astype(f32)
            for other in range(blocks):
                gap = other - block
                part = rounded[:, other * STRIP : (other + 1) * STRIP]
                if abs(gap) <= 1:
                    sums[head, :, (gap + 2) * STRIP : (gap + 3) * STRIP] += part
                elif gap > 0:
                    ahead[head] = ahead[head] + part
                else:
                    behind[head] = behind[head] + part
        dq[at, :] = dq_total
    half = HEAD_SIZE
    dqkv[:, :LANES] = dq[:, :LANES].astype(bf16)
    shifted = pltpu.roll(dk[...], half, 1)
    dqkv[:, LANES : 2 * LANES] = (dq[:, LANES:] + shifted[:, :LANES]).astype(bf16)
    dqkv[:, 2 * LANES : 3 * LANES] = shifted[:, LANES:].astype(bf16)
    dqkv[:, 3 * LANES :] = dv[...].astype(bf16)
    dh1[...] = mm_nt(dqkv[...], wall[...])
    gain_part = None
    for source, at, target in ((x_own, own_at, dh1_own), (x_other, other_at, dh1_other)):
        values = source[...].astype(f32)
        grad = dh1[at, :]
        target[...] = grad.astype(bf16)
        part = jnp.sum(grad * (values * rms_scale(values)), axis=0, keepdims=True)
        gain_part = part if gain_part is None else gain_part + part
    spread = skew(sums[...].reshape(heads * STRIP, 4 * STRIP), False)
    diagonals = jnp.sum(spread.reshape(heads, STRIP, 4 * STRIP), axis=1)
    picks = (bucket_index(iota((4 * STRIP, 1), 0) - 2 * STRIP) == iota((1, LANES), 1)).astype(f32)
    in_buckets = jnp.dot(diagonals, picks, precision=highest, preferred_element_type=f32)
    lane = iota((1, LANES), 1)
    row = lax.rem(iota((wall.shape[0], 1), 0), shard)
    riders = jnp.where(lane == HEAD_SIZE, column_of(gain_part), 0.0)
    for head in range(heads):
        line = in_buckets[head : head + 1]
        line = line + jnp.where(lane == buckets - 1, jnp.sum(ahead[head]), 0.0)
        line = line + jnp.where(lane == buckets // 2 - 1, jnp.sum(behind[head]), 0.0)
        riders = riders + jnp.where(row == head, pltpu.roll(line, HEAD_SIZE + 1, 1), 0.0)
    width = wall.shape[1]
    grads = mm_tn(h1[...], dqkv[...])
    payload[:, : width - LANES] = grads[:, : width - LANES].astype(bf16)
    payload[:, width - LANES : width] = (grads[:, width - LANES :] + riders).astype(bf16)
    grads = mm_tn(db[...], o_all[...])
    payload[:, width : width + lanes - LANES] = grads[:, : lanes - LANES].astype(bf16)
    payload[:, width + lanes - LANES :] = (
        grads[:, lanes - LANES :] + router_grad[...].astype(f32)
    ).astype(bf16)
    half = top_out.shape[0]
    across = pl.multiple_of(meta[3] * shard if 2 * half == shard else 0 * meta[3], 16)
    top_out[...] = payload[pl.ds(across, half), :]
    bottom_out[...] = payload[pl.ds(across + half, half), :]


def ring_add(places, right_mine, left_mine, from_left, from_right, right_out, left_out):
    rows = right_mine.shape[0]
    span = from_left.shape[0]
    right_out[...] = right_mine[...]
    left_out[...] = left_mine[...]
    top, bottom = slice(0, span), slice(rows - span, rows)
    right_out[top] = (right_mine[top].astype(f32) + from_left[...].astype(f32)).astype(bf16)
    left_out[bottom] = (left_mine[bottom].astype(f32) + from_right[...].astype(f32)).astype(bf16)


def ring_end(at, place, sums, own, send, table, riders_own, riders_other):
    rows = own.shape[0]
    first, second = sums[:rows, :], sums[rows : 2 * rows, :]
    mine = jnp.where(place == 0, first, second)
    other = jnp.where(place == 0, second, first)
    own[...] = mine
    send[:rows, :] = other
    send[rows:, :] = sums[:8, :]
    table[...] = sums[:8, at : at + LANES]
    riders_own[...] = mine[:, at : at + LANES]
    riders_other[...] = other[:, at : at + LANES]


def ring_last(at, places, mine, from_left, from_right, own, send, table, riders_own, riders_other):
    total = mine[...].astype(f32) + from_left[...].astype(f32) + from_right[...].astype(f32)
    ring_end(at, places[0], total, own, send, table, riders_own, riders_other)


def ring_whole(at, places, sums, own, send, table, riders_own, riders_other):
    ring_end(at, places[0], sums[...], own, send, table, riders_own, riders_other)


def shards_of_sums(experts, buckets, heads, *refs):
    (meta, own_ref, other, own_top, from_tp, from_far) = refs[:6]
    (query_out, key_out, value_out, output_out, router_out, gain_one, gain_two, table) = refs[6:]
    place = meta[0]
    rows, width = query_out.shape[0], query_out.shape[1] // 2
    lanes = width + HEAD_SIZE
    wide = 3 * width + HEAD_SIZE
    own = own_ref[...]
    more = other[:rows, :]
    lane = iota((1, lanes), 1)
    for at, moved, out in (
        (0, False, query_out),
        (LANES, True, key_out),
        (2 * width, False, value_out),
        (wide, False, output_out),
    ):
        parts = [values[:, at : at + lanes] for values in (own, more)]
        if moved:
            parts = [pltpu.roll(part, lanes - HEAD_SIZE, 1) for part in parts]
        parts = [jnp.where(lane < width, part, 0.0) for part in parts]
        first = jnp.where(place == 0, parts[0], parts[1])
        second = jnp.where(place == 0, parts[1], parts[0])
        for index, block in enumerate(join(first, second)):
            out[:, index * LANES : (index + 1) * LANES] = block
    total = (own + more)[:, wide + lanes - LANES :].T
    router_out[...] = total[HEAD_SIZE : HEAD_SIZE + experts, :]
    gain_two[...] = total[HEAD_SIZE + experts : HEAD_SIZE + experts + 1, :]
    line = (own + more)[:, wide - LANES : wide] + (from_tp[...] + from_far[...])
    gain_one[...] = line.T[HEAD_SIZE : HEAD_SIZE + 1, :]
    own_lines = own_top[...]
    other_lines = other[rows : rows + 8, wide - LANES : wide]
    own_lines = pltpu.roll(own_lines, LANES - HEAD_SIZE - 1, 1)
    other_lines = pltpu.roll(other_lines, LANES - HEAD_SIZE - 1, 1)
    table[:heads, :] = jnp.where(place == 0, own_lines, other_lines)[:heads, :buckets]
    table[heads : 2 * heads, :] = jnp.where(place == 0, other_lines, own_lines)[:heads, :buckets]


def input_backward(x_own, dmiddle, gains, near, far, out):
    values = x_own[...].astype(f32)
    scale = rms_scale(values)
    normed = values * scale
    grad = (near[...].astype(f32) + far[...].astype(f32)) * gains[0:1]
    out[...] = dmiddle[...] + scale * (
        grad - normed * jnp.mean(grad * normed, axis=1, keepdims=True)
    )


def swap(value, axis):
    return lax.ppermute(value, axis, [(0, 1), (1, 0)])


def ring_order(count):
    return list(range(0, count, 2)) + list(range(count - 1, 0, -2))


def ring_steps(count):
    order = ring_order(count)
    right = [(order[i], order[(i + 1) % count]) for i in range(count)]
    return order, right, [(b, a) for a, b in right]


def device_table(fsdp_count, ctx_count, tp_count, aligned):
    order = ring_order(fsdp_count)
    rows = []
    for place in range(fsdp_count):
        spot = order.index(place)
        at = lambda distance: order[(spot + distance) % fsdp_count]
        half = fsdp_count // 2
        ring = [place]
        for step in range(1, half):
            ring += [at(-step), at(step)]
        ring.append(at(half))
        for step in range(half, 0, -1):
            ring += [at(step - 1), at(1 - step)]
        for core in range(ctx_count):
            for share in range(tp_count):
                rows.append([core, share, core if aligned else 0, at(half)] + (ring if aligned else []))
    return np.array(rows, np.int32)


def ring_gather(shard, count, side):
    _, right, left = ring_steps(count)
    shards = [shard]
    going_right, going_left = shard, shard
    for step in range(1, count // 2):
        going_right = lax.ppermute(going_right, "fsdp", right)
        going_left = lax.ppermute(going_left, "fsdp", left)
        if step == 1:
            going_right, going_left, side = lax.optimization_barrier((going_right, going_left, side))
        shards += [going_right, going_left]
    shards.append(lax.ppermute(going_right, "fsdp", right))
    return shards, side


def ring_sums(payload, top, bottom, count, at, meta, sides):
    rows = payload.shape[0] // count
    lanes = payload.shape[1]
    half = rows // 2
    outs = [
        shape((half, lanes), f32),
        shape((half + 8, lanes), f32),
        shape((8, LANES), f32),
        shape((half, LANES), f32),
        shape((half, LANES), f32),
    ]
    if rows % 32 or count % 2:
        sums = lax.psum_scatter(payload.astype(f32), "fsdp", scatter_dimension=0, tiled=True)
        return kernel_call(functools.partial(ring_whole, at), outs, [smem, vmem])(meta, sums)
    _, right, left = ring_steps(count)
    going_right, going_left = top, bottom
    spec = lambda which: pl.BlockSpec((rows, lanes), lambda i, places: (places[which], 0))
    params = pltpu.CompilerParams(vmem_limit_bytes=8 * MIB)
    for step in range(count // 2, 0, -1):
        from_left = lax.ppermute(going_right, "fsdp", right)
        from_right = lax.ppermute(going_left, "fsdp", left)
        if step in sides:
            from_left, from_right, _ = lax.optimization_barrier((from_left, from_right, sides[step]))
        which = 4 + count + 2 * (count // 2 - step)
        whole = lambda dims: pl.BlockSpec(dims, lambda i, places: (0, 0))
        last = step == 1
        step_outs = outs if last else [shape((rows, lanes), bf16)] * 2
        out = pl.pallas_call(
            functools.partial(ring_last, at) if last else ring_add,
            grid_spec=pltpu.PrefetchScalarGridSpec(
                num_scalar_prefetch=1,
                grid=(1,),
                in_specs=([spec(which)] if last else [spec(which), spec(which + 1)])
                + [whole(from_left.shape), whole(from_right.shape)],
                out_specs=[whole(o.shape) for o in step_outs],
            ),
            out_shape=step_outs,
            compiler_params=params,
            cost_estimate=pl.CostEstimate(flops=0, bytes_accessed=1024 * 1024, transcendentals=0),
        )(meta, *([payload] if last else [payload, payload]), from_left, from_right)
        if last:
            return out
        going_right, going_left = out


def body(
    tokens,
    cotangent,
    w_query,
    w_key,
    w_value,
    w_output,
    w_router,
    gain_attn,
    gain_moe,
    rel_table,
    w_in,
    w_out,
    lengths,
    routes,
    keep_mask,
):
    rows, model_width = tokens.shape
    fsdp_count = lax.axis_size("fsdp")
    owners = lax.axis_size(("fsdp", "ctx"))
    tp_count = lax.axis_size("tp")
    place = lax.axis_index("ctx")
    share = lax.axis_index("tp")
    fsdp_place = lax.axis_index("fsdp")
    group = 2 * rows
    experts = w_router.shape[1]
    capacity = max(2, (5 * rows + 4 * experts - 1) // (4 * experts))
    pieces = w_in.shape[0]
    split_count = owners * pieces // experts
    hidden_width = w_in.shape[2]
    heads = rel_table.shape[1] // 2
    heads_all = heads * 2 * tp_count
    width = heads * HEAD_SIZE
    lanes = width + HEAD_SIZE
    shard_rows = w_query.shape[0]
    buckets = rel_table.shape[0]

    def full(dims, dtype):
        return shape(dims, dtype)

    wide = 3 * width + HEAD_SIZE
    aligned = shard_rows % 16 == 0 and fsdp_count % 2 == 0
    count = fsdp_count if aligned else 1
    table = jnp.asarray(device_table(fsdp_count, 2, tp_count, aligned))
    device = lax.axis_index(("fsdp", "ctx", "tp"))
    meta = lax.dynamic_slice(table, (device, 0), (1, table.shape[1])).reshape(-1)
    shard_own, shard_send, wo_shard = kernel_call(
        pack_rows,
        [full((shard_rows, wide), bf16), full((shard_rows, wide), bf16), full((2 * shard_rows, lanes), bf16)],
        [smem] + [vmem] * 7,
        moved=512 * 1024,
        mib=60,
    )(meta, w_query, w_key, w_value, w_output, w_router.T, gain_attn[None, :], gain_moe[None, :])
    shard_other = swap(shard_send, "ctx")
    shard = jnp.concatenate(
        [jnp.concatenate([shard_own, shard_other], axis=0), wo_shard], axis=1
    )
    x_other = swap(tokens, "ctx")

    def ordered(own, other):
        if aligned:
            return own, other
        dims = (fsdp_count, 1, shard_rows, own.shape[1])
        pair = in_order(own.reshape(dims), other.reshape(dims), 1).reshape(2 * own.shape[0], -1)
        return pair[: own.shape[0]], pair[own.shape[0] :]

    def in_order(own, other, axis):
        return jnp.where(
            place == 0,
            jnp.concatenate([own, other], axis=axis),
            jnp.concatenate([other, own], axis=axis),
        )

    strips, far, segment = kernel_call(
        functools.partial(attention_tables, heads),
        [
            full((heads, STRIP, 3 * STRIP), f32),
            full((8, LANES), f32),
            full((8, group), jnp.int32),
        ],
        [smem] * 3,
        moved=1024 * 1024,
        mib=8,
    )(meta, lengths, rel_table.T)
    if aligned:
        shards, (strips, far, segment) = ring_gather(shard, fsdp_count, (strips, far, segment))
        wall, wo_own = kernel_call(
            functools.partial(put_in_rows, len(shards)),
            [full((model_width, wide), bf16), full((model_width // 2, 2 * width), bf16)],
            [smem] + [vmem] * len(shards),
            moved=4 * 1024 * 1024,
        )(meta, *shards)
    else:
        both = lax.all_gather(shard, "fsdp", axis=0, tiled=False)
        upper, lower = both[:, :shard_rows], both[:, shard_rows:]
        wall = jnp.concatenate(
            ordered(upper[:, :, :wide].reshape(-1, wide), lower[:, :, :wide].reshape(-1, wide)), axis=0
        )
        wo_own = jnp.concatenate([upper[:, :, wide : wide + width], lower[:, :, wide : wide + width]], axis=2)
        wo_own = wo_own.reshape(-1, 2 * width)

    h1, q, k, v, o_own, o_other, o_all, probs, gains = kernel_call(
        functools.partial(attention_forward, heads, experts),
        [
            full((group, model_width), bf16),
            full((group, lanes), bf16),
            full((group, lanes), bf16),
            full((group, lanes), bf16),
            full((rows // 2, 2 * width), bf16),
            full((rows // 2, 2 * width), bf16),
            full((group, lanes), bf16),
            full((heads, group, group), f32),
            full((8, model_width), f32),
        ],
        [smem] + [vmem] * 6,
        flops=2 * group * model_width * wide * 8,
        moved=8 * 1024 * 1024,
    )(meta, tokens, x_other, wall, strips, far, segment)
    wo_tp = swap(wo_own, "tp")
    wo_ctx = swap(wo_own, "ctx")
    wo_tp, gains = lax.optimization_barrier((wo_tp, gains))
    wo_far = swap(wo_tp, "ctx")
    wo_own, wo_ctx = ordered(wo_own, wo_ctx)
    wo_tp, wo_far = ordered(wo_tp, wo_far)

    o_tp = swap(o_own, "tp")
    o_ctx = swap(o_other, "ctx")
    o_far = lax.ppermute(o_other, ("ctx", "tp"), [(i, 3 - i) for i in range(4)])

    per_owner = 2 * pieces * capacity
    owner_of = np.repeat(np.arange(owners), per_owner)
    inside = np.tile(np.arange(per_owner), owners)
    kind = inside // (pieces * capacity)
    piece_of = owner_of * pieces + (inside // capacity) % pieces
    slot_of = (piece_of // split_count) * capacity + inside % capacity
    slot_first = np.where(kind == 0, slot_of, -1).astype(np.int32)
    slot_second = np.where(kind == 1, slot_of, -1).astype(np.int32)
    routes_row = routes.reshape(1, rows)
    keep_row = keep_mask.reshape(1, rows)

    middle, sends, wo_full = kernel_call(
        functools.partial(to_experts, experts, capacity, count),
        [
            full((rows, model_width), f32),
            full((owners * per_owner, model_width), bf16),
            full((model_width, 2 * width), bf16),
        ],
        [smem] + [vmem] * 16,
        scratch=[pltpu.VMEM((model_width, 2 * width), bf16)],
        flops=2 * rows * model_width * (model_width + 2 * owners * per_owner),
        moved=6 * 1024 * 1024,
    )(
        meta, tokens, cotangent, o_own, o_tp, o_ctx, o_far, wo_own, wo_tp, wo_ctx, wo_far, wall,
        gains, routes_row, keep_row, slot_first[:, None], slot_second[:, None],
    )

    arrived = lax.all_to_all(
        sends.reshape(owners, per_owner, model_width),
        ("fsdp", "ctx"),
        split_axis=0,
        concat_axis=0,
        tiled=True,
    ).reshape(owners * per_owner, model_width)

    group_owners = min(16, owners)
    half = group_owners * capacity
    spot = np.arange(2 * half) % half
    base = (
        (spot // capacity) * per_owner
        + (np.arange(2 * half) // half) * pieces * capacity
        + spot % capacity
    ).astype(np.int32)
    chunk_width = 768 if hidden_width % 768 == 0 else hidden_width
    chunks = hidden_width // chunk_width
    slot_rows = owners * capacity
    part_width = model_width // tp_count
    whole = lambda *dims: pl.BlockSpec(dims, lambda i, j: (0,) * len(dims))
    outgoing, x_rows, dy_rows, act, dpre = kernel_call(
        functools.partial(expert_kernel, owners, capacity, chunks, group_owners),
        [
            full((owners * tp_count, per_owner, part_width), bf16),
            full((pieces, slot_rows, model_width), bf16),
            full((pieces, slot_rows, model_width), bf16),
            full((pieces, slot_rows, hidden_width), bf16),
            full((pieces, slot_rows, hidden_width), bf16),
        ],
        [
            whole(owners * per_owner, model_width),
            whole(2 * half, 1),
            whole(1, 2 * half),
            pl.BlockSpec((1, model_width, chunk_width), lambda i, j: (i, 0, j)),
            pl.BlockSpec((1, chunk_width, model_width), lambda i, j: (i, j, 0)),
        ],
        out_specs=[
            whole(owners * tp_count, per_owner, part_width),
            pl.BlockSpec((1, slot_rows, model_width), lambda i, j: (i, 0, 0)),
            pl.BlockSpec((1, slot_rows, model_width), lambda i, j: (i, 0, 0)),
            pl.BlockSpec((1, slot_rows, chunk_width), lambda i, j: (i, 0, j)),
            pl.BlockSpec((1, slot_rows, chunk_width), lambda i, j: (i, 0, j)),
        ],
        scratch=[
            pltpu.VMEM((slot_rows, model_width), f32),
            pltpu.VMEM((slot_rows, model_width), f32),
            pltpu.VMEM((owners * per_owner, model_width), f32),
        ],
        grid=(pieces, chunks),
        mib=24,
        flops=8 * pieces * slot_rows * model_width * hidden_width,
        moved=12 * 1024 * 1024,
    )(arrived, base[:, None], base[None, :], w_in, w_out)

    returned = lax.all_to_all(
        outgoing, ("fsdp", "ctx", "tp"), split_axis=0, concat_axis=0, tiled=True
    ).reshape(owners * tp_count * per_owner, part_width)
    part = 512 if hidden_width % 512 == 0 else hidden_width
    rows_spec = pl.BlockSpec((1, slot_rows, model_width), lambda i, j: (i, 0, 0))
    hidden_spec = pl.BlockSpec((1, slot_rows, part), lambda i, j: (i, 0, j))
    w_in_grad, w_out_grad = kernel_call(
        expert_grads,
        [full(w_in.shape, f32), full(w_out.shape, f32)],
        [rows_spec, hidden_spec, hidden_spec, rows_spec],
        out_specs=[
            pl.BlockSpec((1, model_width, part), lambda i, j: (i, 0, j)),
            pl.BlockSpec((1, part, model_width), lambda i, j: (i, j, 0)),
        ],
        grid=(pieces, hidden_width // part),
        flops=4 * pieces * slot_rows * model_width * hidden_width,
        moved=24 * 1024 * 1024,
        mib=24,
    )(x_rows, dpre, act, dy_rows)
    returned, w_in_grad, w_out_grad = lax.optimization_barrier((returned, w_in_grad, w_out_grad))

    back_first = np.repeat(slot_first.reshape(owners, 1, per_owner), tp_count, axis=1).reshape(1, -1)
    back_second = np.repeat(slot_second.reshape(owners, 1, per_owner), tp_count, axis=1).reshape(1, -1)
    y_own, dx_own, part_own = kernel_call(
        functools.partial(from_experts, experts, capacity),
        [
            full((rows, part_width), bf16),
            full((rows, part_width), bf16),
            full((8, rows), f32),
        ],
        [smem] + [vmem] * 6,
        flops=4 * rows * returned.shape[0] * part_width,
        moved=2 * 1024 * 1024,
    )(meta, returned, cotangent, routes_row, keep_row, back_first, back_second)
    dx_tp = swap(dx_own, "tp")
    part_tp = swap(part_own, "tp")

    middle_grad, db_own, router_grad, gate = kernel_call(
        functools.partial(middle_backward, experts),
        [
            full((rows, model_width), f32),
            full((rows, model_width), bf16),
            full((model_width, LANES), bf16),
            full((rows, LANES), f32),
        ],
        [smem] + [vmem] * 10,
        flops=6 * rows * LANES * model_width,
        moved=6 * 1024 * 1024,
    )(meta, dx_own, dx_tp, part_own, part_tp, middle, cotangent, wall, gains, routes_row, keep_row)
    y_own, gate = lax.optimization_barrier((y_own, gate))
    y_tp = swap(y_own, "tp")
    db = lax.all_gather(db_own, "ctx", axis=0, tiled=True)

    half = model_width // fsdp_count // 2
    payload, top, bottom, dh1_own, dh1_other = kernel_call(
        functools.partial(attention_backward, heads, buckets, model_width // fsdp_count),
        [
            full((model_width, wide + lanes), bf16),
            full((half if aligned else 16, wide + lanes), bf16),
            full((half if aligned else 16, wide + lanes), bf16),
            full((rows, model_width), bf16),
            full((rows, model_width), bf16),
        ],
        [smem] + [vmem] * 12,
        scratch=[
            pltpu.VMEM((heads, STRIP, 4 * STRIP), f32),
            pltpu.VMEM((group, lanes), bf16),
            pltpu.VMEM((group, lanes), f32),
            pltpu.VMEM((group, lanes), f32),
            pltpu.VMEM((group, lanes), f32),
            pltpu.VMEM((group, wide), bf16),
            pltpu.VMEM((group, model_width), f32),
        ],
        flops=2 * group * model_width * wide * 12,
        mib=20,
        moved=8 * 1024 * 1024,
    )(
        meta, tokens, x_other, h1, q, k, v, probs, db, o_all, wo_full, wall, router_grad,
    )

    result = kernel_call(
        add_expert,
        [full((rows, model_width), f32)],
        [smem] + [vmem] * 4,
        moved=4 * 1024 * 1024,
    )(meta, middle, gate, y_own, y_tp)[0]
    dh1_sum = (dh1_own.astype(f32) + swap(dh1_other, "ctx").astype(f32)).astype(bf16)
    dh1_far = swap(dh1_sum, "tp")
    input_grad = kernel_call(
        input_backward,
        [full((rows, model_width), f32)],
        [vmem] * 5,
        moved=4 * 1024 * 1024,
    )(tokens, middle_grad, gains, dh1_sum, dh1_far)[0]
    own, send, own_lines, riders_own, riders_other = ring_sums(
        payload, top, bottom, fsdp_count, wide - LANES, meta, {2: result, 1: input_grad}
    )
    other = swap(send, "ctx")
    from_tp = swap(riders_own, "tp")
    from_far = lax.ppermute(riders_other, ("ctx", "tp"), [(i, 3 - i) for i in range(4)])

    shard = full((shard_rows, 2 * width), f32)
    query_grad, key_grad, value_grad, output_grad, router_sum, gain_one, gain_two, table_grad = kernel_call(
        functools.partial(shards_of_sums, experts, buckets, heads),
        [shard] * 4
        + [
            full((experts, shard_rows), f32),
            full((1, shard_rows), f32),
            full((1, shard_rows), f32),
            full((2 * heads, buckets), f32),
        ],
        [smem] + [vmem] * 5,
        moved=1024 * 1024,
    )(meta, own, other, own_lines, from_tp, from_far)
    return (
        result,
        input_grad,
        query_grad,
        key_grad,
        value_grad,
        output_grad,
        router_sum.T,
        gain_one.reshape(shard_rows),
        gain_two.reshape(shard_rows),
        table_grad.T,
        w_in_grad,
        w_out_grad,
    )


def solution(mesh):
    in_specs = (
        P(("fsdp", "ctx"), None),
        P(("fsdp", "ctx"), None),
        P(("fsdp", "ctx"), "tp"),
        P(("fsdp", "ctx"), "tp"),
        P(("fsdp", "ctx"), "tp"),
        P(("fsdp", "ctx"), "tp"),
        P(("fsdp", "ctx"), None),
        P(("fsdp", "ctx")),
        P(("fsdp", "ctx")),
        P(None, "tp"),
        P(("fsdp", "ctx"), None, "tp"),
        P(("fsdp", "ctx"), "tp", None),
        P("fsdp", None),
        P(("fsdp", "ctx"), None),
        P(("fsdp", "ctx")),
    )
    out_specs = (
        P(("fsdp", "ctx"), None),
        P(("fsdp", "ctx"), None),
        P(("fsdp", "ctx"), "tp"),
        P(("fsdp", "ctx"), "tp"),
        P(("fsdp", "ctx"), "tp"),
        P(("fsdp", "ctx"), "tp"),
        P(("fsdp", "ctx"), None),
        P(("fsdp", "ctx")),
        P(("fsdp", "ctx")),
        P(None, "tp"),
        P(("fsdp", "ctx"), None, "tp"),
        P(("fsdp", "ctx"), "tp", None),
    )
    return jax.shard_map(body, mesh=mesh, in_specs=in_specs, out_specs=out_specs, check_vma=False)
```

```python
import functools

import jax
import jax.numpy as jnp
import numpy as np
from jax import lax
from jax.experimental import pallas as pl
from jax.experimental.pallas import tpu as pltpu
from jax.sharding import PartitionSpec as P

epsilon = 1e-06
masked_value = -1e30
bucket_edges = (12, 16, 23, 32, 46, 64, 91)
highest = lax.Precision.HIGHEST
LANES = 128
STRIP = 128
HEAD_SIZE = 64
MIB = 1024 * 1024
f32 = jnp.float32
bf16 = jnp.bfloat16
vmem = pl.BlockSpec(memory_space=pltpu.VMEM)
smem = pl.BlockSpec(memory_space=pltpu.SMEM)
hbm = pl.BlockSpec(memory_space=pltpu.HBM)


def mm(left, right):
    return jnp.dot(left, right, preferred_element_type=f32)


def mm_nt(left, right):
    return lax.dot_general(left, right, (((1,), (1,)), ((), ())), preferred_element_type=f32)


def mm_tn(left, right):
    return lax.dot_general(left, right, (((0,), (0,)), ((), ())), preferred_element_type=f32)


def rms_scale(values):
    return lax.rsqrt(jnp.mean(values * values, axis=-1, keepdims=True) + epsilon)


def iota(shape, dim):
    return lax.broadcasted_iota(jnp.int32, shape, dim)


def bucket_index(offset):
    side = jnp.where(offset > 0, 16, 0).astype(jnp.int32)
    distance = jnp.abs(offset)
    far_bucket = 8 + sum(((distance >= edge).astype(jnp.int32) for edge in bucket_edges))
    return side + jnp.where(distance < 8, distance, far_bucket)


def kernel_call(body, outs, in_specs, out_specs=None, scratch=(), grid=None, flops=0, moved=0, mib=16):
    extra = {} if grid is None else {"grid": grid}
    return pl.pallas_call(
        body,
        out_shape=outs,
        in_specs=in_specs,
        out_specs=[vmem] * len(outs) if out_specs is None else out_specs,
        scratch_shapes=list(scratch),
        compiler_params=pltpu.CompilerParams(vmem_limit_bytes=mib * MIB),
        cost_estimate=pl.CostEstimate(flops=flops, bytes_accessed=moved, transcendentals=0),
        **extra,
    )


def shape(dims, dtype):
    return jax.ShapeDtypeStruct(tuple(dims), dtype)


def segments(lengths_ref, columns, rows):
    places = iota((rows, columns), 1)
    total = jnp.zeros((rows, columns), jnp.int32)
    end = 0
    for entry in range(lengths_ref.shape[1]):
        end = end + lengths_ref[0, entry]
        total = total + (places >= end).astype(jnp.int32)
    return total


def column_of(line):
    return jnp.broadcast_to(line, (LANES, line.shape[1])).T[:, :1]


def skew(values, right):
    rows, lanes = values.shape
    row = lax.rem(iota((rows, 1), 0), STRIP)
    step = 1
    while step < STRIP:
        moved = pltpu.roll(values, step if right else lanes - step, 1)
        values = jnp.where((row & step) > 0, moved, values)
        step *= 2
    return values


def attention_tables(heads, meta, lengths, table, strips, far, segment):
    lanes = 4 * STRIP
    buckets = table.shape[1]
    first_head = meta[0] * heads
    bucket = bucket_index(iota((1, lanes), 1) - 2 * STRIP)
    far[...] = jnp.zeros_like(far)
    for head in range(heads):
        line = jnp.zeros((1, lanes), f32)
        for entry in range(buckets):
            line = jnp.where(bucket == entry, table[first_head + head, entry], line)
        strip = skew(jnp.broadcast_to(line, (STRIP, lanes)), True)
        strips[head] = strip[:, STRIP:]
        far[2 * head : 2 * head + 1, :] = jnp.full((1, LANES), table[first_head + head, buckets - 1], f32)
        far[2 * head + 1 : 2 * head + 2, :] = jnp.full(
            (1, LANES), table[first_head + head, buckets // 2 - 1], f32
        )
    segment[...] = segments(lengths, segment.shape[1], segment.shape[0])


def bias_row(strips, far, head, block, blocks):
    parts = []
    for other in range(blocks):
        gap = other - block
        if abs(gap) <= 1:
            parts.append(strips[head, :, (gap + 1) * STRIP : (gap + 2) * STRIP])
        else:
            row = 2 * head + (0 if gap > 0 else 1)
            parts.append(jnp.broadcast_to(far[row : row + 1, :], (STRIP, STRIP)))
    return jnp.concatenate(parts, axis=1)


def head_mask(head, lanes):
    lane = iota((1, lanes), 1)
    return (lane >= head * HEAD_SIZE) & (lane < (head + 1) * HEAD_SIZE)


def pick_head(values, head, lanes):
    return jnp.where(head_mask(head, lanes), values, 0.0).astype(bf16)


def half_columns(weight, which):
    values = weight[...].astype(f32)
    width = values.shape[1] // 2
    lanes = width + HEAD_SIZE
    high = pltpu.roll(values[:, LANES : LANES + lanes], lanes - HEAD_SIZE, 1)
    picked = jnp.where(which == 0, values[:, :lanes], high)
    return jnp.where(iota((1, lanes), 1) < width, picked, 0.0)


def join(first, second):
    moved = pltpu.roll(second, HEAD_SIZE, 1)
    return first[:, :LANES], first[:, LANES:] + moved[:, :LANES], moved[:, LANES:]


def pack_rows(*refs):
    (meta, w_query, w_key, w_value, w_output, w_router, gain_one, gain_two, own, send, output) = refs
    rows = w_query.shape[0]
    experts = w_router.shape[0]
    width = w_query.shape[1] // 2
    lanes = width + HEAD_SIZE
    lane = iota((1, lanes), 1)
    diagonal = iota((rows, rows), 0) == iota((rows, rows), 1)
    placing = (iota((experts, lanes), 0) + width == iota((experts, lanes), 1)).astype(f32)
    extras = mm_tn(w_router[...], placing.astype(bf16))
    for index, gain in enumerate((gain_one, gain_two)):
        column = jnp.sum(
            jnp.where(diagonal, jnp.broadcast_to(gain[...].astype(f32), (rows, rows)), 0.0),
            axis=1,
            keepdims=True,
        )
        extras = extras + jnp.where(lane == width + experts + index, column, 0.0)
    for which, out in ((meta[0], own), (1 - meta[0], send)):
        at = 0
        for block in join(half_columns(w_query, which), half_columns(w_key, which)):
            out[:, at : at + LANES] = block.astype(bf16)
            at += LANES
        out[:, at:] = (half_columns(w_value, which) + extras).astype(bf16)
    output[:rows, :] = half_columns(w_output, 0).astype(bf16)
    output[rows:, :] = half_columns(w_output, 1).astype(bf16)


def put_in_rows(count, *refs):
    meta = refs[0]
    shards = refs[1 : 1 + count]
    wall, output = refs[1 + count :]
    wide = wall.shape[1]
    place = meta[0]
    for index, shard in enumerate(shards):
        rows = shard.shape[0] // 2
        first = meta[4 + index]
        for half, core in ((0, place), (1, 1 - place)):
            at = pl.multiple_of((2 * first + core) * rows, 16)
            wall[pl.ds(at, rows), :] = shard[half * rows : (half + 1) * rows, :wide]
        blocks = join(shard[:rows, wide:].astype(f32), shard[rows:, wide:].astype(f32))
        at = pl.multiple_of(first * rows, 16)
        for block, values in enumerate(blocks):
            output[pl.ds(at, rows), block * LANES : (block + 1) * LANES] = values.astype(bf16)


def interleave(out, lanes, own, other, place, count):
    rows = own.shape[0] // count
    for index in range(count):
        here = slice(index * rows, (index + 1) * rows)
        first = pl.multiple_of((2 * index + place) * rows, 16)
        second = pl.multiple_of((2 * index + 1 - place) * rows, 16)
        out[pl.ds(first, rows), lanes] = own[here, :]
        out[pl.ds(second, rows), lanes] = other[here, :]


def attention_forward(heads, experts, *refs):
    (meta, x_own, x_other, wall, strips, far, segment) = refs[:7]
    kept = refs[7:12]
    (o_own, o_other, o_all, gains) = refs[12:16]
    (h1, q_out, k_out, v_out, probs, sems) = refs[16:]
    copies = []

    def keep(source, target):
        copy = pltpu.make_async_copy(source, target, sems.at[len(copies)])
        copy.start()
        copies.append(copy)

    place = meta[0]
    rows = x_own.shape[0]
    group = 2 * rows
    width = wall.shape[1]
    extras = wall[:, width - LANES :].astype(f32).T
    gain_at = HEAD_SIZE + experts
    gains[...] = extras[gain_at : gain_at + 8]
    gain_one = gains[0:1]
    for source, start in ((x_own, place * rows), (x_other, (1 - place) * rows)):
        values = source[...].astype(f32)
        h1[pl.ds(pl.multiple_of(start, 16), rows), :] = (
            values * rms_scale(values) * gain_one
        ).astype(bf16)
    keep(h1, kept[0])
    qkv = mm(h1[...], wall[...])
    lanes = q_out.shape[1]
    q_out[...] = qkv[:, :lanes].astype(bf16)
    k_out[...] = pltpu.roll(qkv[:, LANES : LANES + lanes], lanes - HEAD_SIZE, 1).astype(bf16)
    v_out[...] = qkv[:, width - lanes :].astype(bf16)
    for source, target in zip((q_out, k_out, v_out), kept[1:4]):
        keep(source, target)
    segment_row = segment[0:1, :]
    segment_column = column_of(segment_row.astype(f32)).astype(jnp.int32)
    keys = k_out[...]
    blocks = group // STRIP
    values_of = [pick_head(v_out[...], head, lanes) for head in range(heads)]
    for block in range(blocks):
        first = block * STRIP
        same = segment_column[first : first + STRIP] == segment_row
        total = jnp.zeros((STRIP, lanes), f32)
        for head in range(heads):
            query = pick_head(q_out[first : first + STRIP, :], head, lanes)
            scores = mm_nt(query, keys) + bias_row(strips, far, head, block, blocks)
            scores = jnp.where(same, scores, masked_value)
            top = jnp.max(scores, axis=1, keepdims=True)
            raised = jnp.exp(scores - top)
            mass = jnp.sum(raised, axis=1, keepdims=True)
            chances = raised * (1.0 / mass)
            probs[head, first : first + STRIP, :] = chances
            total = total + mm(chances.astype(bf16), values_of[head])
        o_all[first : first + STRIP, :] = total.astype(bf16)
        at = slice(first, first + STRIP)
        keep(probs.at[:, at, :], kept[4].at[:, at, :])
    for out, start in ((o_own, place * rows), (o_other, (1 - place) * rows)):
        values = o_all[pl.ds(pl.multiple_of(start, 16), rows), :].astype(f32)
        for index, part in enumerate(join(values[: rows // 2], values[rows // 2 :])):
            out[:, index * LANES : (index + 1) * LANES] = part.astype(bf16)
    for copy in copies:
        copy.wait()


def columns_of(*lines):
    return [column_of(line[...].astype(f32)).astype(jnp.int32) for line in lines]


def routed(hidden, extras, routes_column, keep_column, experts):
    logits = mm(hidden, extras)
    lane = iota((1, LANES), 1) - HEAD_SIZE
    valid = (lane >= 0) & (lane < experts)
    logits = jnp.where(valid, logits, masked_value)
    raised = jnp.where(valid, jnp.exp(logits - jnp.max(logits, axis=1, keepdims=True)), 0.0)
    probs = raised / jnp.sum(raised, axis=1, keepdims=True)
    onehot = lane == routes_column
    kept = keep_column.astype(f32)
    gate = jnp.sum(jnp.where(onehot, probs, 0.0), axis=1, keepdims=True) * kept
    return probs, onehot, kept, gate


def slots_by_row(routes_row, keep_row, experts, capacity):
    count = routes_row.shape[1]
    chosen = ((iota((experts, count), 0) == routes_row) & (keep_row == 1)).astype(f32)
    before = (iota((count, count), 0) < iota((count, count), 1)).astype(bf16)
    earlier = mm(chosen.astype(bf16), before)
    rank = jnp.sum(earlier * chosen, axis=0, keepdims=True).astype(jnp.int32)
    return jnp.where(keep_row == 1, routes_row * capacity + rank, -2)


def unpacked(pair):
    values = pair[...].astype(f32)
    lanes = values.shape[1] - LANES
    upper = jnp.where(iota((1, lanes), 1) < lanes - HEAD_SIZE, values[:, :lanes], 0.0)
    lower = pltpu.roll(values[:, LANES:], lanes - HEAD_SIZE, 1)
    lower = jnp.where(iota((1, lanes), 1) < lanes - HEAD_SIZE, lower, 0.0)
    return jnp.concatenate([upper, lower], axis=0)


def heads_of(own, other, place):
    own = unpacked(own)
    other = unpacked(other)
    first = jnp.where(place == 0, own, other)
    second = jnp.where(place == 0, other, own)
    return jnp.concatenate(join(first, second), axis=1).astype(bf16)


def to_experts(experts, capacity, count, *refs):
    (meta, x_own, cotangent, o_own, o_tp, o_ctx, o_far, wo_own, wo_tp, wo_ctx, wo_far) = refs[:11]
    (extras, gains, routes_row, keep_row, slot_h, slot_d) = refs[11:17]
    middle_out, sends, wo_out, wo_other = refs[17:]
    routes_column, keep_column = columns_of(routes_row, keep_row)
    extras = extras[:, extras.shape[1] - LANES :]
    place, start = meta[0], meta[2]
    interleave(wo_out, slice(None), wo_own, wo_ctx, start, count)
    interleave(wo_other, slice(None), wo_tp, wo_far, start, count)
    branch = mm_nt(heads_of(o_own, o_ctx, place), wo_out[...])
    branch = branch + mm_nt(heads_of(o_tp, o_far, place), wo_other[...])
    middle = x_own[...].astype(f32) + branch
    middle_out[...] = middle
    hidden = (middle * rms_scale(middle) * gains[1:2]).astype(bf16)
    _, _, _, gate = routed(hidden, extras, routes_column, keep_column, experts)
    out_grad = (gate * cotangent[...].astype(f32)).astype(bf16)
    slot = slots_by_row(routes_row[...], keep_row[...], experts, capacity)
    pick_h = (slot_h[...] == slot).astype(f32).astype(bf16)
    pick_d = (slot_d[...] == slot).astype(f32).astype(bf16)
    sends[...] = (mm(pick_h, hidden) + mm(pick_d, out_grad)).astype(bf16)


def gelu_both(value):
    scale = 0.7978845608028654
    cubic = 0.044715
    square = value * value
    inner = jnp.tanh(scale * value * (1.0 + cubic * square))
    half = 0.5 * (1.0 + inner)
    slope = half + 0.5 * value * (1.0 - inner * inner) * scale * (1.0 + 3.0 * cubic * square)
    return value * half, slope


def expert_kernel(owners, kinds_rows, chunks, group_owners, *refs):
    (rows_in, base_column, base_row, w_in, w_out) = refs[:5]
    (out, x_out, dy_out, act_out, dpre_out, acc_y, acc_x, full) = refs[5:]
    piece = pl.program_id(0)
    chunk = pl.program_id(1)
    pieces = pl.num_programs(0)
    capacity = kinds_rows
    per_owner = rows_in.shape[0] // owners
    span = group_owners * per_owner
    half = group_owners * capacity
    groups = owners // group_owners

    @pl.when(chunk == 0)
    def _():
        pick = (base_column[...] + piece * capacity == iota((2 * half, span), 1)).astype(f32).astype(bf16)
        for group in range(groups):
            got = mm(pick, rows_in[group * span : (group + 1) * span, :]).astype(bf16)
            x_out[0, group * half : (group + 1) * half, :] = got[:half]
            dy_out[0, group * half : (group + 1) * half, :] = got[half:]
        acc_y[...] = jnp.zeros_like(acc_y)
        acc_x[...] = jnp.zeros_like(acc_x)

    pre = mm(x_out[0], w_in[0])
    act, slope = gelu_both(pre)
    act = act.astype(bf16)
    act_out[0] = act
    acc_y[...] += mm(act, w_out[0])
    dpre = (mm_nt(dy_out[0], w_out[0]) * slope).astype(bf16)
    dpre_out[0] = dpre
    acc_x[...] += mm_nt(dpre, w_in[0])

    @pl.when(chunk == chunks - 1)
    def _():
        pick = (base_row[...] + piece * capacity == iota((span, 2 * half), 0)).astype(f32).astype(bf16)
        for group in range(groups):
            here = slice(group * half, (group + 1) * half)
            both = jnp.concatenate([acc_y[here].astype(bf16), acc_x[here].astype(bf16)], axis=0)
            part = mm(pick, both)
            there = slice(group * span, (group + 1) * span)
            full[there] = jnp.where(piece == 0, part, full[there] + part)

    @pl.when((chunk == chunks - 1) & (piece == pieces - 1))
    def _():
        width = out.shape[2]
        shares = out.shape[0] // owners
        for owner in range(owners):
            for share in range(shares):
                out[owner * shares + share] = full[
                    owner * per_owner : (owner + 1) * per_owner, share * width : (share + 1) * width
                ].astype(bf16)


def expert_grads(x_rows, dpre, act, dy, w_in_grad, w_out_grad):
    w_in_grad[0] = mm_tn(x_rows[0], dpre[0])
    w_out_grad[0] = mm_tn(act[0], dy[0])


def from_experts(experts, capacity, *refs):
    meta, rows_in, cotangent, routes_row, keep_row, slots, y_out, dx_out, gate_out = refs
    slot = column_of(slots_by_row(routes_row[...], keep_row[...], experts, capacity).astype(f32))
    slot = slot.astype(jnp.int32)
    width = rows_in.shape[1]
    pick_y = (slot == slots[0:1, :]).astype(f32).astype(bf16)
    pick_x = (slot == slots[1:2, :]).astype(f32).astype(bf16)
    dx_out[...] = mm(pick_x, rows_in[...]).astype(bf16)
    picked = mm(pick_y, rows_in[...]).astype(bf16)
    y_out[...] = picked
    upstream = jnp.where(meta[1] == 0, cotangent[:, :width], cotangent[:, width:])
    part = jnp.sum(upstream.astype(f32) * picked.astype(f32), axis=1, keepdims=True)
    gate_out[...] = jnp.broadcast_to(part, (part.shape[0], LANES)).T[:8]


def add_expert(meta, middle, gate, y_own, y_tp, result):
    width = y_own.shape[1]
    share = meta[1]
    own, other = y_own[...].astype(f32), y_tp[...].astype(f32)
    gates = gate[:, :1]
    result[:, :width] = middle[:, :width] + gates * jnp.where(share == 0, own, other)
    result[:, width:] = middle[:, width:] + gates * jnp.where(share == 0, other, own)


def middle_backward(experts, *refs):
    (meta, dx_own, dx_tp, part_own, part_tp, middle_ref, cotangent, extras) = refs[:8]
    (gains, routes_row, keep_row) = refs[8:11]
    (dmiddle_out, branch_grad, router_grad, gate_out) = refs[11:]
    routes_column, keep_column = columns_of(routes_row, keep_row)
    extras = extras[:, extras.shape[1] - LANES :]
    share = meta[1]
    own, other = dx_own[...].astype(f32), dx_tp[...].astype(f32)
    slot_grad = jnp.concatenate(
        [jnp.where(share == 0, own, other), jnp.where(share == 0, other, own)], axis=1
    )
    middle = middle_ref[...]
    scale = rms_scale(middle)
    normed = middle * scale
    gain = gains[1:2]
    hidden = (normed * gain).astype(bf16)
    probs, onehot, kept, gate = routed(hidden, extras, routes_column, keep_column, experts)
    gate_out[...] = jnp.broadcast_to(gate, gate_out.shape)
    upstream = cotangent[...].astype(f32)
    gate_grad = column_of(part_own[0:1, :] + part_tp[0:1, :])
    prob_grad = jnp.where(onehot, gate_grad * kept, 0.0)
    logit_grad = (
        probs * (prob_grad - jnp.sum(probs * prob_grad, axis=1, keepdims=True))
    ).astype(bf16)
    hidden_grad = slot_grad + mm_nt(logit_grad, extras)
    gain_grad = column_of(jnp.sum(hidden_grad * normed, axis=0, keepdims=True))
    lane = iota((1, LANES), 1)
    router_grad[...] = jnp.where(
        lane == HEAD_SIZE + experts, gain_grad, mm_tn(hidden, logit_grad)
    ).astype(bf16)
    grad = hidden_grad * gain
    dmiddle = upstream + scale * (grad - normed * jnp.mean(grad * normed, axis=1, keepdims=True))
    dmiddle_out[...] = dmiddle
    branch_grad[...] = dmiddle.astype(bf16)


def attention_backward(heads, buckets, shard, *refs):
    (meta, x_own, x_other) = refs[:3]
    kept = refs[3:8]
    (db, o_all, wo_ref, wall, router_grad) = refs[8:13]
    (payload, top_out, bottom_out, dh1_own, dh1_other) = refs[13:18]
    (sums, do_all, dq, dk, dv, dqkv, dh1) = refs[18:25]
    (h1, q_in, k_in, v_in, probs, sems) = refs[25:]
    blocks = q_in.shape[0] // STRIP
    moves = [(kept[1], q_in), (kept[2], k_in), (kept[3], v_in)]
    for block in range(blocks):
        at = slice(block * STRIP, (block + 1) * STRIP)
        moves.append((kept[4].at[:, at, :], probs.at[:, at, :]))
    moves.append((kept[0], h1))
    copies = [pltpu.make_async_copy(a, b, sems.at[i]) for i, (a, b) in enumerate(moves)]
    for copy in copies:
        copy.start()
    place = meta[0]
    rows = x_own.shape[0]
    group = 2 * rows
    lanes = q_in.shape[1]
    own_at = pl.ds(pl.multiple_of(place * rows, 16), rows)
    other_at = pl.ds(pl.multiple_of((1 - place) * rows, 16), rows)
    both = mm(db[...], wo_ref[...])
    high = pltpu.roll(both[:, LANES : LANES + lanes], lanes - HEAD_SIZE, 1)
    do_all[...] = jnp.where(place == 0, both[:, :lanes], high).astype(bf16)
    sums[...] = jnp.zeros_like(sums)
    for copy in copies[:3]:
        copy.wait()
    keys = k_in[...]
    values = v_in[...]
    ahead = [jnp.zeros((STRIP, STRIP), f32) for _ in range(heads)]
    behind = [jnp.zeros((STRIP, STRIP), f32) for _ in range(heads)]
    for block in range(blocks):
        at = slice(block * STRIP, (block + 1) * STRIP)
        copies[3 + block].wait()
        dq_total = jnp.zeros((STRIP, lanes), f32)
        for head in range(heads):
            query = pick_head(q_in[at, :], head, lanes)
            chances = probs[head, at, :]
            grad = pick_head(do_all[at, :], head, lanes)
            chance_grad = mm_nt(grad, values)
            mean = jnp.sum(chances * chance_grad, axis=1, keepdims=True)
            score_grad = (chances * (chance_grad - mean)).astype(bf16)
            dv_part = mm_tn(chances.astype(bf16), grad)
            dk_part = mm_tn(score_grad, query)
            if block == 0 and head == 0:
                dv[...] = dv_part
                dk[...] = dk_part
            else:
                dv[...] += dv_part
                dk[...] += dk_part
            dq_total = dq_total + mm(score_grad, pick_head(keys, head, lanes))
            rounded = score_grad.astype(f32)
            for other in range(blocks):
                gap = other - block
                part = rounded[:, other * STRIP : (other + 1) * STRIP]
                if abs(gap) <= 1:
                    sums[head, :, (gap + 2) * STRIP : (gap + 3) * STRIP] += part
                elif gap > 0:
                    ahead[head] = ahead[head] + part
                else:
                    behind[head] = behind[head] + part
        dq[at, :] = dq_total
    half = HEAD_SIZE
    dqkv[:, :LANES] = dq[:, :LANES].astype(bf16)
    shifted = pltpu.roll(dk[...], half, 1)
    dqkv[:, LANES : 2 * LANES] = (dq[:, LANES:] + shifted[:, :LANES]).astype(bf16)
    dqkv[:, 2 * LANES : 3 * LANES] = shifted[:, LANES:].astype(bf16)
    dqkv[:, 3 * LANES :] = dv[...].astype(bf16)
    dh1[...] = mm_nt(dqkv[...], wall[...])
    gain_part = None
    for source, at, target in ((x_own, own_at, dh1_own), (x_other, other_at, dh1_other)):
        values = source[...].astype(f32)
        grad = dh1[at, :]
        target[...] = grad.astype(bf16)
        part = jnp.sum(grad * (values * rms_scale(values)), axis=0, keepdims=True)
        gain_part = part if gain_part is None else gain_part + part
    spread = skew(sums[...].reshape(heads * STRIP, 4 * STRIP), False)
    diagonals = jnp.sum(spread.reshape(heads, STRIP, 4 * STRIP), axis=1)
    picks = (bucket_index(iota((4 * STRIP, 1), 0) - 2 * STRIP) == iota((1, LANES), 1)).astype(f32)
    in_buckets = jnp.dot(diagonals, picks, precision=highest, preferred_element_type=f32)
    lane = iota((1, LANES), 1)
    row = lax.rem(iota((wall.shape[0], 1), 0), shard)
    riders = jnp.where(lane == HEAD_SIZE, column_of(gain_part), 0.0)
    for head in range(heads):
        line = in_buckets[head : head + 1]
        line = line + jnp.where(lane == buckets - 1, jnp.sum(ahead[head]), 0.0)
        line = line + jnp.where(lane == buckets // 2 - 1, jnp.sum(behind[head]), 0.0)
        riders = riders + jnp.where(row == head, pltpu.roll(line, HEAD_SIZE + 1, 1), 0.0)
    width = wall.shape[1]
    copies[-1].wait()
    grads = mm_tn(h1[...], dqkv[...])
    payload[:, : width - LANES] = grads[:, : width - LANES].astype(bf16)
    payload[:, width - LANES : width] = (grads[:, width - LANES :] + riders).astype(bf16)
    grads = mm_tn(db[...], o_all[...])
    payload[:, width : width + lanes - LANES] = grads[:, : lanes - LANES].astype(bf16)
    payload[:, width + lanes - LANES :] = (
        grads[:, lanes - LANES :] + router_grad[...].astype(f32)
    ).astype(bf16)
    half = top_out.shape[0]
    across = pl.multiple_of(meta[3] * shard if 2 * half == shard else 0 * meta[3], 16)
    top_out[...] = payload[pl.ds(across, half), :]
    bottom_out[...] = payload[pl.ds(across + half, half), :]


def ring_add(places, right_mine, left_mine, from_left, from_right, right_out, left_out):
    rows = right_mine.shape[0]
    span = from_left.shape[0]
    right_out[...] = right_mine[...]
    left_out[...] = left_mine[...]
    top, bottom = slice(0, span), slice(rows - span, rows)
    right_out[top] = (right_mine[top].astype(f32) + from_left[...].astype(f32)).astype(bf16)
    left_out[bottom] = (left_mine[bottom].astype(f32) + from_right[...].astype(f32)).astype(bf16)


def ring_end(at, place, sums, own, send, table, riders_own, riders_other):
    rows = own.shape[0]
    first, second = sums[:rows, :], sums[rows : 2 * rows, :]
    mine = jnp.where(place == 0, first, second)
    other = jnp.where(place == 0, second, first)
    own[...] = mine
    send[:rows, :] = other
    send[rows:, :] = sums[:8, :]
    table[...] = sums[:8, at : at + LANES]
    riders_own[...] = mine[:, at : at + LANES]
    riders_other[...] = other[:, at : at + LANES]


def ring_last(at, places, mine, from_left, from_right, own, send, table, riders_own, riders_other):
    total = mine[...].astype(f32) + from_left[...].astype(f32) + from_right[...].astype(f32)
    ring_end(at, places[0], total, own, send, table, riders_own, riders_other)


def ring_whole(at, places, sums, own, send, table, riders_own, riders_other):
    ring_end(at, places[0], sums[...], own, send, table, riders_own, riders_other)


def shards_of_sums(experts, buckets, heads, *refs):
    (meta, own_ref, other, own_top, from_tp, from_far) = refs[:6]
    (query_out, key_out, value_out, output_out, router_out, gain_one, gain_two, table) = refs[6:]
    place = meta[0]
    rows, width = query_out.shape[0], query_out.shape[1] // 2
    lanes = width + HEAD_SIZE
    wide = 3 * width + HEAD_SIZE
    own = own_ref[...]
    more = other[:rows, :]
    lane = iota((1, lanes), 1)
    for at, moved, out in (
        (0, False, query_out),
        (LANES, True, key_out),
        (2 * width, False, value_out),
        (wide, False, output_out),
    ):
        parts = [values[:, at : at + lanes] for values in (own, more)]
        if moved:
            parts = [pltpu.roll(part, lanes - HEAD_SIZE, 1) for part in parts]
        parts = [jnp.where(lane < width, part, 0.0) for part in parts]
        first = jnp.where(place == 0, parts[0], parts[1])
        second = jnp.where(place == 0, parts[1], parts[0])
        for index, block in enumerate(join(first, second)):
            out[:, index * LANES : (index + 1) * LANES] = block
    total = (own + more)[:, wide + lanes - LANES :].T
    router_out[...] = total[HEAD_SIZE : HEAD_SIZE + experts, :]
    gain_two[...] = total[HEAD_SIZE + experts : HEAD_SIZE + experts + 1, :]
    line = (own + more)[:, wide - LANES : wide] + (from_tp[...] + from_far[...])
    gain_one[...] = line.T[HEAD_SIZE : HEAD_SIZE + 1, :]
    own_lines = own_top[...]
    other_lines = other[rows : rows + 8, wide - LANES : wide]
    own_lines = pltpu.roll(own_lines, LANES - HEAD_SIZE - 1, 1)
    other_lines = pltpu.roll(other_lines, LANES - HEAD_SIZE - 1, 1)
    table[:heads, :] = jnp.where(place == 0, own_lines, other_lines)[:heads, :buckets]
    table[heads : 2 * heads, :] = jnp.where(place == 0, other_lines, own_lines)[:heads, :buckets]


def input_backward(x_own, dmiddle, gains, near, far, out):
    values = x_own[...].astype(f32)
    scale = rms_scale(values)
    normed = values * scale
    grad = (near[...].astype(f32) + far[...].astype(f32)) * gains[0:1]
    out[...] = dmiddle[...] + scale * (
        grad - normed * jnp.mean(grad * normed, axis=1, keepdims=True)
    )


def swap(value, axis):
    return lax.ppermute(value, axis, [(0, 1), (1, 0)])


def ring_order(count):
    return list(range(0, count, 2)) + list(range(count - 1, 0, -2))


def ring_steps(count):
    order = ring_order(count)
    right = [(order[i], order[(i + 1) % count]) for i in range(count)]
    return order, right, [(b, a) for a, b in right]


def device_table(fsdp_count, ctx_count, tp_count, aligned):
    order = ring_order(fsdp_count)
    rows = []
    for place in range(fsdp_count):
        spot = order.index(place)
        at = lambda distance: order[(spot + distance) % fsdp_count]
        half = fsdp_count // 2
        ring = [place]
        for step in range(1, half):
            ring += [at(-step), at(step)]
        ring.append(at(half))
        for step in range(half, 0, -1):
            ring += [at(step - 1), at(1 - step)]
        for core in range(ctx_count):
            for share in range(tp_count):
                rows.append([core, share, core if aligned else 0, at(half)] + (ring if aligned else []))
    return np.array(rows, np.int32)


def ring_gather(shard, count, side):
    _, right, left = ring_steps(count)
    shards = [shard]
    going_right, going_left = shard, shard
    for step in range(1, count // 2):
        going_right = lax.ppermute(going_right, "fsdp", right)
        going_left = lax.ppermute(going_left, "fsdp", left)
        if step == 1:
            going_right, going_left, side = lax.optimization_barrier((going_right, going_left, side))
        shards += [going_right, going_left]
    shards.append(lax.ppermute(going_right, "fsdp", right))
    return shards, side


def ring_sums(payload, top, bottom, count, at, meta, sides):
    rows = payload.shape[0] // count
    lanes = payload.shape[1]
    half = rows // 2
    outs = [
        shape((half, lanes), f32),
        shape((half + 8, lanes), f32),
        shape((8, LANES), f32),
        shape((half, LANES), f32),
        shape((half, LANES), f32),
    ]
    if rows % 32 or count % 2:
        sums = lax.psum_scatter(payload.astype(f32), "fsdp", scatter_dimension=0, tiled=True)
        return kernel_call(functools.partial(ring_whole, at), outs, [smem, vmem])(meta, sums)
    _, right, left = ring_steps(count)
    going_right, going_left = top, bottom
    spec = lambda which: pl.BlockSpec((rows, lanes), lambda i, places: (places[which], 0))
    params = pltpu.CompilerParams(vmem_limit_bytes=8 * MIB)
    for step in range(count // 2, 0, -1):
        from_left = lax.ppermute(going_right, "fsdp", right)
        from_right = lax.ppermute(going_left, "fsdp", left)
        if step in sides:
            from_left, from_right, _ = lax.optimization_barrier((from_left, from_right, sides[step]))
        which = 4 + count + 2 * (count // 2 - step)
        whole = lambda dims: pl.BlockSpec(dims, lambda i, places: (0, 0))
        last = step == 1
        step_outs = outs if last else [shape((rows, lanes), bf16)] * 2
        out = pl.pallas_call(
            functools.partial(ring_last, at) if last else ring_add,
            grid_spec=pltpu.PrefetchScalarGridSpec(
                num_scalar_prefetch=1,
                grid=(1,),
                in_specs=([spec(which)] if last else [spec(which), spec(which + 1)])
                + [whole(from_left.shape), whole(from_right.shape)],
                out_specs=[whole(o.shape) for o in step_outs],
            ),
            out_shape=step_outs,
            compiler_params=params,
            cost_estimate=pl.CostEstimate(flops=0, bytes_accessed=1024 * 1024, transcendentals=0),
        )(meta, *([payload] if last else [payload, payload]), from_left, from_right)
        if last:
            return out
        going_right, going_left = out


def body(
    tokens,
    cotangent,
    w_query,
    w_key,
    w_value,
    w_output,
    w_router,
    gain_attn,
    gain_moe,
    rel_table,
    w_in,
    w_out,
    lengths,
    routes,
    keep_mask,
):
    rows, model_width = tokens.shape
    fsdp_count = lax.axis_size("fsdp")
    owners = lax.axis_size(("fsdp", "ctx"))
    tp_count = lax.axis_size("tp")
    place = lax.axis_index("ctx")
    share = lax.axis_index("tp")
    fsdp_place = lax.axis_index("fsdp")
    group = 2 * rows
    experts = w_router.shape[1]
    capacity = max(2, (5 * rows + 4 * experts - 1) // (4 * experts))
    pieces = w_in.shape[0]
    split_count = owners * pieces // experts
    hidden_width = w_in.shape[2]
    heads = rel_table.shape[1] // 2
    heads_all = heads * 2 * tp_count
    width = heads * HEAD_SIZE
    lanes = width + HEAD_SIZE
    shard_rows = w_query.shape[0]
    buckets = rel_table.shape[0]

    def full(dims, dtype):
        return shape(dims, dtype)

    wide = 3 * width + HEAD_SIZE
    aligned = shard_rows % 16 == 0 and fsdp_count % 2 == 0
    count = fsdp_count if aligned else 1
    table = jnp.asarray(device_table(fsdp_count, 2, tp_count, aligned))
    device = lax.axis_index(("fsdp", "ctx", "tp"))
    meta = lax.dynamic_slice(table, (device, 0), (1, table.shape[1])).reshape(-1)
    shard_own, shard_send, wo_shard = kernel_call(
        pack_rows,
        [full((shard_rows, wide), bf16), full((shard_rows, wide), bf16), full((2 * shard_rows, lanes), bf16)],
        [smem] + [vmem] * 7,
        moved=512 * 1024,
        mib=60,
    )(meta, w_query, w_key, w_value, w_output, w_router.T, gain_attn[None, :], gain_moe[None, :])
    shard_other = swap(shard_send, "ctx")
    shard = jnp.concatenate(
        [jnp.concatenate([shard_own, shard_other], axis=0), wo_shard], axis=1
    )
    x_other = swap(tokens, "ctx")

    def ordered(own, other):
        if aligned:
            return own, other
        dims = (fsdp_count, 1, shard_rows, own.shape[1])
        pair = in_order(own.reshape(dims), other.reshape(dims), 1).reshape(2 * own.shape[0], -1)
        return pair[: own.shape[0]], pair[own.shape[0] :]

    def in_order(own, other, axis):
        return jnp.where(
            place == 0,
            jnp.concatenate([own, other], axis=axis),
            jnp.concatenate([other, own], axis=axis),
        )

    strips, far, segment = kernel_call(
        functools.partial(attention_tables, heads),
        [
            full((heads, STRIP, 3 * STRIP), f32),
            full((8, LANES), f32),
            full((8, group), jnp.int32),
        ],
        [smem] * 3,
        moved=1024 * 1024,
        mib=8,
    )(meta, lengths, rel_table.T)
    if aligned:
        shards, (strips, far, segment) = ring_gather(shard, fsdp_count, (strips, far, segment))
        wall, wo_own = kernel_call(
            functools.partial(put_in_rows, len(shards)),
            [full((model_width, wide), bf16), full((model_width // 2, 2 * width), bf16)],
            [smem] + [vmem] * len(shards),
            moved=4 * 1024 * 1024,
        )(meta, *shards)
    else:
        both = lax.all_gather(shard, "fsdp", axis=0, tiled=False)
        upper, lower = both[:, :shard_rows], both[:, shard_rows:]
        wall = jnp.concatenate(
            ordered(upper[:, :, :wide].reshape(-1, wide), lower[:, :, :wide].reshape(-1, wide)), axis=0
        )
        wo_own = jnp.concatenate([upper[:, :, wide : wide + width], lower[:, :, wide : wide + width]], axis=2)
        wo_own = wo_own.reshape(-1, 2 * width)

    kept_shapes = [(group, model_width)] + [(group, lanes)] * 3
    probs_shape = (heads, group, group)
    blocks = group // STRIP
    kept_scratch = [pltpu.VMEM(dims, bf16) for dims in kept_shapes] + [pltpu.VMEM(probs_shape, f32)]
    h1, q, k, v, probs, o_own, o_other, o_all, gains = kernel_call(
        functools.partial(attention_forward, heads, experts),
        [pltpu.HBM(dims, bf16) for dims in kept_shapes]
        + [
            pltpu.HBM(probs_shape, f32),
            full((rows // 2, 2 * width), bf16),
            full((rows // 2, 2 * width), bf16),
            full((group, lanes), bf16),
            full((8, model_width), f32),
        ],
        [smem] + [vmem] * 6,
        out_specs=[hbm] * 5 + [vmem] * 4,
        scratch=kept_scratch + [pltpu.SemaphoreType.DMA((4 + blocks,))],
        flops=2 * group * model_width * wide * 8,
        moved=8 * 1024 * 1024,
        mib=20,
    )(meta, tokens, x_other, wall, strips, far, segment)
    wo_tp = swap(wo_own, "tp")
    wo_ctx = swap(wo_own, "ctx")
    wo_tp, gains = lax.optimization_barrier((wo_tp, gains))
    wo_far = swap(wo_tp, "ctx")
    wo_own, wo_ctx = ordered(wo_own, wo_ctx)
    wo_tp, wo_far = ordered(wo_tp, wo_far)

    o_tp = swap(o_own, "tp")
    o_ctx = swap(o_other, "ctx")
    o_far = lax.ppermute(o_other, ("ctx", "tp"), [(i, 3 - i) for i in range(4)])

    per_owner = 2 * pieces * capacity
    owner_of = np.repeat(np.arange(owners), per_owner)
    inside = np.tile(np.arange(per_owner), owners)
    kind = inside // (pieces * capacity)
    piece_of = owner_of * pieces + (inside // capacity) % pieces
    slot_of = (piece_of // split_count) * capacity + inside % capacity
    slot_first = np.where(kind == 0, slot_of, -1).astype(np.int32)
    slot_second = np.where(kind == 1, slot_of, -1).astype(np.int32)
    routes_row = routes.reshape(1, rows)
    keep_row = keep_mask.reshape(1, rows)

    middle, sends, wo_full = kernel_call(
        functools.partial(to_experts, experts, capacity, count),
        [
            full((rows, model_width), f32),
            full((owners * per_owner, model_width), bf16),
            full((model_width, 2 * width), bf16),
        ],
        [smem] + [vmem] * 16,
        scratch=[pltpu.VMEM((model_width, 2 * width), bf16)],
        flops=2 * rows * model_width * (model_width + 2 * owners * per_owner),
        moved=6 * 1024 * 1024,
    )(
        meta, tokens, cotangent, o_own, o_tp, o_ctx, o_far, wo_own, wo_tp, wo_ctx, wo_far, wall,
        gains, routes_row, keep_row, slot_first[:, None], slot_second[:, None],
    )

    arrived = lax.all_to_all(
        sends.reshape(owners, per_owner, model_width),
        ("fsdp", "ctx"),
        split_axis=0,
        concat_axis=0,
        tiled=True,
    ).reshape(owners * per_owner, model_width)

    group_owners = min(16, owners)
    half = group_owners * capacity
    spot = np.arange(2 * half) % half
    base = (
        (spot // capacity) * per_owner
        + (np.arange(2 * half) // half) * pieces * capacity
        + spot % capacity
    ).astype(np.int32)
    chunk_width = 768 if hidden_width % 768 == 0 else hidden_width
    chunks = hidden_width // chunk_width
    slot_rows = owners * capacity
    part_width = model_width // tp_count
    whole = lambda *dims: pl.BlockSpec(dims, lambda i, j: (0,) * len(dims))
    outgoing, x_rows, dy_rows, act, dpre = kernel_call(
        functools.partial(expert_kernel, owners, capacity, chunks, group_owners),
        [
            pltpu.HBM((owners * tp_count, per_owner, part_width), bf16),
            pltpu.HBM((pieces, slot_rows, model_width), bf16),
            pltpu.HBM((pieces, slot_rows, model_width), bf16),
            pltpu.HBM((pieces, slot_rows, hidden_width), bf16),
            pltpu.HBM((pieces, slot_rows, hidden_width), bf16),
        ],
        [
            whole(owners * per_owner, model_width),
            whole(2 * half, 1),
            whole(1, 2 * half),
            pl.BlockSpec((1, model_width, chunk_width), lambda i, j: (i, 0, j)),
            pl.BlockSpec((1, chunk_width, model_width), lambda i, j: (i, j, 0)),
        ],
        out_specs=[
            whole(owners * tp_count, per_owner, part_width),
            pl.BlockSpec((1, slot_rows, model_width), lambda i, j: (i, 0, 0)),
            pl.BlockSpec((1, slot_rows, model_width), lambda i, j: (i, 0, 0)),
            pl.BlockSpec((1, slot_rows, chunk_width), lambda i, j: (i, 0, j)),
            pl.BlockSpec((1, slot_rows, chunk_width), lambda i, j: (i, 0, j)),
        ],
        scratch=[
            pltpu.VMEM((slot_rows, model_width), f32),
            pltpu.VMEM((slot_rows, model_width), f32),
            pltpu.VMEM((owners * per_owner, model_width), f32),
        ],
        grid=(pieces, chunks),
        mib=24 if owners <= 16 else 60,
        flops=8 * pieces * slot_rows * model_width * hidden_width,
        moved=12 * 1024 * 1024,
    )(arrived, base[:, None], base[None, :], w_in, w_out)

    returned = lax.all_to_all(
        outgoing, ("fsdp", "ctx", "tp"), split_axis=0, concat_axis=0, tiled=True
    ).reshape(owners * tp_count * per_owner, part_width)
    part = 512 if hidden_width % 512 == 0 else hidden_width
    rows_spec = pl.BlockSpec((1, slot_rows, model_width), lambda i, j: (i, 0, 0))
    hidden_spec = pl.BlockSpec((1, slot_rows, part), lambda i, j: (i, 0, j))
    w_in_grad, w_out_grad = kernel_call(
        expert_grads,
        [full(w_in.shape, f32), full(w_out.shape, f32)],
        [rows_spec, hidden_spec, hidden_spec, rows_spec],
        out_specs=[
            pl.BlockSpec((1, model_width, part), lambda i, j: (i, 0, j)),
            pl.BlockSpec((1, part, model_width), lambda i, j: (i, j, 0)),
        ],
        grid=(pieces, hidden_width // part),
        flops=4 * pieces * slot_rows * model_width * hidden_width,
        moved=24 * 1024 * 1024,
        mib=24,
    )(x_rows, dpre, act, dy_rows)
    returned, w_in_grad, w_out_grad = lax.optimization_barrier((returned, w_in_grad, w_out_grad))

    back_first = np.repeat(slot_first.reshape(owners, 1, per_owner), tp_count, axis=1).reshape(1, -1)
    back_second = np.repeat(slot_second.reshape(owners, 1, per_owner), tp_count, axis=1).reshape(1, -1)
    y_own, dx_own, part_own = kernel_call(
        functools.partial(from_experts, experts, capacity),
        [
            full((rows, part_width), bf16),
            full((rows, part_width), bf16),
            full((8, rows), f32),
        ],
        [smem] + [vmem] * 5,
        flops=4 * rows * returned.shape[0] * part_width,
        moved=2 * 1024 * 1024,
    )(meta, returned, cotangent, routes_row, keep_row, np.concatenate([back_first, back_second], axis=0))
    dx_tp = swap(dx_own, "tp")
    part_tp = swap(part_own, "tp")

    middle_grad, db_own, router_grad, gate = kernel_call(
        functools.partial(middle_backward, experts),
        [
            full((rows, model_width), f32),
            full((rows, model_width), bf16),
            full((model_width, LANES), bf16),
            full((rows, LANES), f32),
        ],
        [smem] + [vmem] * 10,
        flops=6 * rows * LANES * model_width,
        moved=6 * 1024 * 1024,
    )(meta, dx_own, dx_tp, part_own, part_tp, middle, cotangent, wall, gains, routes_row, keep_row)
    y_own, gate = lax.optimization_barrier((y_own, gate))
    y_tp = swap(y_own, "tp")
    db = lax.all_gather(db_own, "ctx", axis=0, tiled=True)

    half = model_width // fsdp_count // 2
    payload, top, bottom, dh1_own, dh1_other = kernel_call(
        functools.partial(attention_backward, heads, buckets, model_width // fsdp_count),
        [
            full((model_width, wide + lanes), bf16),
            full((half if aligned else 16, wide + lanes), bf16),
            full((half if aligned else 16, wide + lanes), bf16),
            full((rows, model_width), bf16),
            full((rows, model_width), bf16),
        ],
        [smem] + [vmem] * 2 + [hbm] * 5 + [vmem] * 5,
        scratch=[
            pltpu.VMEM((heads, STRIP, 4 * STRIP), f32),
            pltpu.VMEM((group, lanes), bf16),
            pltpu.VMEM((group, lanes), f32),
            pltpu.VMEM((group, lanes), f32),
            pltpu.VMEM((group, lanes), f32),
            pltpu.VMEM((group, wide), bf16),
            pltpu.VMEM((group, model_width), f32),
            *kept_scratch,
            pltpu.SemaphoreType.DMA((4 + blocks,)),
        ],
        flops=2 * group * model_width * wide * 12,
        mib=28,
        moved=8 * 1024 * 1024,
    )(
        meta, tokens, x_other, h1, q, k, v, probs, db, o_all, wo_full, wall, router_grad,
    )

    result = kernel_call(
        add_expert,
        [full((rows, model_width), f32)],
        [smem] + [vmem] * 4,
        moved=4 * 1024 * 1024,
    )(meta, middle, gate, y_own, y_tp)[0]
    dh1_sum = (dh1_own.astype(f32) + swap(dh1_other, "ctx").astype(f32)).astype(bf16)
    dh1_far = swap(dh1_sum, "tp")
    input_grad = kernel_call(
        input_backward,
        [full((rows, model_width), f32)],
        [vmem] * 5,
        moved=4 * 1024 * 1024,
    )(tokens, middle_grad, gains, dh1_sum, dh1_far)[0]
    own, send, own_lines, riders_own, riders_other = ring_sums(
        payload, top, bottom, fsdp_count, wide - LANES, meta, {1: (result, input_grad)}
    )
    other = swap(send, "ctx")
    from_tp = swap(riders_own, "tp")
    from_far = lax.ppermute(riders_other, ("ctx", "tp"), [(i, 3 - i) for i in range(4)])

    shard = full((shard_rows, 2 * width), f32)
    query_grad, key_grad, value_grad, output_grad, router_sum, gain_one, gain_two, table_grad = kernel_call(
        functools.partial(shards_of_sums, experts, buckets, heads),
        [shard] * 4
        + [
            full((experts, shard_rows), f32),
            full((1, shard_rows), f32),
            full((1, shard_rows), f32),
            full((2 * heads, buckets), f32),
        ],
        [smem] + [vmem] * 5,
        moved=1024 * 1024,
    )(meta, own, other, own_lines, from_tp, from_far)
    return (
        result,
        input_grad,
        query_grad,
        key_grad,
        value_grad,
        output_grad,
        router_sum.T,
        gain_one.reshape(shard_rows),
        gain_two.reshape(shard_rows),
        table_grad.T,
        w_in_grad,
        w_out_grad,
    )


def solution(mesh):
    in_specs = (
        P(("fsdp", "ctx"), None),
        P(("fsdp", "ctx"), None),
        P(("fsdp", "ctx"), "tp"),
        P(("fsdp", "ctx"), "tp"),
        P(("fsdp", "ctx"), "tp"),
        P(("fsdp", "ctx"), "tp"),
        P(("fsdp", "ctx"), None),
        P(("fsdp", "ctx")),
        P(("fsdp", "ctx")),
        P(None, "tp"),
        P(("fsdp", "ctx"), None, "tp"),
        P(("fsdp", "ctx"), "tp", None),
        P("fsdp", None),
        P(("fsdp", "ctx"), None),
        P(("fsdp", "ctx")),
    )
    out_specs = (
        P(("fsdp", "ctx"), None),
        P(("fsdp", "ctx"), None),
        P(("fsdp", "ctx"), "tp"),
        P(("fsdp", "ctx"), "tp"),
        P(("fsdp", "ctx"), "tp"),
        P(("fsdp", "ctx"), "tp"),
        P(("fsdp", "ctx"), None),
        P(("fsdp", "ctx")),
        P(("fsdp", "ctx")),
        P(None, "tp"),
        P(("fsdp", "ctx"), None, "tp"),
        P(("fsdp", "ctx"), "tp", None),
    )
    return jax.shard_map(body, mesh=mesh, in_specs=in_specs, out_specs=out_specs, check_vma=False)
```

```python
import functools

import jax
import jax.numpy as jnp
import numpy as np
from jax import lax
from jax.experimental import pallas as pl
from jax.experimental.pallas import tpu as pltpu
from jax.sharding import PartitionSpec as P

epsilon = 1e-06
masked_value = -1e30
bucket_edges = (12, 16, 23, 32, 46, 64, 91)
highest = lax.Precision.HIGHEST
LANES = 128
STRIP = 128
HEAD_SIZE = 64
MIB = 1024 * 1024
f32 = jnp.float32
bf16 = jnp.bfloat16
vmem = pl.BlockSpec(memory_space=pltpu.VMEM)
smem = pl.BlockSpec(memory_space=pltpu.SMEM)
hbm = pl.BlockSpec(memory_space=pltpu.HBM)


def mm(left, right):
    return jnp.dot(left, right, preferred_element_type=f32)


def mm_nt(left, right):
    return lax.dot_general(left, right, (((1,), (1,)), ((), ())), preferred_element_type=f32)


def mm_tn(left, right):
    return lax.dot_general(left, right, (((0,), (0,)), ((), ())), preferred_element_type=f32)


def rms_scale(values):
    return lax.rsqrt(jnp.mean(values * values, axis=-1, keepdims=True) + epsilon)


def iota(shape, dim):
    return lax.broadcasted_iota(jnp.int32, shape, dim)


def bucket_index(offset):
    side = jnp.where(offset > 0, 16, 0).astype(jnp.int32)
    distance = jnp.abs(offset)
    far_bucket = 8 + sum(((distance >= edge).astype(jnp.int32) for edge in bucket_edges))
    return side + jnp.where(distance < 8, distance, far_bucket)


def kernel_call(body, outs, in_specs, out_specs=None, scratch=(), grid=None, flops=0, moved=0, mib=16):
    extra = {} if grid is None else {"grid": grid}
    return pl.pallas_call(
        body,
        out_shape=outs,
        in_specs=in_specs,
        out_specs=[vmem] * len(outs) if out_specs is None else out_specs,
        scratch_shapes=list(scratch),
        compiler_params=pltpu.CompilerParams(vmem_limit_bytes=mib * MIB),
        cost_estimate=pl.CostEstimate(flops=flops, bytes_accessed=moved, transcendentals=0),
        **extra,
    )


def shape(dims, dtype):
    return jax.ShapeDtypeStruct(tuple(dims), dtype)


def segments(lengths_ref, columns, rows):
    places = iota((rows, columns), 1)
    total = jnp.zeros((rows, columns), jnp.int32)
    end = 0
    for entry in range(lengths_ref.shape[1]):
        end = end + lengths_ref[0, entry]
        total = total + (places >= end).astype(jnp.int32)
    return total


def column_of(line):
    return jnp.broadcast_to(line, (LANES, line.shape[1])).T[:, :1]


def skew(values, right):
    rows, lanes = values.shape
    row = lax.rem(iota((rows, 1), 0), STRIP)
    step = 1
    while step < STRIP:
        moved = pltpu.roll(values, step if right else lanes - step, 1)
        values = jnp.where((row & step) > 0, moved, values)
        step *= 2
    return values


def attention_tables(heads, meta, lengths, table, strips, far, segment):
    lanes = 4 * STRIP
    buckets = table.shape[1]
    first_head = meta[0] * heads
    bucket = bucket_index(iota((1, lanes), 1) - 2 * STRIP)
    far[...] = jnp.zeros_like(far)
    for head in range(heads):
        line = jnp.zeros((1, lanes), f32)
        for entry in range(buckets):
            line = jnp.where(bucket == entry, table[first_head + head, entry], line)
        strip = skew(jnp.broadcast_to(line, (STRIP, lanes)), True)
        strips[head] = strip[:, STRIP:]
        far[2 * head : 2 * head + 1, :] = jnp.full((1, LANES), table[first_head + head, buckets - 1], f32)
        far[2 * head + 1 : 2 * head + 2, :] = jnp.full(
            (1, LANES), table[first_head + head, buckets // 2 - 1], f32
        )
    segment[...] = segments(lengths, segment.shape[1], segment.shape[0])


def bias_row(strips, far, head, block, blocks):
    parts = []
    for other in range(blocks):
        gap = other - block
        if abs(gap) <= 1:
            parts.append(strips[head, :, (gap + 1) * STRIP : (gap + 2) * STRIP])
        else:
            row = 2 * head + (0 if gap > 0 else 1)
            parts.append(jnp.broadcast_to(far[row : row + 1, :], (STRIP, STRIP)))
    return jnp.concatenate(parts, axis=1)


def head_mask(head, lanes):
    lane = iota((1, lanes), 1)
    return (lane >= head * HEAD_SIZE) & (lane < (head + 1) * HEAD_SIZE)


def pick_head(values, head, lanes):
    return jnp.where(head_mask(head, lanes), values, 0.0).astype(bf16)


def half_columns(weight, which):
    values = weight[...].astype(f32)
    width = values.shape[1] // 2
    lanes = width + HEAD_SIZE
    high = pltpu.roll(values[:, LANES : LANES + lanes], lanes - HEAD_SIZE, 1)
    picked = jnp.where(which == 0, values[:, :lanes], high)
    return jnp.where(iota((1, lanes), 1) < width, picked, 0.0)


def join(first, second):
    moved = pltpu.roll(second, HEAD_SIZE, 1)
    return first[:, :LANES], first[:, LANES:] + moved[:, :LANES], moved[:, LANES:]


def pack_rows(*refs):
    (meta, w_query, w_key, w_value, w_output, w_router, gain_one, gain_two, own, send, output) = refs
    rows = w_query.shape[0]
    experts = w_router.shape[0]
    width = w_query.shape[1] // 2
    lanes = width + HEAD_SIZE
    lane = iota((1, lanes), 1)
    diagonal = iota((rows, rows), 0) == iota((rows, rows), 1)
    placing = (iota((experts, lanes), 0) + width == iota((experts, lanes), 1)).astype(f32)
    extras = mm_tn(w_router[...], placing.astype(bf16))
    for index, gain in enumerate((gain_one, gain_two)):
        column = jnp.sum(
            jnp.where(diagonal, jnp.broadcast_to(gain[...].astype(f32), (rows, rows)), 0.0),
            axis=1,
            keepdims=True,
        )
        extras = extras + jnp.where(lane == width + experts + index, column, 0.0)
    for which, out in ((meta[0], own), (1 - meta[0], send)):
        at = 0
        for block in join(half_columns(w_query, which), half_columns(w_key, which)):
            out[:, at : at + LANES] = block.astype(bf16)
            at += LANES
        out[:, at:] = (half_columns(w_value, which) + extras).astype(bf16)
    output[:rows, :] = half_columns(w_output, 0).astype(bf16)
    output[rows:, :] = half_columns(w_output, 1).astype(bf16)


def put_in_rows(count, *refs):
    meta = refs[0]
    shards = refs[1 : 1 + count]
    wall, output = refs[1 + count :]
    wide = wall.shape[1]
    place = meta[0]
    for index, shard in enumerate(shards):
        rows = shard.shape[0] // 2
        first = meta[4 + index]
        for half, core in ((0, place), (1, 1 - place)):
            at = pl.multiple_of((2 * first + core) * rows, 16)
            wall[pl.ds(at, rows), :] = shard[half * rows : (half + 1) * rows, :wide]
        blocks = join(shard[:rows, wide:].astype(f32), shard[rows:, wide:].astype(f32))
        at = pl.multiple_of(first * rows, 16)
        for block, values in enumerate(blocks):
            output[pl.ds(at, rows), block * LANES : (block + 1) * LANES] = values.astype(bf16)


def interleave(out, lanes, own, other, place, count):
    rows = own.shape[0] // count
    for index in range(count):
        here = slice(index * rows, (index + 1) * rows)
        first = pl.multiple_of((2 * index + place) * rows, 16)
        second = pl.multiple_of((2 * index + 1 - place) * rows, 16)
        out[pl.ds(first, rows), lanes] = own[here, :]
        out[pl.ds(second, rows), lanes] = other[here, :]


def attention_forward(heads, experts, *refs):
    (meta, x_own, x_other, wall, strips, far, segment) = refs[:7]
    kept = refs[7:12]
    (o_own, o_other, o_all, gains) = refs[12:16]
    (h1, q_out, k_out, v_out, probs, sems) = refs[16:]
    copies = []

    def keep(source, target):
        copy = pltpu.make_async_copy(source, target, sems.at[len(copies)])
        copy.start()
        copies.append(copy)

    place = meta[0]
    rows = x_own.shape[0]
    group = 2 * rows
    width = wall.shape[1]
    extras = wall[:, width - LANES :].astype(f32).T
    gain_at = HEAD_SIZE + experts
    gains[...] = extras[gain_at : gain_at + 8]
    gain_one = gains[0:1]
    for source, start in ((x_own, place * rows), (x_other, (1 - place) * rows)):
        values = source[...].astype(f32)
        h1[pl.ds(pl.multiple_of(start, 16), rows), :] = (
            values * rms_scale(values) * gain_one
        ).astype(bf16)
    keep(h1, kept[0])
    qkv = mm(h1[...], wall[...])
    lanes = q_out.shape[1]
    q_out[...] = qkv[:, :lanes].astype(bf16)
    k_out[...] = pltpu.roll(qkv[:, LANES : LANES + lanes], lanes - HEAD_SIZE, 1).astype(bf16)
    v_out[...] = qkv[:, width - lanes :].astype(bf16)
    for source, target in zip((q_out, k_out, v_out), kept[1:4]):
        keep(source, target)
    segment_row = segment[0:1, :]
    segment_column = column_of(segment_row.astype(f32)).astype(jnp.int32)
    keys = k_out[...]
    blocks = group // STRIP
    values_of = [pick_head(v_out[...], head, lanes) for head in range(heads)]
    for block in range(blocks):
        first = block * STRIP
        same = segment_column[first : first + STRIP] == segment_row
        total = jnp.zeros((STRIP, lanes), f32)
        for head in range(heads):
            query = pick_head(q_out[first : first + STRIP, :], head, lanes)
            scores = mm_nt(query, keys) + bias_row(strips, far, head, block, blocks)
            scores = jnp.where(same, scores, masked_value)
            top = jnp.max(scores, axis=1, keepdims=True)
            raised = jnp.exp(scores - top)
            mass = jnp.sum(raised, axis=1, keepdims=True)
            chances = raised * (1.0 / mass)
            probs[head, first : first + STRIP, :] = chances
            total = total + mm(chances.astype(bf16), values_of[head])
        o_all[first : first + STRIP, :] = total.astype(bf16)
        at = slice(first, first + STRIP)
        keep(probs.at[:, at, :], kept[4].at[:, at, :])
    for out, start in ((o_own, place * rows), (o_other, (1 - place) * rows)):
        values = o_all[pl.ds(pl.multiple_of(start, 16), rows), :].astype(f32)
        for index, part in enumerate(join(values[: rows // 2], values[rows // 2 :])):
            out[:, index * LANES : (index + 1) * LANES] = part.astype(bf16)
    for copy in copies:
        copy.wait()


def columns_of(*lines):
    return [column_of(line[...].astype(f32)).astype(jnp.int32) for line in lines]


def routed(hidden, extras, routes_column, keep_column, experts):
    logits = mm(hidden, extras)
    lane = iota((1, LANES), 1) - HEAD_SIZE
    valid = (lane >= 0) & (lane < experts)
    logits = jnp.where(valid, logits, masked_value)
    raised = jnp.where(valid, jnp.exp(logits - jnp.max(logits, axis=1, keepdims=True)), 0.0)
    probs = raised / jnp.sum(raised, axis=1, keepdims=True)
    onehot = lane == routes_column
    kept = keep_column.astype(f32)
    gate = jnp.sum(jnp.where(onehot, probs, 0.0), axis=1, keepdims=True) * kept
    return probs, onehot, kept, gate


def slots_by_row(routes_row, keep_row, experts, capacity):
    count = routes_row.shape[1]
    chosen = ((iota((experts, count), 0) == routes_row) & (keep_row == 1)).astype(f32)
    before = (iota((count, count), 0) < iota((count, count), 1)).astype(bf16)
    earlier = mm(chosen.astype(bf16), before)
    rank = jnp.sum(earlier * chosen, axis=0, keepdims=True).astype(jnp.int32)
    return jnp.where(keep_row == 1, routes_row * capacity + rank, -2)


def unpacked(pair):
    values = pair[...].astype(f32)
    lanes = values.shape[1] - LANES
    upper = jnp.where(iota((1, lanes), 1) < lanes - HEAD_SIZE, values[:, :lanes], 0.0)
    lower = pltpu.roll(values[:, LANES:], lanes - HEAD_SIZE, 1)
    lower = jnp.where(iota((1, lanes), 1) < lanes - HEAD_SIZE, lower, 0.0)
    return jnp.concatenate([upper, lower], axis=0)


def heads_of(own, other, place):
    own = unpacked(own)
    other = unpacked(other)
    first = jnp.where(place == 0, own, other)
    second = jnp.where(place == 0, other, own)
    return jnp.concatenate(join(first, second), axis=1).astype(bf16)


def to_experts(experts, capacity, count, *refs):
    (meta, x_own, cotangent, o_own, o_tp, o_ctx, o_far, wo_own, wo_tp, wo_ctx, wo_far) = refs[:11]
    (extras, gains, routes_row, keep_row, slot_h, slot_d) = refs[11:17]
    middle_out, sends, wo_out, wo_other = refs[17:]
    routes_column, keep_column = columns_of(routes_row, keep_row)
    extras = extras[:, extras.shape[1] - LANES :]
    place, start = meta[0], meta[2]
    interleave(wo_out, slice(None), wo_own, wo_ctx, start, count)
    interleave(wo_other, slice(None), wo_tp, wo_far, start, count)
    branch = mm_nt(heads_of(o_own, o_ctx, place), wo_out[...])
    branch = branch + mm_nt(heads_of(o_tp, o_far, place), wo_other[...])
    middle = x_own[...].astype(f32) + branch
    middle_out[...] = middle
    hidden = (middle * rms_scale(middle) * gains[1:2]).astype(bf16)
    _, _, _, gate = routed(hidden, extras, routes_column, keep_column, experts)
    out_grad = (gate * cotangent[...].astype(f32)).astype(bf16)
    slot = slots_by_row(routes_row[...], keep_row[...], experts, capacity)
    pick_h = (slot_h[...] == slot).astype(f32).astype(bf16)
    pick_d = (slot_d[...] == slot).astype(f32).astype(bf16)
    sends[...] = (mm(pick_h, hidden) + mm(pick_d, out_grad)).astype(bf16)


def gelu_both(value):
    scale = 0.7978845608028654
    cubic = 0.044715
    square = value * value
    inner = jnp.tanh(scale * value * (1.0 + cubic * square))
    half = 0.5 * (1.0 + inner)
    slope = half + 0.5 * value * (1.0 - inner * inner) * scale * (1.0 + 3.0 * cubic * square)
    return value * half, slope


def expert_kernel(owners, kinds_rows, chunks, group_owners, *refs):
    (rows_in, base_column, base_row, w_in, w_out) = refs[:5]
    (out, x_out, dy_out, act_out, dpre_out, acc_y, acc_x, full) = refs[5:]
    piece = pl.program_id(0)
    chunk = pl.program_id(1)
    pieces = pl.num_programs(0)
    capacity = kinds_rows
    per_owner = rows_in.shape[0] // owners
    span = group_owners * per_owner
    half = group_owners * capacity
    groups = owners // group_owners

    @pl.when(chunk == 0)
    def _():
        pick = (base_column[...] + piece * capacity == iota((2 * half, span), 1)).astype(f32).astype(bf16)
        for group in range(groups):
            got = mm(pick, rows_in[group * span : (group + 1) * span, :]).astype(bf16)
            x_out[0, group * half : (group + 1) * half, :] = got[:half]
            dy_out[0, group * half : (group + 1) * half, :] = got[half:]
        acc_y[...] = jnp.zeros_like(acc_y)
        acc_x[...] = jnp.zeros_like(acc_x)

    pre = mm(x_out[0], w_in[0])
    act, slope = gelu_both(pre)
    act = act.astype(bf16)
    act_out[0] = act
    acc_y[...] += mm(act, w_out[0])
    dpre = (mm_nt(dy_out[0], w_out[0]) * slope).astype(bf16)
    dpre_out[0] = dpre
    acc_x[...] += mm_nt(dpre, w_in[0])

    @pl.when(chunk == chunks - 1)
    def _():
        pick = (base_row[...] + piece * capacity == iota((span, 2 * half), 0)).astype(f32).astype(bf16)
        for group in range(groups):
            here = slice(group * half, (group + 1) * half)
            both = jnp.concatenate([acc_y[here].astype(bf16), acc_x[here].astype(bf16)], axis=0)
            part = mm(pick, both)
            there = slice(group * span, (group + 1) * span)
            full[there] = jnp.where(piece == 0, part, full[there] + part)

    @pl.when((chunk == chunks - 1) & (piece == pieces - 1))
    def _():
        width = out.shape[2]
        shares = out.shape[0] // owners
        for owner in range(owners):
            for share in range(shares):
                out[owner * shares + share] = full[
                    owner * per_owner : (owner + 1) * per_owner, share * width : (share + 1) * width
                ].astype(bf16)


def expert_grads(x_rows, dpre, act, dy, w_in_grad, w_out_grad):
    w_in_grad[0] = mm_tn(x_rows[0], dpre[0])
    w_out_grad[0] = mm_tn(act[0], dy[0])


def from_experts(experts, capacity, *refs):
    meta, rows_in, cotangent, routes_row, keep_row, slots, y_out, dx_out, gate_out = refs
    slot = column_of(slots_by_row(routes_row[...], keep_row[...], experts, capacity).astype(f32))
    slot = slot.astype(jnp.int32)
    width = rows_in.shape[1]
    pick_y = (slot == slots[0:1, :]).astype(f32).astype(bf16)
    pick_x = (slot == slots[1:2, :]).astype(f32).astype(bf16)
    dx_out[...] = mm(pick_x, rows_in[...]).astype(bf16)
    picked = mm(pick_y, rows_in[...]).astype(bf16)
    y_out[...] = picked
    upstream = jnp.where(meta[1] == 0, cotangent[:, :width], cotangent[:, width:])
    part = jnp.sum(upstream.astype(f32) * picked.astype(f32), axis=1, keepdims=True)
    gate_out[...] = jnp.broadcast_to(part, (part.shape[0], LANES)).T[:8]


def add_expert(meta, middle, gate, y_own, y_tp, result):
    width = y_own.shape[1]
    share = meta[1]
    own, other = y_own[...].astype(f32), y_tp[...].astype(f32)
    gates = gate[:, :1]
    result[:, :width] = middle[:, :width] + gates * jnp.where(share == 0, own, other)
    result[:, width:] = middle[:, width:] + gates * jnp.where(share == 0, other, own)


def middle_backward(experts, *refs):
    (meta, dx_own, dx_tp, part_own, part_tp, middle_ref, cotangent, extras) = refs[:8]
    (gains, routes_row, keep_row) = refs[8:11]
    (dmiddle_out, branch_grad, router_grad, gate_out) = refs[11:]
    routes_column, keep_column = columns_of(routes_row, keep_row)
    extras = extras[:, extras.shape[1] - LANES :]
    share = meta[1]
    own, other = dx_own[...].astype(f32), dx_tp[...].astype(f32)
    slot_grad = jnp.concatenate(
        [jnp.where(share == 0, own, other), jnp.where(share == 0, other, own)], axis=1
    )
    middle = middle_ref[...]
    scale = rms_scale(middle)
    normed = middle * scale
    gain = gains[1:2]
    hidden = (normed * gain).astype(bf16)
    probs, onehot, kept, gate = routed(hidden, extras, routes_column, keep_column, experts)
    gate_out[...] = jnp.broadcast_to(gate, gate_out.shape)
    upstream = cotangent[...].astype(f32)
    gate_grad = column_of(part_own[0:1, :] + part_tp[0:1, :])
    prob_grad = jnp.where(onehot, gate_grad * kept, 0.0)
    logit_grad = (
        probs * (prob_grad - jnp.sum(probs * prob_grad, axis=1, keepdims=True))
    ).astype(bf16)
    hidden_grad = slot_grad + mm_nt(logit_grad, extras)
    gain_grad = column_of(jnp.sum(hidden_grad * normed, axis=0, keepdims=True))
    lane = iota((1, LANES), 1)
    router_grad[...] = jnp.where(
        lane == HEAD_SIZE + experts, gain_grad, mm_tn(hidden, logit_grad)
    ).astype(bf16)
    grad = hidden_grad * gain
    dmiddle = upstream + scale * (grad - normed * jnp.mean(grad * normed, axis=1, keepdims=True))
    dmiddle_out[...] = dmiddle
    branch_grad[...] = dmiddle.astype(bf16)


def attention_backward(heads, buckets, shard, *refs):
    (meta, x_own, x_other) = refs[:3]
    kept = refs[3:8]
    (db, o_all, wo_ref, wall, router_grad) = refs[8:13]
    (payload, top_out, bottom_out, dh1_own, dh1_other) = refs[13:18]
    (sums, do_all, dq, dk, dv, dqkv, dh1) = refs[18:25]
    (h1, q_in, k_in, v_in, probs, sems) = refs[25:]
    blocks = q_in.shape[0] // STRIP
    moves = [(kept[1], q_in), (kept[2], k_in), (kept[3], v_in)]
    for block in range(blocks):
        at = slice(block * STRIP, (block + 1) * STRIP)
        moves.append((kept[4].at[:, at, :], probs.at[:, at, :]))
    moves.append((kept[0], h1))
    copies = [pltpu.make_async_copy(a, b, sems.at[i]) for i, (a, b) in enumerate(moves)]
    for copy in copies:
        copy.start()
    place = meta[0]
    rows = x_own.shape[0]
    group = 2 * rows
    lanes = q_in.shape[1]
    own_at = pl.ds(pl.multiple_of(place * rows, 16), rows)
    other_at = pl.ds(pl.multiple_of((1 - place) * rows, 16), rows)
    both = mm(db[...], wo_ref[...])
    high = pltpu.roll(both[:, LANES : LANES + lanes], lanes - HEAD_SIZE, 1)
    do_all[...] = jnp.where(place == 0, both[:, :lanes], high).astype(bf16)
    sums[...] = jnp.zeros_like(sums)
    for copy in copies[:3]:
        copy.wait()
    keys = k_in[...]
    values = v_in[...]
    ahead = [jnp.zeros((STRIP, STRIP), f32) for _ in range(heads)]
    behind = [jnp.zeros((STRIP, STRIP), f32) for _ in range(heads)]
    for block in range(blocks):
        at = slice(block * STRIP, (block + 1) * STRIP)
        copies[3 + block].wait()
        dq_total = jnp.zeros((STRIP, lanes), f32)
        for head in range(heads):
            query = pick_head(q_in[at, :], head, lanes)
            chances = probs[head, at, :]
            grad = pick_head(do_all[at, :], head, lanes)
            chance_grad = mm_nt(grad, values)
            mean = jnp.sum(chances * chance_grad, axis=1, keepdims=True)
            score_grad = (chances * (chance_grad - mean)).astype(bf16)
            dv_part = mm_tn(chances.astype(bf16), grad)
            dk_part = mm_tn(score_grad, query)
            if block == 0 and head == 0:
                dv[...] = dv_part
                dk[...] = dk_part
            else:
                dv[...] += dv_part
                dk[...] += dk_part
            dq_total = dq_total + mm(score_grad, pick_head(keys, head, lanes))
            rounded = score_grad.astype(f32)
            for other in range(blocks):
                gap = other - block
                part = rounded[:, other * STRIP : (other + 1) * STRIP]
                if abs(gap) <= 1:
                    sums[head, :, (gap + 2) * STRIP : (gap + 3) * STRIP] += part
                elif gap > 0:
                    ahead[head] = ahead[head] + part
                else:
                    behind[head] = behind[head] + part
        dq[at, :] = dq_total
    half = HEAD_SIZE
    dqkv[:, :LANES] = dq[:, :LANES].astype(bf16)
    shifted = pltpu.roll(dk[...], half, 1)
    dqkv[:, LANES : 2 * LANES] = (dq[:, LANES:] + shifted[:, :LANES]).astype(bf16)
    dqkv[:, 2 * LANES : 3 * LANES] = shifted[:, LANES:].astype(bf16)
    dqkv[:, 3 * LANES :] = dv[...].astype(bf16)
    dh1[...] = mm_nt(dqkv[...], wall[...])
    gain_part = None
    for source, at, target in ((x_own, own_at, dh1_own), (x_other, other_at, dh1_other)):
        values = source[...].astype(f32)
        grad = dh1[at, :]
        target[...] = grad.astype(bf16)
        part = jnp.sum(grad * (values * rms_scale(values)), axis=0, keepdims=True)
        gain_part = part if gain_part is None else gain_part + part
    spread = skew(sums[...].reshape(heads * STRIP, 4 * STRIP), False)
    diagonals = jnp.sum(spread.reshape(heads, STRIP, 4 * STRIP), axis=1)
    picks = (bucket_index(iota((4 * STRIP, 1), 0) - 2 * STRIP) == iota((1, LANES), 1)).astype(f32)
    in_buckets = jnp.dot(diagonals, picks, precision=highest, preferred_element_type=f32)
    lane = iota((1, LANES), 1)
    row = lax.rem(iota((wall.shape[0], 1), 0), shard)
    riders = jnp.where(lane == HEAD_SIZE, column_of(gain_part), 0.0)
    for head in range(heads):
        line = in_buckets[head : head + 1]
        line = line + jnp.where(lane == buckets - 1, jnp.sum(ahead[head]), 0.0)
        line = line + jnp.where(lane == buckets // 2 - 1, jnp.sum(behind[head]), 0.0)
        riders = riders + jnp.where(row == head, pltpu.roll(line, HEAD_SIZE + 1, 1), 0.0)
    width = wall.shape[1]
    copies[-1].wait()
    grads = mm_tn(h1[...], dqkv[...])
    payload[:, : width - LANES] = grads[:, : width - LANES].astype(bf16)
    payload[:, width - LANES : width] = (grads[:, width - LANES :] + riders).astype(bf16)
    grads = mm_tn(db[...], o_all[...])
    payload[:, width : width + lanes - LANES] = grads[:, : lanes - LANES].astype(bf16)
    payload[:, width + lanes - LANES :] = (
        grads[:, lanes - LANES :] + router_grad[...].astype(f32)
    ).astype(bf16)
    half = top_out.shape[0]
    across = pl.multiple_of(meta[3] * shard if 2 * half == shard else 0 * meta[3], 16)
    top_out[...] = payload[pl.ds(across, half), :]
    bottom_out[...] = payload[pl.ds(across + half, half), :]


def ring_add(places, right_mine, left_mine, from_left, from_right, right_out, left_out):
    rows = right_mine.shape[0]
    span = from_left.shape[0]
    right_out[...] = right_mine[...]
    left_out[...] = left_mine[...]
    top, bottom = slice(0, span), slice(rows - span, rows)
    right_out[top] = (right_mine[top].astype(f32) + from_left[...].astype(f32)).astype(bf16)
    left_out[bottom] = (left_mine[bottom].astype(f32) + from_right[...].astype(f32)).astype(bf16)


def ring_end(at, place, sums, own, send, table, riders_own, riders_other):
    rows = own.shape[0]
    first, second = sums[:rows, :], sums[rows : 2 * rows, :]
    mine = jnp.where(place == 0, first, second)
    other = jnp.where(place == 0, second, first)
    own[...] = mine
    send[:rows, :] = other
    send[rows:, :] = sums[:8, :]
    table[...] = sums[:8, at : at + LANES]
    riders_own[...] = mine[:, at : at + LANES]
    riders_other[...] = other[:, at : at + LANES]


def ring_last(at, places, mine, from_left, from_right, own, send, table, riders_own, riders_other):
    total = mine[...].astype(f32) + from_left[...].astype(f32) + from_right[...].astype(f32)
    ring_end(at, places[0], total, own, send, table, riders_own, riders_other)


def ring_whole(at, places, sums, own, send, table, riders_own, riders_other):
    ring_end(at, places[0], sums[...], own, send, table, riders_own, riders_other)


def shards_of_sums(experts, buckets, heads, *refs):
    (meta, own_ref, other, own_top, from_tp, from_far) = refs[:6]
    (query_out, key_out, value_out, output_out, router_out, gain_one, gain_two, table) = refs[6:]
    place = meta[0]
    rows, width = query_out.shape[0], query_out.shape[1] // 2
    lanes = width + HEAD_SIZE
    wide = 3 * width + HEAD_SIZE
    own = own_ref[...]
    more = other[:rows, :]
    lane = iota((1, lanes), 1)
    for at, moved, out in (
        (0, False, query_out),
        (LANES, True, key_out),
        (2 * width, False, value_out),
        (wide, False, output_out),
    ):
        parts = [values[:, at : at + lanes] for values in (own, more)]
        if moved:
            parts = [pltpu.roll(part, lanes - HEAD_SIZE, 1) for part in parts]
        parts = [jnp.where(lane < width, part, 0.0) for part in parts]
        first = jnp.where(place == 0, parts[0], parts[1])
        second = jnp.where(place == 0, parts[1], parts[0])
        for index, block in enumerate(join(first, second)):
            out[:, index * LANES : (index + 1) * LANES] = block
    total = (own + more)[:, wide + lanes - LANES :].T
    router_out[...] = total[HEAD_SIZE : HEAD_SIZE + experts, :]
    gain_two[...] = total[HEAD_SIZE + experts : HEAD_SIZE + experts + 1, :]
    line = (own + more)[:, wide - LANES : wide] + (from_tp[...] + from_far[...])
    gain_one[...] = line.T[HEAD_SIZE : HEAD_SIZE + 1, :]
    own_lines = own_top[...]
    other_lines = other[rows : rows + 8, wide - LANES : wide]
    own_lines = pltpu.roll(own_lines, LANES - HEAD_SIZE - 1, 1)
    other_lines = pltpu.roll(other_lines, LANES - HEAD_SIZE - 1, 1)
    table[:heads, :] = jnp.where(place == 0, own_lines, other_lines)[:heads, :buckets]
    table[heads : 2 * heads, :] = jnp.where(place == 0, other_lines, own_lines)[:heads, :buckets]


def input_backward(x_own, dmiddle, gains, near, far, out):
    values = x_own[...].astype(f32)
    scale = rms_scale(values)
    normed = values * scale
    grad = (near[...].astype(f32) + far[...].astype(f32)) * gains[0:1]
    out[...] = dmiddle[...] + scale * (
        grad - normed * jnp.mean(grad * normed, axis=1, keepdims=True)
    )


def swap(value, axis):
    return lax.ppermute(value, axis, [(0, 1), (1, 0)])


def ring_order(count):
    return list(range(0, count, 2)) + list(range(count - 1, 0, -2))


def ring_steps(count):
    order = ring_order(count)
    right = [(order[i], order[(i + 1) % count]) for i in range(count)]
    return order, right, [(b, a) for a, b in right]


def device_table(fsdp_count, ctx_count, tp_count, aligned):
    order = ring_order(fsdp_count)
    rows = []
    for place in range(fsdp_count):
        spot = order.index(place)
        at = lambda distance: order[(spot + distance) % fsdp_count]
        half = fsdp_count // 2
        ring = [place]
        for step in range(1, half):
            ring += [at(-step), at(step)]
        ring.append(at(half))
        for step in range(half, 0, -1):
            ring += [at(step - 1), at(1 - step)]
        for core in range(ctx_count):
            for share in range(tp_count):
                rows.append([core, share, core if aligned else 0, at(half)] + (ring if aligned else []))
    return np.array(rows, np.int32)


def ring_gather(shard, count, side):
    _, right, left = ring_steps(count)
    shards = [shard]
    going_right, going_left = shard, shard
    for step in range(1, count // 2):
        going_right = lax.ppermute(going_right, "fsdp", right)
        going_left = lax.ppermute(going_left, "fsdp", left)
        if step == 1:
            going_right, going_left, side = lax.optimization_barrier((going_right, going_left, side))
        shards += [going_right, going_left]
    shards.append(lax.ppermute(going_right, "fsdp", right))
    return shards, side


def ring_sums(payload, top, bottom, count, at, meta, sides):
    rows = payload.shape[0] // count
    lanes = payload.shape[1]
    half = rows // 2
    outs = [
        shape((half, lanes), f32),
        shape((half + 8, lanes), f32),
        shape((8, LANES), f32),
        shape((half, LANES), f32),
        shape((half, LANES), f32),
    ]
    if rows % 32 or count % 2:
        sums = lax.psum_scatter(payload.astype(f32), "fsdp", scatter_dimension=0, tiled=True)
        return kernel_call(functools.partial(ring_whole, at), outs, [smem, vmem])(meta, sums)
    _, right, left = ring_steps(count)
    going_right, going_left = top, bottom
    spec = lambda which: pl.BlockSpec((rows, lanes), lambda i, places: (places[which], 0))
    params = pltpu.CompilerParams(vmem_limit_bytes=8 * MIB)
    for step in range(count // 2, 0, -1):
        from_left = lax.ppermute(going_right, "fsdp", right)
        from_right = lax.ppermute(going_left, "fsdp", left)
        if step in sides:
            from_left, from_right, _ = lax.optimization_barrier((from_left, from_right, sides[step]))
        which = 4 + count + 2 * (count // 2 - step)
        whole = lambda dims: pl.BlockSpec(dims, lambda i, places: (0, 0))
        last = step == 1
        step_outs = outs if last else [shape((rows, lanes), bf16)] * 2
        out = pl.pallas_call(
            functools.partial(ring_last, at) if last else ring_add,
            grid_spec=pltpu.PrefetchScalarGridSpec(
                num_scalar_prefetch=1,
                grid=(1,),
                in_specs=([spec(which)] if last else [spec(which), spec(which + 1)])
                + [whole(from_left.shape), whole(from_right.shape)],
                out_specs=[whole(o.shape) for o in step_outs],
            ),
            out_shape=step_outs,
            compiler_params=params,
            cost_estimate=pl.CostEstimate(flops=0, bytes_accessed=1024 * 1024, transcendentals=0),
        )(meta, *([payload] if last else [payload, payload]), from_left, from_right)
        if last:
            return out
        going_right, going_left = out


def body(
    tokens,
    cotangent,
    w_query,
    w_key,
    w_value,
    w_output,
    w_router,
    gain_attn,
    gain_moe,
    rel_table,
    w_in,
    w_out,
    lengths,
    routes,
    keep_mask,
):
    rows, model_width = tokens.shape
    fsdp_count = lax.axis_size("fsdp")
    owners = lax.axis_size(("fsdp", "ctx"))
    tp_count = lax.axis_size("tp")
    place = lax.axis_index("ctx")
    share = lax.axis_index("tp")
    fsdp_place = lax.axis_index("fsdp")
    group = 2 * rows
    experts = w_router.shape[1]
    capacity = max(2, (5 * rows + 4 * experts - 1) // (4 * experts))
    pieces = w_in.shape[0]
    split_count = owners * pieces // experts
    hidden_width = w_in.shape[2]
    heads = rel_table.shape[1] // 2
    heads_all = heads * 2 * tp_count
    width = heads * HEAD_SIZE
    lanes = width + HEAD_SIZE
    shard_rows = w_query.shape[0]
    buckets = rel_table.shape[0]

    def full(dims, dtype):
        return shape(dims, dtype)

    wide = 3 * width + HEAD_SIZE
    aligned = shard_rows % 16 == 0 and fsdp_count % 2 == 0
    count = fsdp_count if aligned else 1
    table = jnp.asarray(device_table(fsdp_count, 2, tp_count, aligned))
    device = lax.axis_index(("fsdp", "ctx", "tp"))
    meta = lax.dynamic_slice(table, (device, 0), (1, table.shape[1])).reshape(-1)
    shard_own, shard_send, wo_shard = kernel_call(
        pack_rows,
        [full((shard_rows, wide), bf16), full((shard_rows, wide), bf16), full((2 * shard_rows, lanes), bf16)],
        [smem] + [vmem] * 7,
        moved=512 * 1024,
        mib=60,
    )(meta, w_query, w_key, w_value, w_output, w_router.T, gain_attn[None, :], gain_moe[None, :])
    shard_other = swap(shard_send, "ctx")
    shard = jnp.concatenate(
        [jnp.concatenate([shard_own, shard_other], axis=0), wo_shard], axis=1
    )
    x_other = swap(tokens, "ctx")

    def ordered(own, other):
        if aligned:
            return own, other
        dims = (fsdp_count, 1, shard_rows, own.shape[1])
        pair = in_order(own.reshape(dims), other.reshape(dims), 1).reshape(2 * own.shape[0], -1)
        return pair[: own.shape[0]], pair[own.shape[0] :]

    def in_order(own, other, axis):
        return jnp.where(
            place == 0,
            jnp.concatenate([own, other], axis=axis),
            jnp.concatenate([other, own], axis=axis),
        )

    strips, far, segment = kernel_call(
        functools.partial(attention_tables, heads),
        [
            full((heads, STRIP, 3 * STRIP), f32),
            full((8, LANES), f32),
            full((8, group), jnp.int32),
        ],
        [smem] * 3,
        moved=1024 * 1024,
        mib=8,
    )(meta, lengths, rel_table.T)
    if aligned:
        shards, (strips, far, segment) = ring_gather(shard, fsdp_count, (strips, far, segment))
        wall, wo_own = kernel_call(
            functools.partial(put_in_rows, len(shards)),
            [full((model_width, wide), bf16), full((model_width // 2, 2 * width), bf16)],
            [smem] + [vmem] * len(shards),
            moved=4 * 1024 * 1024,
        )(meta, *shards)
    else:
        both = lax.all_gather(shard, "fsdp", axis=0, tiled=False)
        upper, lower = both[:, :shard_rows], both[:, shard_rows:]
        wall = jnp.concatenate(
            ordered(upper[:, :, :wide].reshape(-1, wide), lower[:, :, :wide].reshape(-1, wide)), axis=0
        )
        wo_own = jnp.concatenate([upper[:, :, wide : wide + width], lower[:, :, wide : wide + width]], axis=2)
        wo_own = wo_own.reshape(-1, 2 * width)

    kept_shapes = [(group, model_width)] + [(group, lanes)] * 3
    probs_shape = (heads, group, group)
    blocks = group // STRIP
    kept_scratch = [pltpu.VMEM(dims, bf16) for dims in kept_shapes] + [pltpu.VMEM(probs_shape, f32)]
    h1, q, k, v, probs, o_own, o_other, o_all, gains = kernel_call(
        functools.partial(attention_forward, heads, experts),
        [pltpu.HBM(dims, bf16) for dims in kept_shapes]
        + [
            pltpu.HBM(probs_shape, f32),
            full((rows // 2, 2 * width), bf16),
            full((rows // 2, 2 * width), bf16),
            full((group, lanes), bf16),
            full((8, model_width), f32),
        ],
        [smem] + [vmem] * 6,
        out_specs=[hbm] * 5 + [vmem] * 4,
        scratch=kept_scratch + [pltpu.SemaphoreType.DMA((4 + blocks,))],
        flops=2 * group * model_width * wide * 8,
        moved=8 * 1024 * 1024,
        mib=20,
    )(meta, tokens, x_other, wall, strips, far, segment)
    wo_tp = swap(wo_own, "tp")
    wo_ctx = swap(wo_own, "ctx")
    wo_tp, gains = lax.optimization_barrier((wo_tp, gains))
    wo_far = swap(wo_tp, "ctx")
    wo_own, wo_ctx = ordered(wo_own, wo_ctx)
    wo_tp, wo_far = ordered(wo_tp, wo_far)

    o_tp = swap(o_own, "tp")
    o_ctx = swap(o_other, "ctx")
    o_far = lax.ppermute(o_other, ("ctx", "tp"), [(i, 3 - i) for i in range(4)])

    per_owner = 2 * pieces * capacity
    owner_of = np.repeat(np.arange(owners), per_owner)
    inside = np.tile(np.arange(per_owner), owners)
    kind = inside // (pieces * capacity)
    piece_of = owner_of * pieces + (inside // capacity) % pieces
    slot_of = (piece_of // split_count) * capacity + inside % capacity
    slot_first = np.where(kind == 0, slot_of, -1).astype(np.int32)
    slot_second = np.where(kind == 1, slot_of, -1).astype(np.int32)
    routes_row = routes.reshape(1, rows)
    keep_row = keep_mask.reshape(1, rows)

    middle, sends, wo_full = kernel_call(
        functools.partial(to_experts, experts, capacity, count),
        [
            full((rows, model_width), f32),
            full((owners * per_owner, model_width), bf16),
            full((model_width, 2 * width), bf16),
        ],
        [smem] + [vmem] * 16,
        scratch=[pltpu.VMEM((model_width, 2 * width), bf16)],
        flops=2 * rows * model_width * (model_width + 2 * owners * per_owner),
        moved=6 * 1024 * 1024,
    )(
        meta, tokens, cotangent, o_own, o_tp, o_ctx, o_far, wo_own, wo_tp, wo_ctx, wo_far, wall,
        gains, routes_row, keep_row, slot_first[:, None], slot_second[:, None],
    )

    arrived = lax.all_to_all(
        sends.reshape(owners, per_owner, model_width),
        ("fsdp", "ctx"),
        split_axis=0,
        concat_axis=0,
        tiled=True,
    ).reshape(owners * per_owner, model_width)

    group_owners = min(16, owners)
    half = group_owners * capacity
    spot = np.arange(2 * half) % half
    base = (
        (spot // capacity) * per_owner
        + (np.arange(2 * half) // half) * pieces * capacity
        + spot % capacity
    ).astype(np.int32)
    chunk_width = 768 if hidden_width % 768 == 0 else hidden_width
    chunks = hidden_width // chunk_width
    slot_rows = owners * capacity
    part_width = model_width // tp_count
    whole = lambda *dims: pl.BlockSpec(dims, lambda i, j: (0,) * len(dims))
    outgoing, x_rows, dy_rows, act, dpre = kernel_call(
        functools.partial(expert_kernel, owners, capacity, chunks, group_owners),
        [
            pltpu.HBM((owners * tp_count, per_owner, part_width), bf16),
            pltpu.HBM((pieces, slot_rows, model_width), bf16),
            pltpu.HBM((pieces, slot_rows, model_width), bf16),
            pltpu.HBM((pieces, slot_rows, hidden_width), bf16),
            pltpu.HBM((pieces, slot_rows, hidden_width), bf16),
        ],
        [
            whole(owners * per_owner, model_width),
            whole(2 * half, 1),
            whole(1, 2 * half),
            pl.BlockSpec((1, model_width, chunk_width), lambda i, j: (i, 0, j)),
            pl.BlockSpec((1, chunk_width, model_width), lambda i, j: (i, j, 0)),
        ],
        out_specs=[
            whole(owners * tp_count, per_owner, part_width),
            pl.BlockSpec((1, slot_rows, model_width), lambda i, j: (i, 0, 0)),
            pl.BlockSpec((1, slot_rows, model_width), lambda i, j: (i, 0, 0)),
            pl.BlockSpec((1, slot_rows, chunk_width), lambda i, j: (i, 0, j)),
            pl.BlockSpec((1, slot_rows, chunk_width), lambda i, j: (i, 0, j)),
        ],
        scratch=[
            pltpu.VMEM((slot_rows, model_width), f32),
            pltpu.VMEM((slot_rows, model_width), f32),
            pltpu.VMEM((owners * per_owner, model_width), f32),
        ],
        grid=(pieces, chunks),
        mib=24 if owners <= 16 else 60,
        flops=8 * pieces * slot_rows * model_width * hidden_width,
        moved=12 * 1024 * 1024,
    )(arrived, base[:, None], base[None, :], w_in, w_out)

    returned = lax.all_to_all(
        outgoing, ("fsdp", "ctx", "tp"), split_axis=0, concat_axis=0, tiled=True
    ).reshape(owners * tp_count * per_owner, part_width)
    part = 512 if hidden_width % 512 == 0 else hidden_width
    rows_spec = pl.BlockSpec((1, slot_rows, model_width), lambda i, j: (i, 0, 0))
    hidden_spec = pl.BlockSpec((1, slot_rows, part), lambda i, j: (i, 0, j))
    w_in_grad, w_out_grad = kernel_call(
        expert_grads,
        [full(w_in.shape, f32), full(w_out.shape, f32)],
        [rows_spec, hidden_spec, hidden_spec, rows_spec],
        out_specs=[
            pl.BlockSpec((1, model_width, part), lambda i, j: (i, 0, j)),
            pl.BlockSpec((1, part, model_width), lambda i, j: (i, j, 0)),
        ],
        grid=(pieces, hidden_width // part),
        flops=4 * pieces * slot_rows * model_width * hidden_width,
        moved=24 * 1024 * 1024,
        mib=24,
    )(x_rows, dpre, act, dy_rows)
    returned, w_in_grad, w_out_grad = lax.optimization_barrier((returned, w_in_grad, w_out_grad))

    back_first = np.repeat(slot_first.reshape(owners, 1, per_owner), tp_count, axis=1).reshape(1, -1)
    back_second = np.repeat(slot_second.reshape(owners, 1, per_owner), tp_count, axis=1).reshape(1, -1)
    y_own, dx_own, part_own = kernel_call(
        functools.partial(from_experts, experts, capacity),
        [
            full((rows, part_width), bf16),
            full((rows, part_width), bf16),
            full((8, rows), f32),
        ],
        [smem] + [vmem] * 5,
        flops=4 * rows * returned.shape[0] * part_width,
        moved=2 * 1024 * 1024,
    )(meta, returned, cotangent, routes_row, keep_row, np.concatenate([back_first, back_second], axis=0))
    dx_tp = swap(dx_own, "tp")
    part_tp = swap(part_own, "tp")

    middle_grad, db_own, router_grad, gate = kernel_call(
        functools.partial(middle_backward, experts),
        [
            full((rows, model_width), f32),
            full((rows, model_width), bf16),
            full((model_width, LANES), bf16),
            full((rows, LANES), f32),
        ],
        [smem] + [vmem] * 10,
        flops=6 * rows * LANES * model_width,
        moved=6 * 1024 * 1024,
    )(meta, dx_own, dx_tp, part_own, part_tp, middle, cotangent, wall, gains, routes_row, keep_row)
    y_own, gate = lax.optimization_barrier((y_own, gate))
    y_tp = swap(y_own, "tp")
    db = lax.all_gather(db_own, "ctx", axis=0, tiled=True)

    half = model_width // fsdp_count // 2
    payload, top, bottom, dh1_own, dh1_other = kernel_call(
        functools.partial(attention_backward, heads, buckets, model_width // fsdp_count),
        [
            full((model_width, wide + lanes), bf16),
            full((half if aligned else 16, wide + lanes), bf16),
            full((half if aligned else 16, wide + lanes), bf16),
            full((rows, model_width), bf16),
            full((rows, model_width), bf16),
        ],
        [smem] + [vmem] * 2 + [hbm] * 5 + [vmem] * 5,
        scratch=[
            pltpu.VMEM((heads, STRIP, 4 * STRIP), f32),
            pltpu.VMEM((group, lanes), bf16),
            pltpu.VMEM((group, lanes), f32),
            pltpu.VMEM((group, lanes), f32),
            pltpu.VMEM((group, lanes), f32),
            pltpu.VMEM((group, wide), bf16),
            pltpu.VMEM((group, model_width), f32),
            *kept_scratch,
            pltpu.SemaphoreType.DMA((4 + blocks,)),
        ],
        flops=2 * group * model_width * wide * 12,
        mib=60,
        moved=8 * 1024 * 1024,
    )(
        meta, tokens, x_other, h1, q, k, v, probs, db, o_all, wo_full, wall, router_grad,
    )

    result = kernel_call(
        add_expert,
        [full((rows, model_width), f32)],
        [smem] + [vmem] * 4,
        moved=4 * 1024 * 1024,
    )(meta, middle, gate, y_own, y_tp)[0]
    dh1_sum = (dh1_own.astype(f32) + swap(dh1_other, "ctx").astype(f32)).astype(bf16)
    dh1_far = swap(dh1_sum, "tp")
    input_grad = kernel_call(
        input_backward,
        [full((rows, model_width), f32)],
        [vmem] * 5,
        moved=4 * 1024 * 1024,
    )(tokens, middle_grad, gains, dh1_sum, dh1_far)[0]
    own, send, own_lines, riders_own, riders_other = ring_sums(
        payload, top, bottom, fsdp_count, wide - LANES, meta, {1: (result, input_grad)}
    )
    other = swap(send, "ctx")
    from_tp = swap(riders_own, "tp")
    from_far = lax.ppermute(riders_other, ("ctx", "tp"), [(i, 3 - i) for i in range(4)])

    shard = full((shard_rows, 2 * width), f32)
    query_grad, key_grad, value_grad, output_grad, router_sum, gain_one, gain_two, table_grad = kernel_call(
        functools.partial(shards_of_sums, experts, buckets, heads),
        [shard] * 4
        + [
            full((experts, shard_rows), f32),
            full((1, shard_rows), f32),
            full((1, shard_rows), f32),
            full((2 * heads, buckets), f32),
        ],
        [smem] + [vmem] * 5,
        moved=1024 * 1024,
    )(meta, own, other, own_lines, from_tp, from_far)
    return (
        result,
        input_grad,
        query_grad,
        key_grad,
        value_grad,
        output_grad,
        router_sum.T,
        gain_one.reshape(shard_rows),
        gain_two.reshape(shard_rows),
        table_grad.T,
        w_in_grad,
        w_out_grad,
    )


def solution(mesh):
    in_specs = (
        P(("fsdp", "ctx"), None),
        P(("fsdp", "ctx"), None),
        P(("fsdp", "ctx"), "tp"),
        P(("fsdp", "ctx"), "tp"),
        P(("fsdp", "ctx"), "tp"),
        P(("fsdp", "ctx"), "tp"),
        P(("fsdp", "ctx"), None),
        P(("fsdp", "ctx")),
        P(("fsdp", "ctx")),
        P(None, "tp"),
        P(("fsdp", "ctx"), None, "tp"),
        P(("fsdp", "ctx"), "tp", None),
        P("fsdp", None),
        P(("fsdp", "ctx"), None),
        P(("fsdp", "ctx")),
    )
    out_specs = (
        P(("fsdp", "ctx"), None),
        P(("fsdp", "ctx"), None),
        P(("fsdp", "ctx"), "tp"),
        P(("fsdp", "ctx"), "tp"),
        P(("fsdp", "ctx"), "tp"),
        P(("fsdp", "ctx"), "tp"),
        P(("fsdp", "ctx"), None),
        P(("fsdp", "ctx")),
        P(("fsdp", "ctx")),
        P(None, "tp"),
        P(("fsdp", "ctx"), None, "tp"),
        P(("fsdp", "ctx"), "tp", None),
    )
    return jax.shard_map(body, mesh=mesh, in_specs=in_specs, out_specs=out_specs, check_vma=False)
```
